32 devices in a mesh: grid: 2 (over x), gx: 4 (over z), gy: 4 (over y, core).
Axes of the slice: x: 2, y: 2, z: 4, core: 2. Of those that a mesh axis runs over, the one named last changes fastest.
Arguments:
- fields: float32 [2, 9, 24, 96, 384], P('grid', None, 'gx', 'gy'), may hold values from -6 to 6
- material: int32 [2, 24, 96, 384], P('grid', 'gx', 'gy'), may hold values from 0 to 7
- permittivity: float32 [8], replicated, may hold values from 4 to 81
- conductivity: float32 [8], replicated, may hold values from 0.02 to 0.6
- relax_rate: float32 [8], replicated, may hold values from 0.05 to 0.8
- debye_strength: float32 [8], replicated, may hold values from 0.5 to 4
- subgrids: int32 [4, 4, 6], P('gx', 'gy'), may hold values from 0 to 256, as said below
Outputs:
- fields_out: float32 [2, 9, 24, 96, 384], P('grid', None, 'gx', 'gy')
The draws below stay inside these ranges and needn't reach their ends.
Inputs may be any that keep to these rules, and one draw needn't show every extreme that they name: subgrids[a, b] = (x0, y0, z0, lx, ly, lz): x0 <= 4, y0 <= 16, z0 <= 256; lx is at least 1 and at most 2, ly at least 4 and at most 8, lz at least 64 and at most 128; some block reaches every upper bound.
All inputs are finite; a program needn't handle non-finite values.
Results may differ from the reference program's by a relative error of at most 0.0003.
Values sent between devices are 32-bit elements; how exact they have to be, the bound alone decides.
No kernel may reach another device: no remote copies, remote signals or barrier semaphores. Data moves between devices by JAX's collectives and lax.ppermute only.
A program may use at most 128 MiB of HBM per device.

```python
import math
import jax
import jax.numpy as jnp
from jax import lax

CX = 6
CY = 24
CZ = 384
NMAT = 8
COARSE_STEPS = 3
NX = 24
NY = 96
N_GX = 4
N_GY = 4


def draw_subgrids(key, part):
    key = jax.random.fold_in(key, 7)
    keys = jax.random.split(key, 6)
    grid_shape = (N_GX, N_GY)
    widest_x = CX // 3
    widest_y = CY // 3
    widest_z = CZ // 3
    length_x = jax.random.randint(keys[0], grid_shape, max(CX // 6, 1), widest_x + 1)
    length_y = jax.random.randint(keys[1], grid_shape, max(CY // 6, 1), widest_y + 1)
    length_z = jax.random.randint(keys[2], grid_shape, max(CZ // 6, 1), widest_z + 1)
    corner_x = jax.random.randint(keys[3], grid_shape, 0, CX - widest_x + 1)
    corner_y = jax.random.randint(keys[4], grid_shape, 0, CY - widest_y + 1)
    corner_z = jax.random.randint(keys[5], grid_shape, 0, CZ - widest_z + 1)
    leading = (lax.broadcasted_iota(jnp.int32, grid_shape, 0) == 0) & (lax.broadcasted_iota(jnp.int32, grid_shape, 1) == 0)
    length_x = jnp.where(leading, widest_x, length_x)
    length_y = jnp.where(leading, widest_y, length_y)
    length_z = jnp.where(leading, widest_z, length_z)
    corner_x = jnp.where(leading, CX - widest_x, corner_x)
    corner_y = jnp.where(leading, CY - widest_y, corner_y)
    corner_z = jnp.where(leading, CZ - widest_z, corner_z)
    return jnp.stack([corner_x, corner_y, corner_z, length_x, length_y, length_z], axis=-1).astype(jnp.int32)


def plant(drawn, stream_key, smallest, largest):
    shape = drawn.shape
    place = [jax.random.randint(jax.random.fold_in(stream_key, axis), (), 0, shape[axis]) for axis in range(len(shape))]
    drawn = drawn.at[tuple(place)].set(smallest)
    longest = shape.index(max(shape))
    place[longest] = (place[longest] + 1) % shape[longest]
    return drawn.at[tuple(place)].set(largest)


def levels(rng, shape, cuts, low, high):
    def one(position, shards_of):
        draws = jax.random.uniform(jax.random.fold_in(jax.random.fold_in(rng, 6), position), (shards_of,), jnp.float32, low / len(cuts), high / len(cuts))
        return jnp.repeat(jnp.exp(draws), shape[position] // shards_of).reshape((-1,) + (1,) * (len(shape) - position - 1))

    level = one(*cuts[0])
    for cut in cuts[1:]:
        level = level * one(*cut)
    return level


def gaussian(rng, dims, scale, bound, pieces=(), kind=jnp.bfloat16):
    level = levels(rng, dims, pieces, -0.22, 0.18) if pieces else 1.0
    values = jax.random.normal(rng, dims, jnp.float32) * scale * level
    return jnp.minimum(jnp.maximum(values, -bound), bound).astype(kind)


def setup_inputs(seed: int = 0) -> dict:
    streams_of = jax.random.split(jax.random.key(seed), 8)
    fields = gaussian(streams_of[0], (2, 9, NX, NY, CZ), 1.0, 6.0, ((0, 2), (2, 4), (3, 4)), jnp.float32)
    material = plant(jax.random.randint(streams_of[1], (2, NX, NY, CZ), 0, NMAT), jax.random.fold_in(streams_of[1], 1), 0, NMAT - 1).astype(jnp.int32)
    permittivity = jnp.clip(jnp.exp(jax.random.uniform(streams_of[2], (NMAT,), jnp.float32, math.log(4.0), math.log(81.0))), 4.0, 81.0)
    conductivity = jnp.clip(jnp.exp(jax.random.uniform(streams_of[3], (NMAT,), jnp.float32, math.log(0.02), math.log(0.6))), 0.02, 0.6)
    relax_rate = jnp.clip(jnp.exp(jax.random.uniform(streams_of[4], (NMAT,), jnp.float32, math.log(0.05), math.log(0.8))), 0.05, 0.8)
    debye_strength = jnp.clip(jax.random.uniform(streams_of[5], (NMAT,), jnp.float32, 0.5, 4.0), 0.5, 4.0)
    subgrids = draw_subgrids(jax.random.fold_in(streams_of[7], 71), 0)
    return dict(fields=fields, material=material, permittivity=permittivity, conductivity=conductivity, relax_rate=relax_rate, debye_strength=debye_strength, subgrids=subgrids)


courant = 0.5
one_third = 1.0 / 3.0


def lookup(material, entries):
    picked = jnp.zeros(material.shape, entries.dtype)
    for candidate in range(entries.shape[0]):
        picked = jnp.where(material == candidate, entries[candidate], picked)
    return picked


def material_factors(material, permittivity, conductivity, relax_rate, debye_strength, factor):
    permit = lookup(material, permittivity)
    damping = lookup(material, conductivity) * factor / (2.0 * permit)
    relaxing = lookup(material, relax_rate) * factor
    return jnp.stack([(1.0 - damping) / (1.0 + damping), 1.0 / (permit * (1.0 + damping)), relaxing, jnp.exp(-relaxing), lookup(material, debye_strength)])


def diff_ahead(values, direction):
    base_cut = [slice(0, -1)] * 3
    moved_cut = [slice(0, -1)] * 3
    moved_cut[direction] = slice(1, None)
    return values[tuple(moved_cut)] - values[tuple(base_cut)]


def diff_behind(values, direction):
    base_cut = [slice(1, None)] * 3
    moved_cut = [slice(1, None)] * 3
    moved_cut[direction] = slice(0, -1)
    return values[tuple(base_cut)] - values[tuple(moved_cut)]


def curl_ahead(padded):
    return jnp.stack([diff_ahead(padded[2], 1) - diff_ahead(padded[1], 2), diff_ahead(padded[0], 2) - diff_ahead(padded[2], 0), diff_ahead(padded[1], 0) - diff_ahead(padded[0], 1)])


def curl_behind(padded):
    return jnp.stack([diff_behind(padded[2], 1) - diff_behind(padded[1], 2), diff_behind(padded[0], 2) - diff_behind(padded[2], 0), diff_behind(padded[1], 0) - diff_behind(padded[0], 1)])


def electric(efield, polarization, rotation, factors):
    return factors[0] * efield + factors[1] * (courant * rotation - factors[2] * (factors[4] * efield - polarization))


def relaxation(polarization, efield, factors):
    return factors[3] * polarization + (1.0 - factors[3]) * factors[4] * efield


def coarse_update(fields, factors):
    efield, hfield, polarization = fields[0:3], fields[3:6], fields[6:9]
    hfield = hfield - courant * curl_ahead(jnp.pad(efield, ((0, 0), (0, 1), (0, 1), (0, 1))))
    rotation = curl_behind(jnp.pad(hfield, ((0, 0), (1, 0), (1, 0), (1, 0))))
    efield = electric(efield, polarization, rotation, factors)
    polarization = relaxation(polarization, efield, factors)
    return jnp.concatenate([efield, hfield, polarization])


def fine_update(fields, factors, inside, border, driven):
    efield, hfield, polarization = fields[0:3], fields[3:6], fields[6:9]
    hfield = inside * (hfield - courant * curl_ahead(jnp.pad(efield, ((0, 0), (0, 1), (0, 1), (0, 1)))))
    rotation = curl_behind(jnp.pad(hfield, ((0, 0), (1, 0), (1, 0), (1, 0))))
    efield = jnp.where(border, driven, inside * electric(efield, polarization, rotation, factors))
    polarization = inside * relaxation(polarization, efield, factors)
    return jnp.concatenate([efield, hfield, polarization])


def subgrid_masks(extent, cell_shape):
    along_x = lax.broadcasted_iota(jnp.int32, cell_shape, 0)
    along_y = lax.broadcasted_iota(jnp.int32, cell_shape, 1)
    along_z = lax.broadcasted_iota(jnp.int32, cell_shape, 2)
    xlength = 3 * extent[3]
    ylength = 3 * extent[4]
    zlength = 3 * extent[5]
    covered = (along_x < xlength) & (along_y < ylength) & (along_z < zlength)
    xfaces = (along_x == 0) | (along_x == xlength - 1)
    yfaces = (along_y == 0) | (along_y == ylength - 1)
    zfaces = (along_z == 0) | (along_z == zlength - 1)
    border = jnp.stack([covered & (yfaces | zfaces), covered & (xfaces | zfaces), covered & (xfaces | yfaces)])
    return covered.astype(jnp.float32), border


def cut_region(efield, extent):
    region_shape = (3, efield.shape[1] // 3, efield.shape[2] // 3, efield.shape[3] // 3)
    return lax.dynamic_slice(efield, (jnp.int32(0), extent[0], extent[1], extent[2]), region_shape)


def upsample(region):
    sizes = region.shape
    spread = jnp.broadcast_to(region[:, :, None, :, None, :, None], (sizes[0], sizes[1], 3, sizes[2], 3, sizes[3], 3))
    return spread.reshape(sizes[0], 3 * sizes[1], 3 * sizes[2], 3 * sizes[3])


def restrict(efield):
    sizes = efield.shape
    grouped = efield.reshape(sizes[0], sizes[1] // 3, 3, sizes[2] // 3, 3, sizes[3] // 3, 3)
    return grouped.mean(axis=(2, 4, 6))


def overwrite(fields, restricted, extent):
    region = cut_region(fields[0:3], extent)
    along_x = lax.broadcasted_iota(jnp.int32, region.shape, 1)
    along_y = lax.broadcasted_iota(jnp.int32, region.shape, 2)
    along_z = lax.broadcasted_iota(jnp.int32, region.shape, 3)
    covered = (along_x < extent[3]) & (along_y < extent[4]) & (along_z < extent[5])
    updated = jnp.where(covered, restricted, region)
    return lax.dynamic_update_slice(fields, updated, (jnp.int32(0), extent[0], extent[1], extent[2]))


def to_blocks(values):
    components = values.shape[0]
    split = values.reshape(components, N_GX, CX, N_GY, CY, CZ)
    return split.transpose(1, 3, 0, 2, 4, 5).reshape(N_GX * N_GY, components, CX, CY, CZ)


def from_blocks(blocks):
    components = blocks.shape[1]
    split = blocks.reshape(N_GX, N_GY, components, CX, CY, CZ)
    return split.transpose(2, 0, 3, 1, 4, 5).reshape(components, N_GX * CX, N_GY * CY, CZ)


def reference(fields, material, permittivity, conductivity, relax_rate, debye_strength, subgrids):
    coarse_fields = fields[0]
    coarse_factors = material_factors(material[0], permittivity, conductivity, relax_rate, debye_strength, 1.0)
    fine_factors = to_blocks(material_factors(material[1], permittivity, conductivity, relax_rate, debye_strength, one_third))
    extents = subgrids.reshape(N_GX * N_GY, 6)
    inside, border = jax.vmap(lambda extent: subgrid_masks(extent, (CX, CY, CZ)))(extents)
    fine_fields = to_blocks(fields[1]) * inside[:, None]
    for number in range(COARSE_STEPS):
        earlier = jax.vmap(cut_region)(to_blocks(coarse_fields[0:3]), extents)
        coarse_fields = coarse_update(coarse_fields, coarse_factors)
        latest = jax.vmap(cut_region)(to_blocks(coarse_fields[0:3]), extents)
        for substep in range(1, 4):
            weight = substep / 3.0
            driven = earlier + weight * (latest - earlier)
            fine_fields = lax.map(lambda items: fine_update(items[0], items[1], items[2], items[3], upsample(items[4])), (fine_fields, fine_factors, inside, border, driven))
        restricted = jax.vmap(restrict)(fine_fields[:, 0:3])
        blocks = jax.vmap(overwrite)(to_blocks(coarse_fields), restricted, extents)
        coarse_fields = from_blocks(blocks)
    return jnp.stack([coarse_fields, from_blocks(fine_fields)])
```

```python
import functools

import jax
import jax.numpy as jnp
from jax import lax
from jax.experimental import pallas as pl
from jax.experimental.pallas import tpu as pltpu
from jax.sharding import PartitionSpec as P

COARSE_STEPS = 3
LIMIT = 40 * 1024 * 1024
VM = pl.BlockSpec(memory_space=pltpu.VMEM)
SM = pl.BlockSpec(memory_space=pltpu.SMEM)
F32 = jnp.float32


def shifted(value, axis, by):
    peers = lax.axis_size(axis)
    pairs = [(i, i + by) for i in range(peers) if 0 <= i + by < peers]
    return lax.ppermute(value, axis, pairs)


def lanes(shape=(8, 128)):
    return lax.broadcasted_iota(jnp.int32, shape, len(shape) - 1)


def rows(shape=(8, 128)):
    return lax.broadcasted_iota(jnp.int32, shape, len(shape) - 2)


def gather(tile, index):
    return jnp.take_along_axis(tile, index, axis=1)


def tables(perm, cond, relax, debye, factor):
    lane = lanes()

    def spread(ref):
        value = jnp.full((8, 128), ref[0], F32)
        for k in range(1, ref.shape[0]):
            value = jnp.where(lane == k, ref[k], value)
        return value

    eps = spread(perm)
    damp = spread(cond) * factor / (2.0 * eps)
    rate = spread(relax) * factor
    f0 = (1.0 - damp) / (1.0 + damp)
    f1 = 1.0 / (eps * (1.0 + damp))
    f3 = jnp.exp(-rate)
    f4 = spread(debye)
    c = f1 * rate
    return (f0 - c * f4, 0.5 * f1, c, f3, (1.0 - f3) * f4)


def to_tiles(parts):
    lane = lanes()
    kind = lane % 3
    out = []
    for t in range(3):
        mixed = jnp.where(
            kind == t, parts[0], jnp.where(kind == (t + 1) % 3, parts[1], parts[2])
        )
        out.append(gather(mixed, (3 * lane + t) & 127))
    return out


def from_tiles(tiles):
    lane = lanes()
    spread = [gather(tiles[t], (43 * (lane - t + 128)) & 127) for t in range(3)]
    out = []
    for a in range(3):
        kind = (2 * a + lane) % 3
        out.append(jnp.where(kind == 0, spread[0], jnp.where(kind == 1, spread[1], spread[2])))
    return out


def prep_kernel(f0, f1, f2, m0, m1, m2, perm, cond, relax, debye, sub, slab_e, slab_h, slab_p, box, coef):
    coarse = lax.axis_index("grid") == 0
    fields, material = (f0, f1, f2), (m0, m1, m2)

    @pl.when(coarse)
    def _():
        table = tables(perm, cond, relax, debye, 1.0)
        for x in range(6):
            for yt in range(3):
                for zt in range(3):
                    index = material[zt][0, x, pl.ds(8 * yt, 8)]
                    for k in range(5):
                        coef[k, x, 3 * yt + zt] = gather(table[k], index)
        for a in range(3):
            for k, part in enumerate((slab_e, slab_h, slab_p)):
                part[:, :, :, pl.ds(128 * a, 128)] = fields[a][0, 3 * k : 3 * k + 3]

    @pl.when(jnp.logical_not(coarse))
    def _():
        table = tables(perm, cond, relax, debye, F32(1.0 / 3.0))
        row, lane = rows(), lanes()
        ly, lz = sub[0, 0, 4], sub[0, 0, 5]
        within = (row < ly) & (lane < lz)
        for x in range(6):
            inside = within & (x < 3 * sub[0, 0, 3])
            for u in range(3):
                cut = pl.ds(u, 8, stride=3)
                parts = [material[a][0, x, cut] for a in range(3)]
                for t, index in enumerate(to_tiles(parts)):
                    for k in range(5):
                        coef[k, x, 3 * u + t] = gather(table[k], index)
                for c in range(9):
                    parts = [fields[a][0, c, x, cut] for a in range(3)]
                    for t, tile in enumerate(to_tiles(parts)):
                        box[c, x, 3 * u + t] = jnp.where(inside, tile, 0.0)


def whole(ref, *index):
    return jnp.concatenate(
        [
            jnp.concatenate([ref[(*index, 3 * yt + zt)] for zt in range(3)], axis=1)
            for yt in range(3)
        ],
        axis=0,
    )


def magnetic_kernel(slab_e, slab_h, next_x, next_y, out_h, last_x, last_y):
    coarse = lax.axis_index("grid") == 0

    @pl.when(coarse)
    def _():
        row, lane = rows((24, 384)), lanes((24, 384))

        def ahead_y(value, edge):
            return jnp.where(row == 23, edge, pltpu.roll(value, 23, 0))

        def ahead_z(value):
            return jnp.where(lane == 383, 0.0, pltpu.roll(value, 383, 1))

        for x in range(6):
            ex, ey, ez = (slab_e[c, x] for c in range(3))
            if x < 5:
                ey_x, ez_x = slab_e[1, x + 1], slab_e[2, x + 1]
            else:
                ey_x, ez_x = next_x[1, 0], next_x[2, 0]
            ex_y = ahead_y(ex, next_y[0, x : x + 1])
            ez_y = ahead_y(ez, next_y[2, x : x + 1])
            ex_z, ey_z = ahead_z(ex), ahead_z(ey)
            hx = slab_h[0, x] - 0.5 * ((ez_y - ez) - (ey_z - ey))
            hy = slab_h[1, x] - 0.5 * ((ex_z - ex) - (ez_x - ez))
            hz = slab_h[2, x] - 0.5 * ((ey_x - ey) - (ex_y - ex))
            for c, value in enumerate((hx, hy, hz)):
                out_h[c, x] = value
                last_y[c, x : x + 1] = value[23:24]
                if x == 5:
                    last_x[c, 0] = value


def row_pair(sub):
    y0 = sub[0, 0, 1]
    base = pl.multiple_of(8 * jnp.minimum(y0 // 8, 1), 8)
    return base, y0 - base


def region_of(slab, sub):
    x0, z0 = sub[0, 0, 0], sub[0, 0, 2]
    base, over = row_pair(sub)
    place = lanes() + z0
    index, part = place & 127, place >> 7

    def cut(c, i):
        tiles = []
        for a in range(3):
            pair = slab[c, x0 + i, pl.ds(base, 16), pl.ds(128 * a, 128)]
            tiles.append(gather(pltpu.roll(pair, (16 - over) & 15, 0)[0:8], index))
        return jnp.where(part == 0, tiles[0], jnp.where(part == 1, tiles[1], tiles[2]))

    return cut


def electric_kernel(slab_e, slab_h, slab_p, coef, prev_x, prev_y, sub, out_e, out_p, sent):
    coarse = lax.axis_index("grid") == 0

    @pl.when(coarse)
    def _():
        row, lane = rows((24, 384)), lanes((24, 384))
        cut = region_of(slab_e, sub)
        for c in range(3):
            for i in range(2):
                sent[0, c, i] = cut(c, i)

        def behind_y(value, edge):
            return jnp.where(row == 0, edge, pltpu.roll(value, 1, 0))

        def behind_z(value):
            return jnp.where(lane == 0, 0.0, pltpu.roll(value, 1, 1))

        for x in range(6):
            hx, hy, hz = (slab_h[c, x] for c in range(3))
            if x > 0:
                hy_x, hz_x = slab_h[1, x - 1], slab_h[2, x - 1]
            else:
                hy_x, hz_x = prev_x[1, 0], prev_x[2, 0]
            hx_y = behind_y(hx, prev_y[0, x : x + 1])
            hz_y = behind_y(hz, prev_y[2, x : x + 1])
            hx_z, hy_z = behind_z(hx), behind_z(hy)
            rotation = (
                (hz - hz_y) - (hy - hy_z),
                (hx - hx_z) - (hz - hz_x),
                (hy - hy_x) - (hx - hx_y),
            )
            a, b, p, f3, g = (whole(coef, k, x) for k in range(5))
            for c in range(3):
                old = slab_p[c, x]
                new = a * slab_e[c, x] + b * rotation[c] + p * old
                out_e[c, x] = new
                out_p[c, x] = f3 * old + g * new
        cut = region_of(out_e, sub)
        for c in range(3):
            for i in range(2):
                sent[1, c, i] = cut(c, i)


def put_back(slab, received, sub):
    x0, z0 = sub[0, 0, 0], sub[0, 0, 2]
    lx, ly, lz = sub[0, 0, 3], sub[0, 0, 4], sub[0, 0, 5]
    base, over = row_pair(sub)
    row, lane = rows((16, 128)) - over, lanes()
    for i in range(2):
        for a in range(3):
            place = lane + (128 * a) - z0
            index = place & 127
            wide = lanes((16, 128)) + (128 * a) - z0
            covered = (wide >= 0) & (wide < lz) & (row >= 0) & (row < ly) & (i < lx)
            for c in range(3):
                spot = (c, x0 + i, pl.ds(base, 16), pl.ds(128 * a, 128))
                tile = gather(received[c, i], index)
                pair = pltpu.roll(jnp.concatenate([tile, tile]), over, 0)
                slab[spot] = jnp.where(covered, pair, slab[spot])


def overwrite_kernel(slab_e, received, sub, slab, first_x, first_y):
    coarse = lax.axis_index("grid") == 0

    @pl.when(coarse)
    def _():
        slab[...] = slab_e[...]
        put_back(slab, received, sub)
        for c in range(3):
            first_x[c, 0] = slab[c, 0]
            for x in range(6):
                first_y[c, x : x + 1] = slab[c, x, 0:1]


def fine_kernel(box_in, coef, region, sub, box, restricted):
    coarse = lax.axis_index("grid") == 0

    @pl.when(jnp.logical_not(coarse))
    def _():
        box[...] = box_in[...]
        row, lane = rows(), lanes()
        lx, ly, lz = sub[0, 0, 3], sub[0, 0, 4], sub[0, 0, 5]
        within = (row < ly) & (lane < lz)
        inside = [within, within & (lx == 2)]
        y_face = [row == 0, None, row == ly - 1]
        z_face = [lane == 0, None, lane == lz - 1]

        def up(value):
            return jnp.where(row == 7, 0.0, pltpu.roll(value, 7, 0))

        def left(value):
            return jnp.where(lane == 127, 0.0, pltpu.roll(value, 127, 1))

        def down(value):
            return jnp.where(row == 0, 0.0, pltpu.roll(value, 1, 0))

        def right(value):
            return jnp.where(lane == 0, 0.0, pltpu.roll(value, 1, 1))

        def ahead_y(values, u, t):
            return values[3 * u + 3 + t] if u < 2 else up(values[t])

        def ahead_z(values, u, t):
            return values[3 * u + t + 1] if t < 2 else left(values[3 * u])

        def behind_y(values, u, t):
            return values[3 * u - 3 + t] if u > 0 else down(values[6 + t])

        def behind_z(values, u, t):
            return values[3 * u + t - 1] if t > 0 else right(values[3 * u + 2])

        def either(p, q):
            if p is None:
                return q
            return p if q is None else p | q

        zero = jnp.zeros((8, 128), F32)

        def substep(number, carry):
            weight = (number.astype(F32) + 1.0) / 3.0
            driven = [
                [region[0, c, i] + weight * (region[1, c, i] - region[0, c, i]) for i in range(2)]
                for c in range(3)
            ]
            for x in range(6):
                part = x // 3
                e = [[box[c, x, k] for k in range(9)] for c in range(3)]
                if x < 5:
                    ey_x = [box[1, x + 1, k] for k in range(9)]
                    ez_x = [box[2, x + 1, k] for k in range(9)]
                else:
                    ey_x = ez_x = [zero] * 9
                h = [[], [], []]
                for u in range(3):
                    for t in range(3):
                        k = 3 * u + t
                        ex, ey, ez = e[0][k], e[1][k], e[2][k]
                        turn = (
                            (ahead_y(e[2], u, t) - ez) - (ahead_z(e[1], u, t) - ey),
                            (ahead_z(e[0], u, t) - ex) - (ez_x[k] - ez),
                            (ey_x[k] - ey) - (ahead_y(e[0], u, t) - ex),
                        )
                        for c in range(3):
                            value = box[3 + c, x, k] - 0.5 * turn[c]
                            box[3 + c, x, k] = value
                            h[c].append(value)
                x_face = x == 0
                if x in (2, 5):
                    x_face = jnp.full((8, 128), 3 * lx - 1, jnp.int32) == x
                for u in range(3):
                    for t in range(3):
                        k = 3 * u + t
                        hx, hy, hz = h[0][k], h[1][k], h[2][k]
                        hy_x = box[4, x - 1, k] if x > 0 else zero
                        hz_x = box[5, x - 1, k] if x > 0 else zero
                        rotation = (
                            (hz - behind_y(h[2], u, t)) - (hy - behind_z(h[1], u, t)),
                            (hx - behind_z(h[0], u, t)) - (hz - hz_x),
                            (hy - hy_x) - (hx - behind_y(h[0], u, t)),
                        )
                        a, b, p, f3, g = (coef[q, x, k] for q in range(5))
                        faces = (
                            either(y_face[u], z_face[t]),
                            None if x_face is True else either(x_face if x in (2, 5) else None, z_face[t]),
                            None if x_face is True else either(x_face if x in (2, 5) else None, y_face[u]),
                        )
                        for c in range(3):
                            old = box[6 + c, x, k]
                            new = a * e[c][k] + b * rotation[c] + p * old
                            if c > 0 and x_face is True:
                                new = driven[c][part]
                            elif faces[c] is not None:
                                new = jnp.where(faces[c], driven[c][part], new)
                            new = jnp.where(inside[part], new, 0.0)
                            box[c, x, k] = new
                            box[6 + c, x, k] = f3 * old + g * new
            return carry

        lax.fori_loop(0, 3, substep, 0)
        for c in range(3):
            for i in range(2):
                total = zero
                for x in range(3 * i, 3 * i + 3):
                    for k in range(9):
                        total = total + box[c, x, k]
                restricted[c, i] = total * F32(1.0 / 27.0)


def finish_kernel(slab_e, slab_h, slab_p, box, received, sub, out, mixed):
    coarse = lax.axis_index("grid") == 0

    @pl.when(coarse)
    def _():
        for k, part in enumerate((slab_e, slab_h, slab_p)):
            out[3 * k : 3 * k + 3] = part[...]
        put_back(out, received, sub)

    @pl.when(jnp.logical_not(coarse))
    def _():
        for c in range(9):
            for x in range(6):
                for u in range(3):
                    parts = from_tiles([box[c, x, 3 * u + t] for t in range(3)])
                    for a in range(3):
                        mixed[c, x, a, pl.ds(u, 8, stride=3)] = parts[a]
                for a in range(3):
                    out[c, x, :, pl.ds(128 * a, 128)] = mixed[c, x, a]


def third(shape, a):
    return pl.BlockSpec(shape, lambda i: (0,) * (len(shape) - 1) + (a,))


def call(kernel, operands, specs, outs, scratch=(), grid=()):
    params = pltpu.CompilerParams(vmem_limit_bytes=LIMIT)
    return pl.pallas_call(
        kernel,
        out_shape=[jax.ShapeDtypeStruct(shape, F32) for shape in outs],
        in_specs=specs,
        out_specs=[VM] * len(outs),
        grid=grid,
        scratch_shapes=scratch,
        compiler_params=params,
    )(*operands)


PART = (3, 6, 24, 384)
SLAB = (9, 6, 24, 384)
BOX = (9, 6, 9, 8, 128)
COEF = (5, 6, 9, 8, 128)
REGION = (3, 2, 8, 128)
X_EDGE = (3, 1, 24, 384)
Y_EDGE = (3, 6, 384)


def body(fields, material, permittivity, conductivity, relax_rate, debye_strength, subgrids):
    first_x = fields[0, 0:3, 0:1]
    first_y = fields[0, 0:3, :, 0]
    slab_e, slab_h, slab_p, box, coef = call(
        prep_kernel,
        (fields,) * 3
        + (material,) * 3
        + (permittivity, conductivity, relax_rate, debye_strength, subgrids),
        [third((1, 9, 6, 24, 128), a) for a in range(3)]
        + [third((1, 6, 24, 128), a) for a in range(3)]
        + [SM] * 5,
        [PART] * 3 + [BOX, COEF],
        grid=(1,),
    )
    for number in range(COARSE_STEPS):
        next_x = shifted(first_x, "gx", -1)
        next_y = shifted(first_y, "gy", -1)
        slab_h, last_x, last_y = call(
            magnetic_kernel,
            (slab_e, slab_h, next_x, next_y),
            [VM] * 4,
            [PART, X_EDGE, Y_EDGE],
        )
        prev_x = shifted(last_x, "gx", 1)
        prev_y = shifted(last_y, "gy", 1)
        slab_e, slab_p, sent = call(
            electric_kernel,
            (slab_e, slab_h, slab_p, coef, prev_x, prev_y, subgrids),
            [VM] * 6 + [SM],
            [PART, PART, (2, *REGION)],
        )
        region = shifted(sent, "grid", 1)
        box, restricted = call(
            fine_kernel, (box, coef, region, subgrids), [VM] * 3 + [SM], [BOX, REGION]
        )
        received = shifted(restricted, "grid", -1)
        if number < COARSE_STEPS - 1:
            slab_e, first_x, first_y = call(
                overwrite_kernel,
                (slab_e, received, subgrids),
                [VM] * 2 + [SM],
                [PART, X_EDGE, Y_EDGE],
            )
    (out,) = call(
        finish_kernel,
        (slab_e, slab_h, slab_p, box, received, subgrids),
        [VM] * 5 + [SM],
        [SLAB],
        scratch=[pltpu.VMEM((9, 6, 3, 24, 128), F32)],
    )
    return out[None]


def solution(mesh):
    in_specs = (
        P("grid", None, "gx", "gy", None),
        P("grid", "gx", "gy", None),
        P(),
        P(),
        P(),
        P(),
        P("gx", "gy", None),
    )
    out_specs = P("grid", None, "gx", "gy", None)
    return jax.shard_map(body, mesh=mesh, in_specs=in_specs, out_specs=out_specs, check_vma=False)
```

```python
import functools

import jax
import jax.numpy as jnp
from jax import lax
from jax.experimental import pallas as pl
from jax.experimental.pallas import tpu as pltpu
from jax.sharding import PartitionSpec as P

COARSE_STEPS = 3
LIMIT = 40 * 1024 * 1024
VM = pl.BlockSpec(memory_space=pltpu.VMEM)
SM = pl.BlockSpec(memory_space=pltpu.SMEM)
F32 = jnp.float32


def shifted(value, axis, by):
    peers = lax.axis_size(axis)
    pairs = [(i, i + by) for i in range(peers) if 0 <= i + by < peers]
    return lax.ppermute(value, axis, pairs)


def lanes(shape=(8, 128)):
    return lax.broadcasted_iota(jnp.int32, shape, len(shape) - 1)


def rows(shape=(8, 128)):
    return lax.broadcasted_iota(jnp.int32, shape, len(shape) - 2)


def gather(tile, index):
    return jnp.take_along_axis(tile, index, axis=1)


def tables(perm, cond, relax, debye, factor):
    lane = lanes()

    def spread(ref):
        value = jnp.full((8, 128), ref[0], F32)
        for k in range(1, ref.shape[0]):
            value = jnp.where(lane == k, ref[k], value)
        return value

    eps = spread(perm)
    damp = spread(cond) * factor / (2.0 * eps)
    rate = spread(relax) * factor
    f0 = (1.0 - damp) / (1.0 + damp)
    f1 = 1.0 / (eps * (1.0 + damp))
    f3 = jnp.exp(-rate)
    f4 = spread(debye)
    c = f1 * rate
    return (f0 - c * f4, 0.5 * f1, c, f3, (1.0 - f3) * f4)


def to_tiles(parts):
    lane = lanes()
    kind = lane % 3
    out = []
    for t in range(3):
        mixed = jnp.where(
            kind == t, parts[0], jnp.where(kind == (t + 1) % 3, parts[1], parts[2])
        )
        out.append(gather(mixed, (3 * lane + t) & 127))
    return out


def from_tiles(tiles):
    lane = lanes()
    spread = [gather(tiles[t], (43 * (lane - t + 128)) & 127) for t in range(3)]
    out = []
    for a in range(3):
        kind = (2 * a + lane) % 3
        out.append(jnp.where(kind == 0, spread[0], jnp.where(kind == 1, spread[1], spread[2])))
    return out


def prep_kernel(f0, f1, f2, m0, m1, m2, perm, cond, relax, debye, sub, slab_e, slab_h, slab_p, box, coef):
    coarse = lax.axis_index("grid") == 0
    fields, material = (f0, f1, f2), (m0, m1, m2)

    @pl.when(coarse)
    def _():
        table = tables(perm, cond, relax, debye, 1.0)
        for x in range(6):
            for yt in range(3):
                for zt in range(3):
                    index = material[zt][0, x, pl.ds(8 * yt, 8)]
                    for k in range(5):
                        coef[k, x, 3 * yt + zt] = gather(table[k], index)
        for a in range(3):
            for k, part in enumerate((slab_e, slab_h, slab_p)):
                part[:, :, :, pl.ds(128 * a, 128)] = fields[a][0, 3 * k : 3 * k + 3]

    @pl.when(jnp.logical_not(coarse))
    def _():
        table = tables(perm, cond, relax, debye, F32(1.0 / 3.0))
        row, lane = rows(), lanes()
        ly, lz = sub[0, 0, 4], sub[0, 0, 5]
        within = (row < ly) & (lane < lz)
        for x in range(6):
            inside = within & (x < 3 * sub[0, 0, 3])
            for u in range(3):
                cut = pl.ds(u, 8, stride=3)
                parts = [material[a][0, x, cut] for a in range(3)]
                for t, index in enumerate(to_tiles(parts)):
                    for k in range(5):
                        coef[k, x, 3 * u + t] = gather(table[k], index)
                for c in range(9):
                    parts = [fields[a][0, c, x, cut] for a in range(3)]
                    for t, tile in enumerate(to_tiles(parts)):
                        box[c, x, 3 * u + t] = jnp.where(inside, tile, 0.0)


def whole(ref, *index):
    return jnp.concatenate(
        [
            jnp.concatenate([ref[(*index, 3 * yt + zt)] for zt in range(3)], axis=1)
            for yt in range(3)
        ],
        axis=0,
    )


def row_pair(sub):
    y0 = sub[0, 0, 1]
    base = pl.multiple_of(8 * jnp.minimum(y0 // 8, 1), 8)
    return base, y0 - base


def neighbour(da, db):
    a, b = lax.axis_index("gx") + da, lax.axis_index("gy") + db
    na, nb = lax.axis_size("gx"), lax.axis_size("gy")
    there = (a >= 0) & (a < na) & (b >= 0) & (b < nb)
    return there, jnp.clip(a, 0, na - 1) * nb + jnp.clip(b, 0, nb - 1)


def lay_over(wide, boxes, subs, da, db, kinds):
    there, block = neighbour(da, db)
    x0, y0, z0, lx, ly, lz = (subs[block, 0, k] for k in range(6))
    if da == 1:
        there = there & (x0 == 0)
    if da == -1:
        there = there & (x0 + lx == 6)
    if db == 1:
        there = there & (y0 == 0)
    if db == -1:
        there = there & (y0 + ly == 24)

    @pl.when(there)
    def _():
        base = pl.multiple_of(8 * jnp.minimum(y0 // 8, 1), 8)
        over = y0 - base
        row = rows((16, 128)) - over
        for a in range(3):
            index = (lanes() + (128 * a) - z0) & 127
            place = lanes((16, 128)) + (128 * a) - z0
            flat = (place >= 0) & (place < lz) & (row >= 0) & (row < ly)
            for i in range(2):
                covered = flat & (i < lx)
                for c in kinds:
                    spot = (
                        c,
                        6 + 6 * da + x0 + i,
                        pl.ds(24 + 24 * db + base, 16),
                        pl.ds(128 * a, 128),
                    )
                    tile = gather(boxes[block, c, i], index)
                    pair = pltpu.roll(jnp.concatenate([tile, tile]), over, 0)
                    wide[spot] = jnp.where(covered, pair, wide[spot])


def step_kernel(with_boxes, *refs):
    slab_e, slab_h, slab_p, coef, ax, ay, bx, by, d1, d2, sub = refs[:11]
    refs = refs[11:]
    if with_boxes:
        boxes, subs = refs[:2]
        refs = refs[2:]
    out_e, out_h, out_p, sent, oax, oay, obx, oby, od1, od2, wide = refs
    coarse = lax.axis_index("grid") == 0

    @pl.when(coarse)
    def _():
        row, lane = rows((24, 384)), lanes((24, 384))
        edge_lane = lanes((1, 384))
        own = pl.ds(24, 24)
        for c in range(3):
            for x in range(6):
                wide[c, 6 + x, own] = slab_e[c, x]
                wide[c, 6 + x, 23:24] = by[c, x : x + 1]
            wide[c, 5, own] = bx[c]
        for k, c in enumerate((1, 2)):
            wide[c, 12, own] = ax[k]
        for k, c in enumerate((0, 2)):
            for x in range(6):
                wide[c, 6 + x, 48:49] = ay[k, x : x + 1]
        wide[0, 5, 48:49] = d1[...]
        wide[1, 12, 23:24] = d2[...]
        if with_boxes:
            lay_over(wide, boxes, subs, 0, 0, (0, 1, 2))
            lay_over(wide, boxes, subs, 1, 0, (1, 2))
            lay_over(wide, boxes, subs, 0, 1, (0, 2))
            lay_over(wide, boxes, subs, -1, 0, (0, 1, 2))
            lay_over(wide, boxes, subs, 0, -1, (0, 1, 2))
            lay_over(wide, boxes, subs, -1, 1, (0,))
            lay_over(wide, boxes, subs, 1, -1, (1,))

        cut = region_of(wide, sub, 6, 24)
        for c in range(3):
            for i in range(2):
                sent[0, c, i] = cut(c, i)

        def ahead_y(value, edge):
            return jnp.where(row == 23, edge, pltpu.roll(value, 23, 0))

        def ahead_z(value):
            last = lanes(value.shape) == 383
            return jnp.where(last, 0.0, pltpu.roll(value, 383, 1))

        def behind_y(value, edge):
            return jnp.where(row == 0, edge, pltpu.roll(value, 1, 0))

        def behind_z(value):
            return jnp.where(lane == 0, 0.0, pltpu.roll(value, 1, 1))

        has_x = (lax.axis_index("gx") > 0).astype(F32)
        has_y = (lax.axis_index("gy") > 0).astype(F32)
        ex, ey, ez = (wide[c, 5, own] for c in range(3))
        hy_b = bx[3] - 0.5 * ((ahead_z(ex) - ex) - (wide[2, 6, own] - ez))
        hz_b = bx[4] - 0.5 * ((wide[1, 6, own] - ey) - (ahead_y(ex, wide[0, 5, 48:49]) - ex))
        hy_b, hz_b = hy_b * has_x, hz_b * has_x
        for x in range(6):
            ex, ey, ez = (wide[c, 6 + x, own] for c in range(3))
            ey_x, ez_x = wide[1, 7 + x, own], wide[2, 7 + x, own]
            ex_y = ahead_y(ex, wide[0, 6 + x, 48:49])
            ez_y = ahead_y(ez, wide[2, 6 + x, 48:49])
            ex_z, ey_z = ahead_z(ex), ahead_z(ey)
            hx = slab_h[0, x] - 0.5 * ((ez_y - ez) - (ey_z - ey))
            hy = slab_h[1, x] - 0.5 * ((ex_z - ex) - (ez_x - ez))
            hz = slab_h[2, x] - 0.5 * ((ey_x - ey) - (ex_y - ex))
            out_h[0, x], out_h[1, x], out_h[2, x] = hx, hy, hz
            ex_r, ey_r, ez_r = (wide[c, 6 + x, 23:24] for c in range(3))
            hx_r = by[3, x : x + 1] - 0.5 * ((ez[0:1] - ez_r) - (ahead_z(ey_r) - ey_r))
            hz_r = by[4, x : x + 1] - 0.5 * ((wide[1, 7 + x, 23:24] - ey_r) - (ex[0:1] - ex_r))
            hx_y = behind_y(hx, hx_r * has_y)
            hz_y = behind_y(hz, hz_r * has_y)
            hx_z, hy_z = behind_z(hx), behind_z(hy)
            rotation = (
                (hz - hz_y) - (hy - hy_z),
                (hx - hx_z) - (hz - hz_b),
                (hy - hy_b) - (hx - hx_y),
            )
            hy_b, hz_b = hy, hz
            a, b, p, f3, g = (whole(coef, k, x) for k in range(5))
            for c, old_e in enumerate((ex, ey, ez)):
                old = slab_p[c, x]
                new = a * old_e + b * rotation[c] + p * old
                out_e[c, x] = new
                out_p[c, x] = f3 * old + g * new
                if x == 5:
                    obx[c] = new
                if x == 0 and c > 0:
                    oax[c - 1] = new
                oby[c, x : x + 1] = new[23:24]
                if c != 1:
                    oay[c // 2, x : x + 1] = new[0:1]
                if c == 0 and x == 5:
                    od1[...] = new[0:1]
                if c == 1 and x == 0:
                    od2[...] = new[23:24]
            oby[3, x : x + 1] = hx[23:24]
            oby[4, x : x + 1] = hz[23:24]
            if x == 5:
                obx[3], obx[4] = hy, hz
        cut = region_of(out_e, sub, 0, 0)
        for c in range(3):
            for i in range(2):
                sent[1, c, i] = cut(c, i)


def region_of(slab, sub, x_base, y_base):
    x0, z0 = sub[0, 0, 0], sub[0, 0, 2]
    base, over = row_pair(sub)
    place = lanes() + z0
    index, part = place & 127, place >> 7

    def cut(c, i):
        tiles = []
        for a in range(3):
            pair = slab[c, x_base + x0 + i, pl.ds(y_base + base, 16), pl.ds(128 * a, 128)]
            tiles.append(gather(pltpu.roll(pair, (16 - over) & 15, 0)[0:8], index))
        return jnp.where(part == 0, tiles[0], jnp.where(part == 1, tiles[1], tiles[2]))

    return cut


def put_back(slab, received, sub):
    x0, z0 = sub[0, 0, 0], sub[0, 0, 2]
    lx, ly, lz = sub[0, 0, 3], sub[0, 0, 4], sub[0, 0, 5]
    base, over = row_pair(sub)
    row, lane = rows((16, 128)) - over, lanes()
    for i in range(2):
        for a in range(3):
            place = lane + (128 * a) - z0
            index = place & 127
            wide = lanes((16, 128)) + (128 * a) - z0
            covered = (wide >= 0) & (wide < lz) & (row >= 0) & (row < ly) & (i < lx)
            for c in range(3):
                spot = (c, x0 + i, pl.ds(base, 16), pl.ds(128 * a, 128))
                tile = gather(received[c, i], index)
                pair = pltpu.roll(jnp.concatenate([tile, tile]), over, 0)
                slab[spot] = jnp.where(covered, pair, slab[spot])


def fine_kernel(box_in, coef, region, sub, box, restricted):
    coarse = lax.axis_index("grid") == 0

    @pl.when(jnp.logical_not(coarse))
    def _():
        box[...] = box_in[...]
        row, lane = rows(), lanes()
        lx, ly, lz = sub[0, 0, 3], sub[0, 0, 4], sub[0, 0, 5]
        within = (row < ly) & (lane < lz)
        inside = [within, within & (lx == 2)]
        y_face = [row == 0, None, row == ly - 1]
        z_face = [lane == 0, None, lane == lz - 1]

        def up(value):
            return jnp.where(row == 7, 0.0, pltpu.roll(value, 7, 0))

        def left(value):
            return jnp.where(lane == 127, 0.0, pltpu.roll(value, 127, 1))

        def down(value):
            return jnp.where(row == 0, 0.0, pltpu.roll(value, 1, 0))

        def right(value):
            return jnp.where(lane == 0, 0.0, pltpu.roll(value, 1, 1))

        def ahead_y(values, u, t):
            return values[3 * u + 3 + t] if u < 2 else up(values[t])

        def ahead_z(values, u, t):
            return values[3 * u + t + 1] if t < 2 else left(values[3 * u])

        def behind_y(values, u, t):
            return values[3 * u - 3 + t] if u > 0 else down(values[6 + t])

        def behind_z(values, u, t):
            return values[3 * u + t - 1] if t > 0 else right(values[3 * u + 2])

        def either(p, q):
            if p is None:
                return q
            return p if q is None else p | q

        zero = jnp.zeros((8, 128), F32)

        def substep(number, carry):
            weight = (number.astype(F32) + 1.0) / 3.0
            driven = [
                [region[0, c, i] + weight * (region[1, c, i] - region[0, c, i]) for i in range(2)]
                for c in range(3)
            ]
            for x in range(6):
                part = x // 3
                e = [[box[c, x, k] for k in range(9)] for c in range(3)]
                if x < 5:
                    ey_x = [box[1, x + 1, k] for k in range(9)]
                    ez_x = [box[2, x + 1, k] for k in range(9)]
                else:
                    ey_x = ez_x = [zero] * 9
                h = [[], [], []]
                for u in range(3):
                    for t in range(3):
                        k = 3 * u + t
                        ex, ey, ez = e[0][k], e[1][k], e[2][k]
                        turn = (
                            (ahead_y(e[2], u, t) - ez) - (ahead_z(e[1], u, t) - ey),
                            (ahead_z(e[0], u, t) - ex) - (ez_x[k] - ez),
                            (ey_x[k] - ey) - (ahead_y(e[0], u, t) - ex),
                        )
                        for c in range(3):
                            value = box[3 + c, x, k] - 0.5 * turn[c]
                            box[3 + c, x, k] = value
                            h[c].append(value)
                x_face = x == 0
                if x in (2, 5):
                    x_face = jnp.full((8, 128), 3 * lx - 1, jnp.int32) == x
                for u in range(3):
                    for t in range(3):
                        k = 3 * u + t
                        hx, hy, hz = h[0][k], h[1][k], h[2][k]
                        hy_x = box[4, x - 1, k] if x > 0 else zero
                        hz_x = box[5, x - 1, k] if x > 0 else zero
                        rotation = (
                            (hz - behind_y(h[2], u, t)) - (hy - behind_z(h[1], u, t)),
                            (hx - behind_z(h[0], u, t)) - (hz - hz_x),
                            (hy - hy_x) - (hx - behind_y(h[0], u, t)),
                        )
                        a, b, p, f3, g = (coef[q, x, k] for q in range(5))
                        faces = (
                            either(y_face[u], z_face[t]),
                            None if x_face is True else either(x_face if x in (2, 5) else None, z_face[t]),
                            None if x_face is True else either(x_face if x in (2, 5) else None, y_face[u]),
                        )
                        for c in range(3):
                            old = box[6 + c, x, k]
                            new = a * e[c][k] + b * rotation[c] + p * old
                            if c > 0 and x_face is True:
                                new = driven[c][part]
                            elif faces[c] is not None:
                                new = jnp.where(faces[c], driven[c][part], new)
                            new = jnp.where(inside[part], new, 0.0)
                            box[c, x, k] = new
                            box[6 + c, x, k] = f3 * old + g * new
            return carry

        lax.fori_loop(0, 3, substep, 0)
        for c in range(3):
            for i in range(2):
                total = zero
                for x in range(3 * i, 3 * i + 3):
                    for k in range(9):
                        total = total + box[c, x, k]
                restricted[c, i] = total * F32(1.0 / 27.0)


def finish_kernel(slab_e, slab_h, slab_p, box, received, sub, out, mixed):
    coarse = lax.axis_index("grid") == 0

    @pl.when(coarse)
    def _():
        for k, part in enumerate((slab_e, slab_h, slab_p)):
            out[3 * k : 3 * k + 3] = part[...]
        put_back(out, received, sub)

    @pl.when(jnp.logical_not(coarse))
    def _():
        for c in range(9):
            for x in range(6):
                for u in range(3):
                    parts = from_tiles([box[c, x, 3 * u + t] for t in range(3)])
                    for a in range(3):
                        mixed[c, x, a, pl.ds(u, 8, stride=3)] = parts[a]
                for a in range(3):
                    out[c, x, :, pl.ds(128 * a, 128)] = mixed[c, x, a]


def third(shape, a):
    return pl.BlockSpec(shape, lambda i: (0,) * (len(shape) - 1) + (a,))


def call(kernel, operands, specs, outs, scratch=(), grid=()):
    params = pltpu.CompilerParams(vmem_limit_bytes=LIMIT)
    return pl.pallas_call(
        kernel,
        out_shape=[jax.ShapeDtypeStruct(shape, F32) for shape in outs],
        in_specs=specs,
        out_specs=[VM] * len(outs),
        grid=grid,
        scratch_shapes=scratch,
        compiler_params=params,
    )(*operands)


PART = (3, 6, 24, 384)
SLAB = (9, 6, 24, 384)
BOX = (9, 6, 9, 8, 128)
COEF = (5, 6, 9, 8, 128)
REGION = (3, 2, 8, 128)
EDGES = [(2, 24, 384), (2, 6, 384), (5, 24, 384), (5, 6, 384), (1, 384), (1, 384)]
WAYS = [(-1, 0), (0, -1), (1, 0), (0, 1), (1, -1), (-1, 1)]
AXES = ("grid", "gx", "gy")


def between_coarse(value, da, db):
    na, nb = lax.axis_size("gx"), lax.axis_size("gy")
    pairs = [
        (a * nb + b, (a + da) * nb + b + db)
        for a in range(na)
        for b in range(nb)
        if 0 <= a + da < na and 0 <= b + db < nb
    ]
    return lax.ppermute(value, AXES, pairs)


def body(fields, material, permittivity, conductivity, relax_rate, debye_strength, subgrids):
    blocks = lax.axis_size("gx") * lax.axis_size("gy")
    subs = lax.all_gather(subgrids[0], ("gx", "gy"))
    f = fields[0]
    edges = [
        f[1:3, 0],
        f[0:3:2, :, 0],
        jnp.concatenate([f[0:3, 5], f[4:6, 5]]),
        jnp.concatenate([f[0:4, :, 23], f[5:6, :, 23]]),
        f[0, 5, 0:1],
        f[1, 0, 23:24],
    ]
    slab_e, slab_h, slab_p, box, coef = call(
        prep_kernel,
        (fields,) * 3
        + (material,) * 3
        + (permittivity, conductivity, relax_rate, debye_strength, subgrids),
        [third((1, 9, 6, 24, 128), a) for a in range(3)]
        + [third((1, 6, 24, 128), a) for a in range(3)]
        + [SM] * 5,
        [PART] * 3 + [BOX, COEF],
        grid=(1,),
    )
    boxes = None
    for number in range(COARSE_STEPS):
        edges = [between_coarse(edge, *way) for edge, way in zip(edges, WAYS)]
        extra = () if number == 0 else (boxes, subs)
        slab_e, slab_h, slab_p, sent, *edges = call(
            functools.partial(step_kernel, number > 0),
            (slab_e, slab_h, slab_p, coef, *edges, subgrids, *extra),
            [VM] * 10 + [SM] + [VM, SM][: len(extra)],
            [PART] * 3 + [(2, *REGION)] + EDGES,
            scratch=[pltpu.VMEM((3, 18, 72, 384), F32)],
        )
        region = shifted(sent, "grid", 1)
        box, restricted = call(
            fine_kernel, (box, coef, region, subgrids), [VM] * 3 + [SM], [BOX, REGION]
        )
        if number < COARSE_STEPS - 1:
            boxes = lax.all_gather(restricted, AXES)[blocks:]
    received = shifted(restricted, "grid", -1)
    (out,) = call(
        finish_kernel,
        (slab_e, slab_h, slab_p, box, received, subgrids),
        [VM] * 5 + [SM],
        [SLAB],
        scratch=[pltpu.VMEM((9, 6, 3, 24, 128), F32)],
    )
    return out[None]


def solution(mesh):
    in_specs = (
        P("grid", None, "gx", "gy", None),
        P("grid", "gx", "gy", None),
        P(),
        P(),
        P(),
        P(),
        P("gx", "gy", None),
    )
    out_specs = P("grid", None, "gx", "gy", None)
    return jax.shard_map(body, mesh=mesh, in_specs=in_specs, out_specs=out_specs, check_vma=False)
```

```python
import functools

import jax
import jax.numpy as jnp
from jax import lax
from jax.experimental import pallas as pl
from jax.experimental.pallas import tpu as pltpu
from jax.sharding import PartitionSpec as P

COARSE_STEPS = 3
LIMIT = 40 * 1024 * 1024
VM = pl.BlockSpec(memory_space=pltpu.VMEM)
SM = pl.BlockSpec(memory_space=pltpu.SMEM)
F32 = jnp.float32


def shifted(value, axis, by):
    peers = lax.axis_size(axis)
    pairs = [(i, i + by) for i in range(peers) if 0 <= i + by < peers]
    return lax.ppermute(value, axis, pairs)


def lanes(shape=(8, 128)):
    return lax.broadcasted_iota(jnp.int32, shape, len(shape) - 1)


def rows(shape=(8, 128)):
    return lax.broadcasted_iota(jnp.int32, shape, len(shape) - 2)


def gather(tile, index):
    return jnp.take_along_axis(tile, index, axis=1)


def tables(perm, cond, relax, debye, factor):
    lane = lanes()

    def spread(ref):
        value = jnp.full((8, 128), ref[0], F32)
        for k in range(1, ref.shape[0]):
            value = jnp.where(lane == k, ref[k], value)
        return value

    eps = spread(perm)
    damp = spread(cond) * factor / (2.0 * eps)
    rate = spread(relax) * factor
    f0 = (1.0 - damp) / (1.0 + damp)
    f1 = 1.0 / (eps * (1.0 + damp))
    f3 = jnp.exp(-rate)
    f4 = spread(debye)
    c = f1 * rate
    return (f0 - c * f4, 0.5 * f1, c, f3, (1.0 - f3) * f4)


def to_tiles(parts):
    lane = lanes()
    kind = lane % 3
    out = []
    for t in range(3):
        mixed = jnp.where(
            kind == t, parts[0], jnp.where(kind == (t + 1) % 3, parts[1], parts[2])
        )
        out.append(gather(mixed, (3 * lane + t) & 127))
    return out


def from_tiles(tiles):
    lane = lanes()
    spread = [gather(tiles[t], (43 * (lane - t + 128)) & 127) for t in range(3)]
    out = []
    for a in range(3):
        kind = (2 * a + lane) % 3
        out.append(jnp.where(kind == 0, spread[0], jnp.where(kind == 1, spread[1], spread[2])))
    return out


def prep_kernel(f0, f1, f2, m0, m1, m2, perm, cond, relax, debye, sub, e, h, p, box, coef, desc, wide):
    coarse = lax.axis_index("grid") == 0
    fields, material = (f0, f1, f2), (m0, m1, m2)
    for k in range(6):
        desc[k] = jnp.full((8, 128), sub[0, 0, k], jnp.int32)

    @pl.when(coarse)
    def _():
        table = tables(perm, cond, relax, debye, 1.0)
        for x in range(6):
            for yt in range(3):
                for zt in range(3):
                    index = material[zt][0, x, pl.ds(8 * yt, 8)]
                    for k in range(5):
                        coef[k, x, 3 * yt + zt] = gather(table[k], index)
        for a in range(3):
            for k, part in enumerate((e, h, p)):
                part[:, :, :, pl.ds(128 * a, 128)] = fields[a][0, 3 * k : 3 * k + 3]

    @pl.when(jnp.logical_not(coarse))
    def _():
        for k, tile in enumerate(tables(perm, cond, relax, debye, 1.0)):
            wide[k] = tile
        table = tables(perm, cond, relax, debye, F32(1.0 / 3.0))
        row, lane = rows(), lanes()
        ly, lz = sub[0, 0, 4], sub[0, 0, 5]
        within = (row < ly) & (lane < lz)
        for x in range(6):
            inside = within & (x < 3 * sub[0, 0, 3])
            for u in range(3):
                cut = pl.ds(u, 8, stride=3)
                parts = [material[a][0, x, cut] for a in range(3)]
                for t, index in enumerate(to_tiles(parts)):
                    for k in range(5):
                        coef[k, x, 3 * u + t] = gather(table[k], index)
                for c in range(9):
                    parts = [fields[a][0, c, x, cut] for a in range(3)]
                    for t, tile in enumerate(to_tiles(parts)):
                        box[c, x, 3 * u + t] = jnp.where(inside, tile, 0.0)


def whole(ref, *index):
    return jnp.concatenate(
        [
            jnp.concatenate([ref[(*index, 3 * yt + zt)] for zt in range(3)], axis=1)
            for yt in range(3)
        ],
        axis=0,
    )


def magnetic(e, h, next_x, next_y, out):
    row, lane = rows((24, 384)), lanes((24, 384))

    def ahead_y(value, edge):
        return jnp.where(row == 23, edge, pltpu.roll(value, 23, 0))

    def ahead_z(value):
        return jnp.where(lane == 383, 0.0, pltpu.roll(value, 383, 1))

    for x in range(6):
        ex, ey, ez = (e[c, x] for c in range(3))
        if x < 5:
            ey_x, ez_x = e[1, x + 1], e[2, x + 1]
        else:
            ey_x, ez_x = next_x(0), next_x(1)
        ex_y = ahead_y(ex, next_y(0, x))
        ez_y = ahead_y(ez, next_y(1, x))
        ex_z, ey_z = ahead_z(ex), ahead_z(ey)
        turn = ((ez_y - ez) - (ey_z - ey), (ex_z - ex) - (ez_x - ez), (ey_x - ey) - (ex_y - ex))
        for c in range(3):
            if h is None:
                out[c, x] = -0.5 * turn[c]
            else:
                out[c, x] = h[c, x] - 0.5 * turn[c]


def last_layers(h, out_x, out_y):
    out_x[0], out_x[1] = h[1, 5], h[2, 5]
    for x in range(6):
        out_y[0, x : x + 1] = h[0, x, 23:24]
        out_y[1, x : x + 1] = h[2, x, 23:24]


def first_layers(e, out_x, out_y):
    out_x[0], out_x[1] = e[1, 0], e[2, 0]
    for x in range(6):
        out_y[0, x : x + 1] = e[0, x, 0:1]
        out_y[1, x : x + 1] = e[2, x, 0:1]


def curl_behind(h, x, prev_x, prev_y):
    row, lane = rows((24, 384)), lanes((24, 384))

    def behind_y(value, edge):
        return jnp.where(row == 0, edge, pltpu.roll(value, 1, 0))

    def behind_z(value):
        return jnp.where(lane == 0, 0.0, pltpu.roll(value, 1, 1))

    hx, hy, hz = (h[c, x] for c in range(3))
    if isinstance(x, int):
        hy_x, hz_x = (h[1, x - 1], h[2, x - 1]) if x > 0 else (prev_x(0), prev_x(1))
    else:
        before = jnp.maximum(x - 1, 0)
        first = jnp.full((24, 384), x, jnp.int32) == 0
        hy_x = jnp.where(first, prev_x(0), h[1, before])
        hz_x = jnp.where(first, prev_x(1), h[2, before])
    hx_y = behind_y(hx, prev_y(0, x))
    hz_y = behind_y(hz, prev_y(1, x))
    hx_z, hy_z = behind_z(hx), behind_z(hy)
    return ((hz - hz_y) - (hy - hy_z), (hx - hx_z) - (hz - hz_x), (hy - hy_x) - (hx - hx_y))


def electric(e, h, p, coef, prev_x, prev_y, out_e, out_p, more=None):
    for x in range(6):
        rotation = curl_behind(h, x, prev_x, prev_y)
        a, b, q, f3, g = (whole(coef, k, x) for k in range(5))
        for c in range(3):
            new = a * e[c, x] + b * rotation[c]
            old = None if p is None else p[c, x]
            if old is not None:
                new = new + q * old
            last = g * new if old is None else f3 * old + g * new
            if more is not None:
                new, last = new + more[0][c, x], last + more[1][c, x]
            out_e[c, x] = new
            out_p[c, x] = last


def edge_x(ref):
    return lambda k: ref[k]


def edge_y(ref):
    return lambda k, x: ref[k, pl.ds(x, 1)]


def corner(desc):
    x0 = jnp.max(desc[0].astype(F32)).astype(jnp.int32)
    y0 = jnp.max(desc[1].astype(F32)).astype(jnp.int32)
    base = pl.multiple_of(8 * jnp.minimum(y0 // 8, 1), 8)
    return x0, base, y0 - base


def cut_region(e, desc, spot):
    x0, base, over = spot
    place = lanes() + desc[2]
    index, part = place & 127, place >> 7

    def cut(c, i):
        tiles = []
        for a in range(3):
            pair = e[c, x0 + i, pl.ds(base, 16), pl.ds(128 * a, 128)]
            tiles.append(gather(pltpu.roll(pair, (16 - over) & 15, 0)[0:8], index))
        return jnp.where(part == 0, tiles[0], jnp.where(part == 1, tiles[1], tiles[2]))

    return [[cut(c, i) for i in range(2)] for c in range(3)]


def covered_of(desc):
    within = (rows() < desc[4]) & (lanes() < desc[5])
    return [within & (desc[3] > i) for i in range(2)]


def put(e, values, desc, spot, replace=None):
    x0, base, over = spot
    empty = jnp.zeros((8, 128), F32)
    for a in range(3):
        place = lanes() + (128 * a) - desc[2]
        index = place & 127
        here = (place >= 0) & (place < 128)
        for i in range(2):
            keep = None
            if replace is not None:
                keep = jnp.where(here, gather(replace[i], index), 0.0)
                keep = pltpu.roll(jnp.concatenate([keep, empty]), over, 0) > 0.5
            for c in range(3):
                spot = (c, x0 + i, pl.ds(base, 16), pl.ds(128 * a, 128))
                tile = jnp.where(here, gather(values(c, i), index), 0.0)
                pair = pltpu.roll(jnp.concatenate([tile, empty]), over, 0)
                if replace is None:
                    e[spot] = e[spot] + pair
                else:
                    e[spot] = jnp.where(keep, pair, e[spot])


def pack(out, box, in_x, in_y, at=0):
    if box is not None:
        for c in range(3):
            for i in range(2):
                out[pl.ds(8 * i, 8), pl.ds(128 * c, 128)] = box[c][i]
        at += 16
    for k in range(2):
        out[pl.ds(at + 24 * k, 24)] = in_x[k]
        out[pl.ds(at + 48 + 8 * k, 6)] = in_y[k]


def packed_box(ref):
    return lambda c, i: ref[pl.ds(8 * i, 8), pl.ds(128 * c, 128)]


def packed_x(ref, at):
    return lambda k: ref[pl.ds(at + 24 * k, 24)]


def packed_y(ref, at):
    return lambda k, x: ref[pl.ds(at + 48 + 8 * k + x, 1)]


def fine_steps(box, coef, desc, earlier, latest):
    row, lane = rows(), lanes()
    lx, ly, lz = desc[3], desc[4], desc[5]
    inside = covered_of(desc)
    y_face = [row == 0, None, row == ly - 1]
    z_face = [lane == 0, None, lane == lz - 1]

    def up(value):
        return jnp.where(row == 7, 0.0, pltpu.roll(value, 7, 0))

    def left(value):
        return jnp.where(lane == 127, 0.0, pltpu.roll(value, 127, 1))

    def down(value):
        return jnp.where(row == 0, 0.0, pltpu.roll(value, 1, 0))

    def right(value):
        return jnp.where(lane == 0, 0.0, pltpu.roll(value, 1, 1))

    def ahead_y(values, u, t):
        return values[3 * u + 3 + t] if u < 2 else up(values[t])

    def ahead_z(values, u, t):
        return values[3 * u + t + 1] if t < 2 else left(values[3 * u])

    def behind_y(values, u, t):
        return values[3 * u - 3 + t] if u > 0 else down(values[6 + t])

    def behind_z(values, u, t):
        return values[3 * u + t - 1] if t > 0 else right(values[3 * u + 2])

    def either(p, q):
        if p is None:
            return q
        return p if q is None else p | q

    zero = jnp.zeros((8, 128), F32)

    def substep(number, carry):
        weight = (number.astype(F32) + 1.0) / 3.0
        driven = [
            [earlier[c][i] + weight * (latest[c][i] - earlier[c][i]) for i in range(2)]
            for c in range(3)
        ]
        for x in range(6):
            part = x // 3
            e = [[box[c, x, k] for k in range(9)] for c in range(3)]
            if x < 5:
                ey_x = [box[1, x + 1, k] for k in range(9)]
                ez_x = [box[2, x + 1, k] for k in range(9)]
            else:
                ey_x = ez_x = [zero] * 9
            h = [[], [], []]
            for u in range(3):
                for t in range(3):
                    k = 3 * u + t
                    ex, ey, ez = e[0][k], e[1][k], e[2][k]
                    turn = (
                        (ahead_y(e[2], u, t) - ez) - (ahead_z(e[1], u, t) - ey),
                        (ahead_z(e[0], u, t) - ex) - (ez_x[k] - ez),
                        (ey_x[k] - ey) - (ahead_y(e[0], u, t) - ex),
                    )
                    for c in range(3):
                        value = box[3 + c, x, k] - 0.5 * turn[c]
                        box[3 + c, x, k] = value
                        h[c].append(value)
            x_face = x == 0
            if x in (2, 5):
                x_face = 3 * lx - 1 == x
            for u in range(3):
                for t in range(3):
                    k = 3 * u + t
                    hx, hy, hz = h[0][k], h[1][k], h[2][k]
                    hy_x = box[4, x - 1, k] if x > 0 else zero
                    hz_x = box[5, x - 1, k] if x > 0 else zero
                    rotation = (
                        (hz - behind_y(h[2], u, t)) - (hy - behind_z(h[1], u, t)),
                        (hx - behind_z(h[0], u, t)) - (hz - hz_x),
                        (hy - hy_x) - (hx - behind_y(h[0], u, t)),
                    )
                    a, b, p, f3, g = (coef[q, x, k] for q in range(5))
                    faces = (
                        either(y_face[u], z_face[t]),
                        None if x_face is True else either(x_face if x in (2, 5) else None, z_face[t]),
                        None if x_face is True else either(x_face if x in (2, 5) else None, y_face[u]),
                    )
                    for c in range(3):
                        old = box[6 + c, x, k]
                        new = a * e[c][k] + b * rotation[c] + p * old
                        if c > 0 and x_face is True:
                            new = driven[c][part]
                        elif faces[c] is not None:
                            new = jnp.where(faces[c], driven[c][part], new)
                        new = jnp.where(inside[part], new, 0.0)
                        box[c, x, k] = new
                        box[6 + c, x, k] = f3 * old + g * new
        return carry

    lax.fori_loop(0, 3, substep, 0)
    restricted = [[zero, zero] for c in range(3)]
    for c in range(3):
        for i in range(2):
            total = zero
            for x in range(3 * i, 3 * i + 3):
                for k in range(9):
                    total = total + box[c, x, k]
            restricted[c][i] = total * F32(1.0 / 27.0)
    return restricted


def feed_back(restricted, latest, desc):
    covered = covered_of(desc)
    after = [[jnp.where(covered[i], restricted[c][i], latest[c][i]) for i in range(2)] for c in range(3)]
    return after, [[after[c][i] - latest[c][i] for i in range(2)] for c in range(3)]


def store_box(ref, values):
    for c in range(3):
        for i in range(2):
            ref[c, i] = values[c][i]


def load_box(ref):
    return [[ref[c, i] for i in range(2)] for c in range(3)]


def is_coarse():
    return lax.axis_index("grid") == 0


def is_fine():
    return lax.axis_index("grid") == 1


def h1_kernel(e, h, ax, ay, out_h, bx, by):
    @pl.when(is_coarse())
    def _():
        magnetic(e, h, edge_x(ax), edge_y(ay), out_h)
        last_layers(out_h, bx, by)


def e1_kernel(e, h, p, coef, bx, by, desc, out_e, out_p, ax, ay, sent):
    @pl.when(is_coarse())
    def _():
        spot = corner(desc)
        before = cut_region(e, desc, spot)
        electric(e, h, p, coef, edge_x(bx), edge_y(by), out_e, out_p)
        first_layers(out_e, ax, ay)
        after = cut_region(out_e, desc, spot)
        for c in range(3):
            for i in range(2):
                sent[0, c, i] = before[c][i]
                sent[1, c, i] = after[c][i]


def h2_kernel(e, h, ax, ay, box_in, coef, region, desc, out_e, out_h, bx, by, box, now, change):
    @pl.when(is_coarse())
    def _():
        out_e[...] = e[...]
        magnetic(e, h, edge_x(ax), edge_y(ay), out_h)
        last_layers(out_h, bx, by)

    @pl.when(is_fine())
    def _():
        box[...] = box_in[...]
        out_e[...] = jnp.zeros(out_e.shape, F32)
        out_h[...] = jnp.zeros(out_h.shape, F32)
        earlier = [[region[0, c, i] for i in range(2)] for c in range(3)]
        latest = [[region[1, c, i] for i in range(2)] for c in range(3)]
        restricted = fine_steps(box, coef, desc, earlier, latest)
        after, delta = feed_back(restricted, latest, desc)
        store_box(now, after)
        store_box(change, delta)
        put(out_e, lambda c, i: delta[c][i], desc, corner(desc))


def e2_kernel(e, h, p, coef, bx, by, desc, material, table, out_e, out_p, ax, ay, sent, wide_coef):
    @pl.when(is_coarse())
    def _():
        electric(e, h, p, coef, edge_x(bx), edge_y(by), out_e, out_p)
        first_layers(out_e, ax, ay)
        store_box(sent, cut_region(out_e, desc, corner(desc)))

    @pl.when(is_fine())
    def _():
        out_e[...] = e[...]
        out_p[...] = jnp.zeros(out_p.shape, F32)
        first_layers(e, ax, ay)
        tiles = [table[k] for k in range(5)]
        for x in range(6):
            for yt in range(3):
                for zt in range(3):
                    index = material[0, x, pl.ds(8 * yt, 8), pl.ds(128 * zt, 128)]
                    for k in range(5):
                        wide_coef[k, x, 3 * yt + zt] = gather(tiles[k], index)


def h3_kernel(e, h, ax, ay, change, out_h, bx, by, relay):
    magnetic(e, h, edge_x(ax), edge_y(ay), out_h)
    last_layers(out_h, bx, by)

    @pl.when(is_fine())
    def _():
        pack(relay, load_box(change), ax, ay)


def e3_kernel(
    e, h, p, coef, wide_coef, bx, by, desc, box_in, region, was,
    out_e, out_p, ax, ay, sent, box, now, relay,
):
    @pl.when(is_coarse())
    def _():
        electric(e, h, p, coef, edge_x(bx), edge_y(by), out_e, out_p)
        store_box(sent, cut_region(out_e, desc, corner(desc)))

    @pl.when(is_fine())
    def _():
        box[...] = box_in[...]
        spot = corner(desc)
        electric(e, h, p, wide_coef, edge_x(bx), edge_y(by), out_e, out_p)
        fix = cut_region(out_e, desc, spot)
        latest = [[region[c, i] + fix[c][i] for i in range(2)] for c in range(3)]
        restricted = fine_steps(box, coef, desc, load_box(was), latest)
        after, delta = feed_back(restricted, latest, desc)
        store_box(now, after)
        put(out_e, lambda c, i: delta[c][i], desc, spot)
        first_layers(out_e, ax, ay)
        pack(relay, delta, bx, by)


def h4_kernel(e, h, ax, ay, out_h, bx, by, relay):
    @pl.when(is_fine())
    def _():
        magnetic(e, h, edge_x(ax), edge_y(ay), out_h)
        last_layers(out_h, bx, by)
        pack(relay, None, ax, ay)


def e4_kernel(e, h, p, coef, wide_coef, bx, by, desc, box_in, region, was, box, relay, layer):
    @pl.when(is_fine())
    def _():
        box[...] = box_in[...]
        spot = corner(desc)
        x0 = spot[0]
        for i in range(2):
            x = x0 + i
            rotation = curl_behind(h, x, edge_x(bx), edge_y(by))
            a, b, q = (whole(wide_coef, k, x) for k in range(3))
            for c in range(3):
                layer[c, i] = a * e[c, x] + b * rotation[c] + q * p[c, x]
        fix = cut_region(layer, desc, (0, *spot[1:]))
        latest = [[region[c, i] + fix[c][i] for i in range(2)] for c in range(3)]
        restricted = fine_steps(box, coef, desc, load_box(was), latest)
        pack(relay, restricted, bx, by)


def redo_kernel(coef, desc, relay1, relay2, relay3, out_e, out_h, out_p, one_e, one_h):
    @pl.when(is_coarse())
    def _():
        spot = corner(desc)
        one_e[...] = jnp.zeros(one_e.shape, F32)
        put(one_e, packed_box(relay1), desc, spot)
        magnetic(one_e, None, packed_x(relay1, 16), packed_y(relay1, 16), one_h)
        electric(
            one_e, one_h, None, coef, packed_x(relay2, 16), packed_y(relay2, 16), out_e, out_p
        )
        put(out_e, packed_box(relay2), desc, spot)
        magnetic(out_e, one_h, packed_x(relay3, 0), packed_y(relay3, 0), out_h)


def finish_kernel(e, h, p, fix_e, fix_h, fix_p, coef, desc, relay, box, out, mixed):
    @pl.when(is_coarse())
    def _():
        view_e, view_p = out.at[pl.ds(0, 3)], out.at[pl.ds(6, 3)]
        electric(
            fix_e, fix_h, fix_p, coef, packed_x(relay, 16), packed_y(relay, 16),
            view_e, view_p, (e, p),
        )
        out[3:6] = h[...] + fix_h[...]
        covered = [jnp.where(value, F32(1.0), 0.0) for value in covered_of(desc)]
        put(view_e, packed_box(relay), desc, corner(desc), covered)

    @pl.when(is_fine())
    def _():
        for c in range(9):
            for x in range(6):
                for u in range(3):
                    parts = from_tiles([box[c, x, 3 * u + t] for t in range(3)])
                    for a in range(3):
                        mixed[c, x, a, pl.ds(u, 8, stride=3)] = parts[a]
                for a in range(3):
                    out[c, x, :, pl.ds(128 * a, 128)] = mixed[c, x, a]


def third(shape, a):
    return pl.BlockSpec(shape, lambda i: (0,) * (len(shape) - 1) + (a,))


def call(kernel, operands, outs, specs=None, scratch=(), grid=()):
    shapes = [out if isinstance(out, jax.ShapeDtypeStruct) else jax.ShapeDtypeStruct(out, F32) for out in outs]
    return pl.pallas_call(
        kernel,
        out_shape=shapes,
        in_specs=specs or [VM] * len(operands),
        out_specs=[VM] * len(outs),
        grid=grid,
        scratch_shapes=scratch,
        compiler_params=pltpu.CompilerParams(vmem_limit_bytes=LIMIT),
    )(*operands)


PART = (3, 6, 24, 384)
SLAB = (9, 6, 24, 384)
BOX = (9, 6, 9, 8, 128)
COEF = (5, 6, 9, 8, 128)
REGION = (3, 2, 8, 128)
X_EDGE = (2, 24, 384)
Y_EDGE = (2, 6, 384)
EDGES = [X_EDGE, Y_EDGE]
AXES = ("grid", "gx", "gy")


def exchange(x_edge, y_edge, by, groups):
    na, nb = lax.axis_size("gx"), lax.axis_size("gy")

    def pairs(da, db):
        return [
            ((g * na + a) * nb + b, (g * na + a + da) * nb + b + db)
            for g in groups
            for a in range(na)
            for b in range(nb)
            if 0 <= a + da < na and 0 <= b + db < nb
        ]

    return (
        lax.ppermute(x_edge, AXES, pairs(by, 0)),
        lax.ppermute(y_edge, AXES, pairs(0, by)),
    )


def to_fine(value):
    return shifted(value, "grid", 1)


def to_coarse(value):
    return shifted(value, "grid", -1)


def body(fields, material, permittivity, conductivity, relax_rate, debye_strength, subgrids):
    f = fields[0]
    ax, ay = exchange(f[1:3, 0], f[0:3:2, :, 0], -1, (0,))
    e, h, p, box, coef, desc, table = call(
        prep_kernel,
        (fields,) * 3
        + (material,) * 3
        + (permittivity, conductivity, relax_rate, debye_strength, subgrids),
        [PART] * 3
        + [BOX, COEF, jax.ShapeDtypeStruct((6, 8, 128), jnp.int32), (5, 8, 128)],
        [third((1, 9, 6, 24, 128), a) for a in range(3)]
        + [third((1, 6, 24, 128), a) for a in range(3)]
        + [SM] * 5,
        grid=(1,),
    )
    h, bx, by = call(h1_kernel, (e, h, ax, ay), [PART] + EDGES)
    bx, by = exchange(bx, by, 1, (0,))
    e, p, ax, ay, sent = call(
        e1_kernel, (e, h, p, coef, bx, by, desc), [PART] * 2 + EDGES + [(2, *REGION)]
    )
    region = to_fine(sent)
    ax, ay = exchange(ax, ay, -1, (0,))
    slab_material = to_fine(material)
    e, h, bx, by, box, now, change = call(
        h2_kernel,
        (e, h, ax, ay, box, coef, region, desc),
        [PART] * 2 + EDGES + [BOX, REGION, REGION],
    )
    bx, by = exchange(bx, by, 1, (0,))
    e, p, ax, ay, sent, wide_coef = call(
        e2_kernel,
        (e, h, p, coef, bx, by, desc, slab_material, table),
        [PART] * 2 + EDGES + [REGION, COEF],
    )
    region = to_fine(sent)
    ax, ay = exchange(ax, ay, -1, (0, 1))
    h, bx, by, relay1 = call(h3_kernel, (e, h, ax, ay, change), [PART] + EDGES + [(80, 384)])
    bx, by = exchange(bx, by, 1, (0, 1))
    relay1 = to_coarse(relay1)
    e, p, ax, ay, sent, box, now, relay2 = call(
        e3_kernel,
        (e, h, p, coef, wide_coef, bx, by, desc, box, region, now),
        [PART] * 2 + EDGES + [REGION, BOX, REGION, (80, 384)],
    )
    base_e, base_h, base_p = e, h, p
    region = to_fine(sent)
    ax, ay = exchange(ax, ay, -1, (1,))
    relay2 = to_coarse(relay2)
    h, bx, by, relay3 = call(h4_kernel, (e, h, ax, ay), [PART] + EDGES + [(64, 384)])
    bx, by = exchange(bx, by, 1, (1,))
    relay3 = to_coarse(relay3)
    box, relay4 = call(
        e4_kernel,
        (e, h, p, coef, wide_coef, bx, by, desc, box, region, now),
        [BOX, (80, 384)],
        scratch=[pltpu.VMEM((3, 2, 24, 384), F32)],
    )
    relay4 = to_coarse(relay4)
    fix = call(
        redo_kernel,
        (coef, desc, relay1, relay2, relay3),
        [PART] * 3,
        scratch=[pltpu.VMEM(PART, F32)] * 2,
    )
    (out,) = call(
        finish_kernel,
        (base_e, base_h, base_p, *fix, coef, desc, relay4, box),
        [SLAB],
        scratch=[pltpu.VMEM((9, 6, 3, 24, 128), F32)],
    )
    return out[None]


def solution(mesh):
    in_specs = (
        P("grid", None, "gx", "gy", None),
        P("grid", "gx", "gy", None),
        P(),
        P(),
        P(),
        P(),
        P("gx", "gy", None),
    )
    out_specs = P("grid", None, "gx", "gy", None)
    return jax.shard_map(body, mesh=mesh, in_specs=in_specs, out_specs=out_specs, check_vma=False)
```

```python
import functools

import jax
import jax.numpy as jnp
from jax import lax
from jax.experimental import pallas as pl
from jax.experimental.pallas import tpu as pltpu
from jax.sharding import PartitionSpec as P

COARSE_STEPS = 3
LIMIT = 40 * 1024 * 1024
VM = pl.BlockSpec(memory_space=pltpu.VMEM)
SM = pl.BlockSpec(memory_space=pltpu.SMEM)
F32 = jnp.float32


def shifted(value, axis, by):
    peers = lax.axis_size(axis)
    pairs = [(i, i + by) for i in range(peers) if 0 <= i + by < peers]
    return lax.ppermute(value, axis, pairs)


def lanes(shape=(8, 128)):
    return lax.broadcasted_iota(jnp.int32, shape, len(shape) - 1)


def rows(shape=(8, 128)):
    return lax.broadcasted_iota(jnp.int32, shape, len(shape) - 2)


def gather(tile, index):
    return jnp.take_along_axis(tile, index, axis=1)


def tables(perm, cond, relax, debye, factor):
    lane = lanes()

    def spread(ref):
        value = jnp.full((8, 128), ref[0], F32)
        for k in range(1, ref.shape[0]):
            value = jnp.where(lane == k, ref[k], value)
        return value

    eps = spread(perm)
    damp = spread(cond) * factor / (2.0 * eps)
    rate = spread(relax) * factor
    f0 = (1.0 - damp) / (1.0 + damp)
    f1 = 1.0 / (eps * (1.0 + damp))
    f3 = jnp.exp(-rate)
    f4 = spread(debye)
    c = f1 * rate
    return (f0 - c * f4, 0.5 * f1, c, f3, (1.0 - f3) * f4)


def to_tiles(parts):
    lane = lanes()
    kind = lane % 3
    out = []
    for t in range(3):
        mixed = jnp.where(
            kind == t, parts[0], jnp.where(kind == (t + 1) % 3, parts[1], parts[2])
        )
        out.append(gather(mixed, (3 * lane + t) & 127))
    return out


def from_tiles(tiles):
    lane = lanes()
    spread = [gather(tiles[t], (43 * (lane - t + 128)) & 127) for t in range(3)]
    out = []
    for a in range(3):
        kind = (2 * a + lane) % 3
        out.append(jnp.where(kind == 0, spread[0], jnp.where(kind == 1, spread[1], spread[2])))
    return out


def prep_kernel(f0, f1, f2, m0, m1, m2, perm, cond, relax, debye, sub, e, h, p, box, coef, desc, wide):
    coarse = lax.axis_index("grid") == 0
    fields, material = (f0, f1, f2), (m0, m1, m2)
    for k in range(6):
        desc[k] = jnp.full((8, 128), sub[0, 0, k], jnp.int32)

    @pl.when(coarse)
    def _():
        table = tables(perm, cond, relax, debye, 1.0)
        for x in range(6):
            for yt in range(3):
                for zt in range(3):
                    index = material[zt][0, x, pl.ds(8 * yt, 8)]
                    for k in range(5):
                        coef[k, x, 3 * yt + zt] = gather(table[k], index)
        for a in range(3):
            for k, part in enumerate((e, h, p)):
                part[:, :, :, pl.ds(128 * a, 128)] = fields[a][0, 3 * k : 3 * k + 3]

    @pl.when(jnp.logical_not(coarse))
    def _():
        for k, tile in enumerate(tables(perm, cond, relax, debye, 1.0)):
            wide[k] = tile
        table = tables(perm, cond, relax, debye, F32(1.0 / 3.0))
        row, lane = rows(), lanes()
        ly, lz = sub[0, 0, 4], sub[0, 0, 5]
        within = (row < ly) & (lane < lz)
        for x in range(6):
            inside = within & (x < 3 * sub[0, 0, 3])
            for u in range(3):
                cut = pl.ds(u, 8, stride=3)
                parts = [material[a][0, x, cut] for a in range(3)]
                for t, index in enumerate(to_tiles(parts)):
                    for k in range(5):
                        coef[k, x, 3 * u + t] = gather(table[k], index)
                for c in range(9):
                    parts = [fields[a][0, c, x, cut] for a in range(3)]
                    for t, tile in enumerate(to_tiles(parts)):
                        box[c, x, 3 * u + t] = jnp.where(inside, tile, 0.0)


def whole(ref, *index):
    return jnp.concatenate(
        [
            jnp.concatenate([ref[(*index, 3 * yt + zt)] for zt in range(3)], axis=1)
            for yt in range(3)
        ],
        axis=0,
    )


def magnetic(e, h, next_x, next_y, out):
    row, lane = rows((24, 384)), lanes((24, 384))

    def ahead_y(value, edge):
        return jnp.where(row == 23, edge, pltpu.roll(value, 23, 0))

    def ahead_z(value):
        return jnp.where(lane == 383, 0.0, pltpu.roll(value, 383, 1))

    for x in range(6):
        ex, ey, ez = (e[c, x] for c in range(3))
        if x < 5:
            ey_x, ez_x = e[1, x + 1], e[2, x + 1]
        else:
            ey_x, ez_x = next_x(0), next_x(1)
        ex_y = ahead_y(ex, next_y(0, x))
        ez_y = ahead_y(ez, next_y(1, x))
        ex_z, ey_z = ahead_z(ex), ahead_z(ey)
        turn = ((ez_y - ez) - (ey_z - ey), (ex_z - ex) - (ez_x - ez), (ey_x - ey) - (ex_y - ex))
        for c in range(3):
            if h is None:
                out[c, x] = -0.5 * turn[c]
            else:
                out[c, x] = h[c, x] - 0.5 * turn[c]


def last_layers(h, out_x, out_y):
    out_x[0], out_x[1] = h[1, 5], h[2, 5]
    for x in range(6):
        out_y[0, x : x + 1] = h[0, x, 23:24]
        out_y[1, x : x + 1] = h[2, x, 23:24]


def first_layers(e, out_x, out_y):
    out_x[0], out_x[1] = e[1, 0], e[2, 0]
    for x in range(6):
        out_y[0, x : x + 1] = e[0, x, 0:1]
        out_y[1, x : x + 1] = e[2, x, 0:1]


def curl_behind(h, x, prev_x, prev_y):
    row, lane = rows((24, 384)), lanes((24, 384))

    def behind_y(value, edge):
        return jnp.where(row == 0, edge, pltpu.roll(value, 1, 0))

    def behind_z(value):
        return jnp.where(lane == 0, 0.0, pltpu.roll(value, 1, 1))

    hx, hy, hz = (h[c, x] for c in range(3))
    if isinstance(x, int):
        hy_x, hz_x = (h[1, x - 1], h[2, x - 1]) if x > 0 else (prev_x(0), prev_x(1))
    else:
        before = jnp.maximum(x - 1, 0)
        first = jnp.full((24, 384), x, jnp.int32) == 0
        hy_x = jnp.where(first, prev_x(0), h[1, before])
        hz_x = jnp.where(first, prev_x(1), h[2, before])
    hx_y = behind_y(hx, prev_y(0, x))
    hz_y = behind_y(hz, prev_y(1, x))
    hx_z, hy_z = behind_z(hx), behind_z(hy)
    return ((hz - hz_y) - (hy - hy_z), (hx - hx_z) - (hz - hz_x), (hy - hy_x) - (hx - hx_y))


def electric(e, h, p, coef, prev_x, prev_y, out_e, out_p, more=None):
    for x in range(6):
        rotation = curl_behind(h, x, prev_x, prev_y)
        a, b, q, f3, g = (whole(coef, k, x) for k in range(5))
        for c in range(3):
            new = a * e[c, x] + b * rotation[c]
            old = None if p is None else p[c, x]
            if old is not None:
                new = new + q * old
            last = g * new if old is None else f3 * old + g * new
            if more is not None:
                new, last = new + more[0][c, x], last + more[1][c, x]
            out_e[c, x] = new
            out_p[c, x] = last


def edge_x(ref):
    return lambda k: ref[k]


def edge_y(ref):
    return lambda k, x: ref[k, pl.ds(x, 1)]


def corner(desc):
    x0 = jnp.max(desc[0].astype(F32)).astype(jnp.int32)
    y0 = jnp.max(desc[1].astype(F32)).astype(jnp.int32)
    base = pl.multiple_of(8 * jnp.minimum(y0 // 8, 1), 8)
    return x0, base, y0 - base


def cut_region(e, desc, spot):
    x0, base, over = spot
    place = lanes() + desc[2]
    index, part = place & 127, place >> 7

    def cut(c, i):
        tiles = []
        for a in range(3):
            pair = e[c, x0 + i, pl.ds(base, 16), pl.ds(128 * a, 128)]
            tiles.append(gather(pltpu.roll(pair, (16 - over) & 15, 0)[0:8], index))
        return jnp.where(part == 0, tiles[0], jnp.where(part == 1, tiles[1], tiles[2]))

    return [[cut(c, i) for i in range(2)] for c in range(3)]


def covered_of(desc):
    within = (rows() < desc[4]) & (lanes() < desc[5])
    return [within & (desc[3] > i) for i in range(2)]


def put(e, values, desc, spot, replace=None):
    x0, base, over = spot
    empty = jnp.zeros((8, 128), F32)
    for a in range(3):
        place = lanes() + (128 * a) - desc[2]
        index = place & 127
        here = (place >= 0) & (place < 128)
        for i in range(2):
            keep = None
            if replace is not None:
                keep = jnp.where(here, gather(replace[i], index), 0.0)
                keep = pltpu.roll(jnp.concatenate([keep, empty]), over, 0) > 0.5
            for c in range(3):
                spot = (c, x0 + i, pl.ds(base, 16), pl.ds(128 * a, 128))
                tile = jnp.where(here, gather(values(c, i), index), 0.0)
                pair = pltpu.roll(jnp.concatenate([tile, empty]), over, 0)
                if replace is None:
                    e[spot] = e[spot] + pair
                else:
                    e[spot] = jnp.where(keep, pair, e[spot])


def pack(out, box, in_x, in_y, at=0):
    if box is not None:
        for c in range(3):
            for i in range(2):
                out[pl.ds(8 * i, 8), pl.ds(128 * c, 128)] = box[c][i]
        at += 16
    for k in range(2):
        out[pl.ds(at + 24 * k, 24)] = in_x[k]
        out[pl.ds(at + 48 + 8 * k, 6)] = in_y[k]


def packed_box(ref):
    return lambda c, i: ref[pl.ds(8 * i, 8), pl.ds(128 * c, 128)]


def packed_x(ref, at):
    return lambda k: ref[pl.ds(at + 24 * k, 24)]


def packed_y(ref, at):
    return lambda k, x: ref[pl.ds(at + 48 + 8 * k + x, 1)]


def fine_steps(box, coef, desc, earlier, latest):
    row, lane = rows(), lanes()
    lx, ly, lz = desc[3], desc[4], desc[5]
    inside = covered_of(desc)
    y_face = [row == 0, None, row == ly - 1]
    z_face = [lane == 0, None, lane == lz - 1]

    def up(value):
        return jnp.where(row == 7, 0.0, pltpu.roll(value, 7, 0))

    def left(value):
        return jnp.where(lane == 127, 0.0, pltpu.roll(value, 127, 1))

    def down(value):
        return jnp.where(row == 0, 0.0, pltpu.roll(value, 1, 0))

    def right(value):
        return jnp.where(lane == 0, 0.0, pltpu.roll(value, 1, 1))

    def ahead_y(values, u, t):
        return values[3 * u + 3 + t] if u < 2 else up(values[t])

    def ahead_z(values, u, t):
        return values[3 * u + t + 1] if t < 2 else left(values[3 * u])

    def behind_y(values, u, t):
        return values[3 * u - 3 + t] if u > 0 else down(values[6 + t])

    def behind_z(values, u, t):
        return values[3 * u + t - 1] if t > 0 else right(values[3 * u + 2])

    def either(p, q):
        if p is None:
            return q
        return p if q is None else p | q

    zero = jnp.zeros((8, 128), F32)

    def substep(number, carry):
        weight = (number.astype(F32) + 1.0) / 3.0
        driven = [
            [earlier[c][i] + weight * (latest[c][i] - earlier[c][i]) for i in range(2)]
            for c in range(3)
        ]
        for x in range(6):
            part = x // 3
            e = [[box[c, x, k] for k in range(9)] for c in range(3)]
            if x < 5:
                ey_x = [box[1, x + 1, k] for k in range(9)]
                ez_x = [box[2, x + 1, k] for k in range(9)]
            else:
                ey_x = ez_x = [zero] * 9
            h = [[], [], []]
            for u in range(3):
                for t in range(3):
                    k = 3 * u + t
                    ex, ey, ez = e[0][k], e[1][k], e[2][k]
                    turn = (
                        (ahead_y(e[2], u, t) - ez) - (ahead_z(e[1], u, t) - ey),
                        (ahead_z(e[0], u, t) - ex) - (ez_x[k] - ez),
                        (ey_x[k] - ey) - (ahead_y(e[0], u, t) - ex),
                    )
                    for c in range(3):
                        value = box[3 + c, x, k] - 0.5 * turn[c]
                        box[3 + c, x, k] = value
                        h[c].append(value)
            x_face = x == 0
            if x in (2, 5):
                x_face = 3 * lx - 1 == x
            for u in range(3):
                for t in range(3):
                    k = 3 * u + t
                    hx, hy, hz = h[0][k], h[1][k], h[2][k]
                    hy_x = box[4, x - 1, k] if x > 0 else zero
                    hz_x = box[5, x - 1, k] if x > 0 else zero
                    rotation = (
                        (hz - behind_y(h[2], u, t)) - (hy - behind_z(h[1], u, t)),
                        (hx - behind_z(h[0], u, t)) - (hz - hz_x),
                        (hy - hy_x) - (hx - behind_y(h[0], u, t)),
                    )
                    a, b, p, f3, g = (coef[q, x, k] for q in range(5))
                    faces = (
                        either(y_face[u], z_face[t]),
                        None if x_face is True else either(x_face if x in (2, 5) else None, z_face[t]),
                        None if x_face is True else either(x_face if x in (2, 5) else None, y_face[u]),
                    )
                    for c in range(3):
                        old = box[6 + c, x, k]
                        new = a * e[c][k] + b * rotation[c] + p * old
                        if c > 0 and x_face is True:
                            new = driven[c][part]
                        elif faces[c] is not None:
                            new = jnp.where(faces[c], driven[c][part], new)
                        new = jnp.where(inside[part], new, 0.0)
                        box[c, x, k] = new
                        box[6 + c, x, k] = f3 * old + g * new
        return carry

    lax.fori_loop(0, 3, substep, 0)
    restricted = [[zero, zero] for c in range(3)]
    for c in range(3):
        for i in range(2):
            total = zero
            for x in range(3 * i, 3 * i + 3):
                for k in range(9):
                    total = total + box[c, x, k]
            restricted[c][i] = total * F32(1.0 / 27.0)
    return restricted


def feed_back(restricted, latest, desc):
    covered = covered_of(desc)
    after = [[jnp.where(covered[i], restricted[c][i], latest[c][i]) for i in range(2)] for c in range(3)]
    return after, [[after[c][i] - latest[c][i] for i in range(2)] for c in range(3)]


def store_box(ref, values):
    for c in range(3):
        for i in range(2):
            ref[c, i] = values[c][i]


def load_box(ref):
    return [[ref[c, i] for i in range(2)] for c in range(3)]


def is_coarse():
    return lax.axis_index("grid") == 0


def is_fine():
    return lax.axis_index("grid") == 1


def edge_kernel(near_x, near_y, ax, ay):
    @pl.when(is_coarse())
    def _():
        ax[0], ax[1] = near_x[0, 1, 0], near_x[0, 2, 0]
        for x in range(6):
            ay[0, x : x + 1] = near_y[0, 0, x, 0:1]
            ay[1, x : x + 1] = near_y[0, 2, x, 0:1]


def h1_kernel(e, h, ax, ay, out_h, bx, by):
    @pl.when(is_coarse())
    def _():
        magnetic(e, h, edge_x(ax), edge_y(ay), out_h)
        last_layers(out_h, bx, by)


def e1_kernel(e, h, p, coef, bx, by, desc, material, out_e, out_p, sent, out_material):
    @pl.when(is_coarse())
    def _():
        spot = corner(desc)
        before = cut_region(e, desc, spot)
        electric(e, h, p, coef, edge_x(bx), edge_y(by), out_e, out_p)
        after = cut_region(out_e, desc, spot)
        for c in range(3):
            for i in range(2):
                sent[0, c, i] = before[c][i]
                sent[1, c, i] = after[c][i]
        out_material[...] = material[...]


def f1_kernel(e, h, p, box_in, coef, region, desc, out_e, out_h, out_p, ax, ay, box, now, change):
    @pl.when(is_coarse())
    def _():
        out_e[...], out_h[...], out_p[...] = e[...], h[...], p[...]
        first_layers(e, ax, ay)

    @pl.when(is_fine())
    def _():
        box[...] = box_in[...]
        for out in (out_e, out_h, out_p):
            out[...] = jnp.zeros(out.shape, F32)
        earlier = [[region[0, c, i] for i in range(2)] for c in range(3)]
        latest = [[region[1, c, i] for i in range(2)] for c in range(3)]
        restricted = fine_steps(box, coef, desc, earlier, latest)
        after, delta = feed_back(restricted, latest, desc)
        store_box(now, after)
        store_box(change, delta)
        put(out_e, lambda c, i: delta[c][i], desc, corner(desc))
        first_layers(out_e, ax, ay)


def h2_kernel(e, h, ax, ay, change, coef, material, table, out_h, bx, by, relay, slab_coef):
    magnetic(e, h, edge_x(ax), edge_y(ay), out_h)
    last_layers(out_h, bx, by)

    @pl.when(is_coarse())
    def _():
        slab_coef[...] = coef[...]

    @pl.when(is_fine())
    def _():
        pack(relay, load_box(change), ax, ay)
        tiles = [table[k] for k in range(5)]
        for x in range(6):
            for yt in range(3):
                for zt in range(3):
                    index = material[0, x, pl.ds(8 * yt, 8), pl.ds(128 * zt, 128)]
                    for k in range(5):
                        slab_coef[k, x, 3 * yt + zt] = gather(tiles[k], index)


def base_kernel(e, h, p, coef, bx, by, desc, out_e, out_p, sent):
    @pl.when(is_coarse())
    def _():
        electric(e, h, p, coef, edge_x(bx), edge_y(by), out_e, out_p)
        store_box(sent, cut_region(out_e, desc, corner(desc)))


def f2_kernel(
    e, h, p, base_e, base_p, coef, slab_coef, bx, by, desc, box_in, region, was, relay1,
    out_e, out_p, ax, ay, box, now, relay, fix_h, one_e,
):
    @pl.when(is_coarse())
    def _():
        out_e[...], out_p[...] = base_e[...], base_p[...]
        first_layers(base_e, ax, ay)
        one_e[...] = jnp.zeros(one_e.shape, F32)
        put(one_e, packed_box(relay1), desc, corner(desc))
        magnetic(one_e, None, packed_x(relay1, 16), packed_y(relay1, 16), fix_h)

    @pl.when(is_fine())
    def _():
        box[...] = box_in[...]
        spot = corner(desc)
        electric(e, h, p, slab_coef, edge_x(bx), edge_y(by), out_e, out_p)
        fix = cut_region(out_e, desc, spot)
        latest = [[region[c, i] + fix[c][i] for i in range(2)] for c in range(3)]
        restricted = fine_steps(box, coef, desc, load_box(was), latest)
        after, delta = feed_back(restricted, latest, desc)
        store_box(now, after)
        put(out_e, lambda c, i: delta[c][i], desc, spot)
        first_layers(out_e, ax, ay)
        pack(relay, delta, bx, by)


def h3_kernel(e, h, ax, ay, out_h, bx, by, relay):
    magnetic(e, h, edge_x(ax), edge_y(ay), out_h)
    last_layers(out_h, bx, by)

    @pl.when(is_fine())
    def _():
        pack(relay, None, ax, ay)


def f3_kernel(
    e, h, p, coef, slab_coef, bx, by, desc, box_in, region, was, relay1, relay2, relay3, one_h,
    box, relay, fix_e, fix_h, fix_p, layer, one_e,
):
    @pl.when(is_coarse())
    def _():
        one_e[...] = jnp.zeros(one_e.shape, F32)
        spot = corner(desc)
        put(one_e, packed_box(relay1), desc, spot)
        electric(
            one_e, one_h, None, coef, packed_x(relay2, 16), packed_y(relay2, 16), fix_e, fix_p
        )
        put(fix_e, packed_box(relay2), desc, spot)
        magnetic(fix_e, one_h, packed_x(relay3, 0), packed_y(relay3, 0), fix_h)

    @pl.when(is_fine())
    def _():
        box[...] = box_in[...]
        spot = corner(desc)
        x0 = spot[0]
        for i in range(2):
            x = x0 + i
            rotation = curl_behind(h, x, edge_x(bx), edge_y(by))
            a, b, q = (whole(slab_coef, k, x) for k in range(3))
            for c in range(3):
                layer[c, i] = a * e[c, x] + b * rotation[c] + q * p[c, x]
        fix = cut_region(layer, desc, (0, *spot[1:]))
        latest = [[region[c, i] + fix[c][i] for i in range(2)] for c in range(3)]
        restricted = fine_steps(box, coef, desc, load_box(was), latest)
        pack(relay, restricted, bx, by)


def finish_kernel(e, h, p, fix_e, fix_h, fix_p, coef, desc, relay, box, out, mixed):
    @pl.when(is_coarse())
    def _():
        view_e, view_p = out.at[pl.ds(0, 3)], out.at[pl.ds(6, 3)]
        electric(
            fix_e, fix_h, fix_p, coef, packed_x(relay, 16), packed_y(relay, 16),
            view_e, view_p, (e, p),
        )
        out[3:6] = h[...] + fix_h[...]
        covered = [jnp.where(value, F32(1.0), 0.0) for value in covered_of(desc)]
        put(view_e, packed_box(relay), desc, corner(desc), covered)

    @pl.when(is_fine())
    def _():
        for c in range(9):
            for x in range(6):
                for u in range(3):
                    parts = from_tiles([box[c, x, 3 * u + t] for t in range(3)])
                    for a in range(3):
                        mixed[c, x, a, pl.ds(u, 8, stride=3)] = parts[a]
                for a in range(3):
                    out[c, x, :, pl.ds(128 * a, 128)] = mixed[c, x, a]


def third(shape, a):
    return pl.BlockSpec(shape, lambda i: (0,) * (len(shape) - 1) + (a,))


def call(kernel, operands, outs, specs=None, scratch=(), grid=()):
    shapes = [out if isinstance(out, jax.ShapeDtypeStruct) else jax.ShapeDtypeStruct(out, F32) for out in outs]
    return pl.pallas_call(
        kernel,
        out_shape=shapes,
        in_specs=specs or [VM] * len(operands),
        out_specs=[VM] * len(outs),
        grid=grid,
        scratch_shapes=scratch,
        compiler_params=pltpu.CompilerParams(vmem_limit_bytes=LIMIT),
    )(*operands)


PART = (3, 6, 24, 384)
SLAB = (9, 6, 24, 384)
BOX = (9, 6, 9, 8, 128)
COEF = (5, 6, 9, 8, 128)
REGION = (3, 2, 8, 128)
X_EDGE = (2, 24, 384)
Y_EDGE = (2, 6, 384)
EDGES = [X_EDGE, Y_EDGE]
AXES = ("grid", "gx", "gy")


def exchange(x_edge, y_edge, by, groups):
    na, nb = lax.axis_size("gx"), lax.axis_size("gy")

    def pairs(da, db):
        return [
            ((g * na + a) * nb + b, (g * na + a + da) * nb + b + db)
            for g in groups
            for a in range(na)
            for b in range(nb)
            if 0 <= a + da < na and 0 <= b + db < nb
        ]

    return (
        lax.ppermute(x_edge, AXES, pairs(by, 0)),
        lax.ppermute(y_edge, AXES, pairs(0, by)),
    )


def to_fine(value):
    return shifted(value, "grid", 1)


def to_coarse(value):
    return shifted(value, "grid", -1)


def body(fields, material, permittivity, conductivity, relax_rate, debye_strength, subgrids):
    ax, ay = call(
        edge_kernel,
        (fields, fields),
        EDGES,
        [
            pl.BlockSpec((1, 3, 1, 24, 384), lambda i: (0, 0, 0, 0, 0)),
            pl.BlockSpec((1, 3, 6, 8, 384), lambda i: (0, 0, 0, 0, 0)),
        ],
        grid=(1,),
    )
    ax, ay = exchange(ax, ay, -1, (0,))
    e, h, p, box, coef, desc, table = call(
        prep_kernel,
        (fields,) * 3
        + (material,) * 3
        + (permittivity, conductivity, relax_rate, debye_strength, subgrids),
        [PART] * 3
        + [BOX, COEF, jax.ShapeDtypeStruct((6, 8, 128), jnp.int32), (5, 8, 128)],
        [third((1, 9, 6, 24, 128), a) for a in range(3)]
        + [third((1, 6, 24, 128), a) for a in range(3)]
        + [SM] * 5,
        grid=(1,),
    )
    h, bx, by = call(h1_kernel, (e, h, ax, ay), [PART] + EDGES)
    bx, by = exchange(bx, by, 1, (0,))
    e, p, sent, slab_material = call(
        e1_kernel,
        (e, h, p, coef, bx, by, desc, material),
        [PART] * 2 + [(2, *REGION), jax.ShapeDtypeStruct(material.shape, jnp.int32)],
    )
    region = to_fine(sent)
    slab_material = to_fine(slab_material)
    e, h, p, ax, ay, box, now, change = call(
        f1_kernel,
        (e, h, p, box, coef, region, desc),
        [PART] * 3 + EDGES + [BOX, REGION, REGION],
    )
    ax, ay = exchange(ax, ay, -1, (0, 1))
    h, bx, by, relay1, slab_coef = call(
        h2_kernel,
        (e, h, ax, ay, change, coef, slab_material, table),
        [PART] + EDGES + [(80, 384), COEF],
    )
    fine_bx, fine_by = exchange(bx, by, 1, (1,))
    bx, by = exchange(bx, by, 1, (0,))
    base_e, base_p, sent = call(
        base_kernel, (e, h, p, slab_coef, bx, by, desc), [PART] * 2 + [REGION]
    )
    region = to_fine(sent)
    relay1 = to_coarse(relay1)
    e, p, ax, ay, box, now, relay2, fix_h = call(
        f2_kernel,
        (e, h, p, base_e, base_p, coef, slab_coef, fine_bx, fine_by, desc, box, region, now, relay1),
        [PART] * 2 + EDGES + [BOX, REGION, (80, 384), PART],
        scratch=[pltpu.VMEM(PART, F32)],
    )
    ax, ay = exchange(ax, ay, -1, (0, 1))
    relay2 = to_coarse(relay2)
    h, bx, by, relay3 = call(h3_kernel, (e, h, ax, ay), [PART] + EDGES + [(64, 384)])
    fine_bx, fine_by = exchange(bx, by, 1, (1,))
    bx, by = exchange(bx, by, 1, (0,))
    base_e, base_p, sent = call(
        base_kernel, (e, h, p, slab_coef, bx, by, desc), [PART] * 2 + [REGION]
    )
    region = to_fine(sent)
    relay3 = to_coarse(relay3)
    box, relay4, *fix = call(
        f3_kernel,
        (e, h, p, coef, slab_coef, fine_bx, fine_by, desc, box, region, now)
        + (relay1, relay2, relay3, fix_h),
        [BOX, (80, 384)] + [PART] * 3,
        scratch=[pltpu.VMEM((3, 2, 24, 384), F32), pltpu.VMEM(PART, F32)],
    )
    relay4 = to_coarse(relay4)
    (out,) = call(
        finish_kernel,
        (base_e, h, base_p, *fix, coef, desc, relay4, box),
        [SLAB],
        scratch=[pltpu.VMEM((9, 6, 3, 24, 128), F32)],
    )
    return out[None]


def solution(mesh):
    in_specs = (
        P("grid", None, "gx", "gy", None),
        P("grid", "gx", "gy", None),
        P(),
        P(),
        P(),
        P(),
        P("gx", "gy", None),
    )
    out_specs = P("grid", None, "gx", "gy", None)
    return jax.shard_map(body, mesh=mesh, in_specs=in_specs, out_specs=out_specs, check_vma=False)
```

```python
import functools

import jax
import jax.numpy as jnp
from jax import lax
from jax.experimental import pallas as pl
from jax.experimental.pallas import tpu as pltpu
from jax.sharding import PartitionSpec as P

COARSE_STEPS = 3
LIMIT = 40 * 1024 * 1024
VM = pl.BlockSpec(memory_space=pltpu.VMEM)
SM = pl.BlockSpec(memory_space=pltpu.SMEM)
F32 = jnp.float32


def shifted(value, axis, by):
    peers = lax.axis_size(axis)
    pairs = [(i, i + by) for i in range(peers) if 0 <= i + by < peers]
    return lax.ppermute(value, axis, pairs)


def lanes(shape=(8, 128)):
    return lax.broadcasted_iota(jnp.int32, shape, len(shape) - 1)


def rows(shape=(8, 128)):
    return lax.broadcasted_iota(jnp.int32, shape, len(shape) - 2)


def gather(tile, index):
    return jnp.take_along_axis(tile, index, axis=1)


def tables(perm, cond, relax, debye, factor):
    lane = lanes()

    def spread(ref):
        value = jnp.full((8, 128), ref[0], F32)
        for k in range(1, ref.shape[0]):
            value = jnp.where(lane == k, ref[k], value)
        return value

    eps = spread(perm)
    damp = spread(cond) * factor / (2.0 * eps)
    rate = spread(relax) * factor
    f0 = (1.0 - damp) / (1.0 + damp)
    f1 = 1.0 / (eps * (1.0 + damp))
    f3 = jnp.exp(-rate)
    f4 = spread(debye)
    c = f1 * rate
    return (f0 - c * f4, 0.5 * f1, c, f3, (1.0 - f3) * f4)


def to_tiles(parts):
    lane = lanes()
    kind = lane % 3
    out = []
    for t in range(3):
        mixed = jnp.where(
            kind == t, parts[0], jnp.where(kind == (t + 1) % 3, parts[1], parts[2])
        )
        out.append(gather(mixed, (3 * lane + t) & 127))
    return out


def from_tiles(tiles):
    lane = lanes()
    spread = [gather(tiles[t], (43 * (lane - t + 128)) & 127) for t in range(3)]
    out = []
    for a in range(3):
        kind = (2 * a + lane) % 3
        out.append(jnp.where(kind == 0, spread[0], jnp.where(kind == 1, spread[1], spread[2])))
    return out


def prep_kernel(f0, f1, f2, m0, m1, m2, perm, cond, relax, debye, sub, e, h, p, box, coef, desc, wide):
    coarse = lax.axis_index("grid") == 0
    fields, material = (f0, f1, f2), (m0, m1, m2)
    for k in range(6):
        desc[k] = jnp.full((8, 128), sub[0, 0, k], jnp.int32)

    @pl.when(coarse)
    def _():
        table = tables(perm, cond, relax, debye, 1.0)
        for x in range(6):
            for yt in range(3):
                for zt in range(3):
                    index = material[zt][0, x, pl.ds(8 * yt, 8)]
                    for k in range(5):
                        coef[k, x, 3 * yt + zt] = gather(table[k], index)
        for a in range(3):
            for k, part in enumerate((e, h, p)):
                part[:, :, :, pl.ds(128 * a, 128)] = fields[a][0, 3 * k : 3 * k + 3]

    @pl.when(jnp.logical_not(coarse))
    def _():
        for k, tile in enumerate(tables(perm, cond, relax, debye, 1.0)):
            wide[k] = tile
        table = tables(perm, cond, relax, debye, F32(1.0 / 3.0))
        row, lane = rows(), lanes()
        ly, lz = sub[0, 0, 4], sub[0, 0, 5]
        within = (row < ly) & (lane < lz)
        for x in range(6):
            inside = within & (x < 3 * sub[0, 0, 3])
            for u in range(3):
                cut = pl.ds(u, 8, stride=3)
                parts = [material[a][0, x, cut] for a in range(3)]
                for t, index in enumerate(to_tiles(parts)):
                    for k in range(5):
                        coef[k, x, 3 * u + t] = gather(table[k], index)
                for c in range(9):
                    parts = [fields[a][0, c, x, cut] for a in range(3)]
                    for t, tile in enumerate(to_tiles(parts)):
                        box[c, x, 3 * u + t] = jnp.where(inside, tile, 0.0)


def whole(ref, *index):
    return jnp.concatenate(
        [
            jnp.concatenate([ref[(*index, 3 * yt + zt)] for zt in range(3)], axis=1)
            for yt in range(3)
        ],
        axis=0,
    )


def ahead_y(value, edge):
    return jnp.where(rows(value.shape) == 23, edge, pltpu.roll(value, 23, 0))


def ahead_z(value):
    return jnp.where(lanes(value.shape) == 383, 0.0, pltpu.roll(value, 383, 1))


def behind_y(value, edge):
    return jnp.where(rows(value.shape) == 0, edge, pltpu.roll(value, 1, 0))


def behind_z(value):
    return jnp.where(lanes(value.shape) == 0, 0.0, pltpu.roll(value, 1, 1))


def send_edges(e, h, outs):
    ax, ay, bx, by, d1, d2 = outs
    ax[0], ax[1] = e[1, 0], e[2, 0]
    ex, ey, ez = (e[c, 5] for c in range(3))
    hy, hz = (0.0, 0.0) if h is None else (h[1, 5], h[2, 5])
    bx[0] = hy - 0.5 * ((ahead_z(ex) - ex) + ez)
    bx[1] = hz + 0.5 * (ey + (ahead_y(ex, 0.0) - ex))
    for x in range(6):
        ay[0, x : x + 1] = e[0, x, 0:1]
        ay[1, x : x + 1] = e[2, x, 0:1]
        ex, ey, ez = (e[c, x, 23:24] for c in range(3))
        ey_x = e[1, x + 1, 23:24] if x < 5 else 0.0
        hx, hz = (0.0, 0.0) if h is None else (h[0, x, 23:24], h[2, x, 23:24])
        by[0, x : x + 1] = hx + 0.5 * (ez + (ahead_z(ey) - ey))
        by[1, x : x + 1] = hz - 0.5 * ((ey_x - ey) + ex)
    d1[...] = e[0, 5, 0:1]
    d2[...] = e[1, 0, 23:24]


class Edges:
    def __init__(self, refs=None, packed=None, at=0):
        self.refs, self.packed, self.at = refs, packed, at

    def layer(self, which, k):
        if self.packed is None:
            return self.refs[which][k]
        return self.packed[pl.ds(self.at + 32 * which + 24 * k, 24)]

    def row(self, which, k, x):
        if self.packed is None:
            return self.refs[which][k, x : x + 1]
        return self.packed[pl.ds(self.at + 48 + 64 * (which // 2) + 8 * k + x, 1)]

    def diagonal(self, which):
        if self.packed is None:
            return self.refs[which][...]
        return self.packed[pl.ds(self.at + 124 + which, 1)]


def pack(out, boxes, edges):
    at = 0
    for box in boxes:
        for c in range(3):
            for i in range(2):
                out[pl.ds(at + 8 * i, 8), pl.ds(128 * c, 128)] = box[c][i]
        at += 16
    for which in (0, 2):
        for k in range(2):
            out[pl.ds(at + 32 * which + 24 * k, 24)] = edges[which][k]
            row = at + 48 + 64 * (which // 2) + 8 * k
            out[pl.ds(row, 6)] = edges[which + 1][k]
    for which in (4, 5):
        out[pl.ds(at + 124 + which, 1)] = edges[which][...]


def packed_box(ref, at=0):
    return lambda c, i: ref[pl.ds(at + 8 * i, 8), pl.ds(128 * c, 128)]


def magnetic(e, h, edges, out):
    for x in range(6):
        ex, ey, ez = (e[c, x] for c in range(3))
        if x < 5:
            ey_x, ez_x = e[1, x + 1], e[2, x + 1]
        else:
            ey_x, ez_x = edges.layer(0, 0), edges.layer(0, 1)
        ex_y = ahead_y(ex, edges.row(1, 0, x))
        ez_y = ahead_y(ez, edges.row(1, 1, x))
        ex_z, ey_z = ahead_z(ex), ahead_z(ey)
        turn = ((ez_y - ez) - (ey_z - ey), (ex_z - ex) - (ez_x - ez), (ey_x - ey) - (ex_y - ex))
        for c in range(3):
            if h is None:
                out[c, x] = -0.5 * turn[c]
            else:
                out[c, x] = h[c, x] - 0.5 * turn[c]


def behind(e, edges):
    has_x = (lax.axis_index("gx") > 0).astype(F32)
    has_y = (lax.axis_index("gy") > 0).astype(F32)
    row = rows((24, 384))
    corner_row = jnp.where(row == 23, 0.5 * edges.diagonal(4), 0.0)
    hy = has_x * (edges.layer(2, 0) + 0.5 * e[2, 0])
    hz = has_x * (edges.layer(2, 1) - 0.5 * e[1, 0] + corner_row)
    hx_rows, hz_rows = [], []
    for x in range(6):
        hx_rows.append(has_y * (edges.row(3, 0, x) - 0.5 * e[2, x, 0:1]))
        value = edges.row(3, 1, x) + 0.5 * e[0, x, 0:1]
        if x == 5:
            value = value - 0.5 * edges.diagonal(5)
        hz_rows.append(has_y * value)
    return hy, hz, hx_rows, hz_rows


def curl_behind(h, x, hy_x, hz_x, hx_row, hz_row):
    hx, hy, hz = (h[c, x] for c in range(3))
    hx_y, hz_y = behind_y(hx, hx_row), behind_y(hz, hz_row)
    hx_z, hy_z = behind_z(hx), behind_z(hy)
    return ((hz - hz_y) - (hy - hy_z), (hx - hx_z) - (hz - hz_x), (hy - hy_x) - (hx - hx_y))


def step(e, h, p, coef, edges, out_e, out_h, out_p, more=None):
    magnetic(e, h, edges, out_h)
    hy_x, hz_x, hx_rows, hz_rows = behind(e, edges)
    for x in range(6):
        rotation = curl_behind(out_h, x, hy_x, hz_x, hx_rows[x], hz_rows[x])
        hy_x, hz_x = out_h[1, x], out_h[2, x]
        a, b, q, f3, g = (whole(coef, k, x) for k in range(5))
        for c in range(3):
            new = a * e[c, x] + b * rotation[c]
            if p is None:
                last = g * new
            else:
                old = p[c, x]
                new = new + q * old
                last = f3 * old + g * new
            if more is not None:
                new, last = new + more[0][c, x], last + more[1][c, x]
            out_e[c, x] = new
            out_p[c, x] = last


def corner(desc):
    x0 = jnp.max(desc[0].astype(F32)).astype(jnp.int32)
    y0 = jnp.max(desc[1].astype(F32)).astype(jnp.int32)
    base = pl.multiple_of(8 * jnp.minimum(y0 // 8, 1), 8)
    return x0, base, y0 - base


def cut_region(e, desc, spot):
    x0, base, over = spot
    place = lanes() + desc[2]
    index, part = place & 127, place >> 7

    def cut(c, i):
        tiles = []
        for a in range(3):
            pair = e[c, x0 + i, pl.ds(base, 16), pl.ds(128 * a, 128)]
            tiles.append(gather(pltpu.roll(pair, (16 - over) & 15, 0)[0:8], index))
        return jnp.where(part == 0, tiles[0], jnp.where(part == 1, tiles[1], tiles[2]))

    return [[cut(c, i) for i in range(2)] for c in range(3)]


def covered_of(desc):
    within = (rows() < desc[4]) & (lanes() < desc[5])
    return [within & (desc[3] > i) for i in range(2)]


def put(e, values, desc, spot, replace=None):
    x0, base, over = spot
    empty = jnp.zeros((8, 128), F32)
    for a in range(3):
        place = lanes() + (128 * a) - desc[2]
        index = place & 127
        here = (place >= 0) & (place < 128)
        for i in range(2):
            keep = None
            if replace is not None:
                keep = jnp.where(here, gather(replace[i], index), 0.0)
                keep = pltpu.roll(jnp.concatenate([keep, empty]), over, 0) > 0.5
            for c in range(3):
                spot = (c, x0 + i, pl.ds(base, 16), pl.ds(128 * a, 128))
                tile = jnp.where(here, gather(values(c, i), index), 0.0)
                pair = pltpu.roll(jnp.concatenate([tile, empty]), over, 0)
                if replace is None:
                    e[spot] = e[spot] + pair
                else:
                    e[spot] = jnp.where(keep, pair, e[spot])


def fine_steps(box, coef, desc, earlier, latest):
    row, lane = rows(), lanes()
    lx, ly, lz = desc[3], desc[4], desc[5]
    inside = covered_of(desc)
    y_face = [row == 0, None, row == ly - 1]
    z_face = [lane == 0, None, lane == lz - 1]

    def up(value):
        return jnp.where(row == 7, 0.0, pltpu.roll(value, 7, 0))

    def left(value):
        return jnp.where(lane == 127, 0.0, pltpu.roll(value, 127, 1))

    def down(value):
        return jnp.where(row == 0, 0.0, pltpu.roll(value, 1, 0))

    def right(value):
        return jnp.where(lane == 0, 0.0, pltpu.roll(value, 1, 1))

    def ahead_y(values, u, t):
        return values[3 * u + 3 + t] if u < 2 else up(values[t])

    def ahead_z(values, u, t):
        return values[3 * u + t + 1] if t < 2 else left(values[3 * u])

    def behind_y(values, u, t):
        return values[3 * u - 3 + t] if u > 0 else down(values[6 + t])

    def behind_z(values, u, t):
        return values[3 * u + t - 1] if t > 0 else right(values[3 * u + 2])

    def either(p, q):
        if p is None:
            return q
        return p if q is None else p | q

    zero = jnp.zeros((8, 128), F32)

    def substep(number, carry):
        weight = (number.astype(F32) + 1.0) / 3.0
        driven = [
            [earlier[c][i] + weight * (latest[c][i] - earlier[c][i]) for i in range(2)]
            for c in range(3)
        ]
        for x in range(6):
            part = x // 3
            e = [[box[c, x, k] for k in range(9)] for c in range(3)]
            if x < 5:
                ey_x = [box[1, x + 1, k] for k in range(9)]
                ez_x = [box[2, x + 1, k] for k in range(9)]
            else:
                ey_x = ez_x = [zero] * 9
            h = [[], [], []]
            for u in range(3):
                for t in range(3):
                    k = 3 * u + t
                    ex, ey, ez = e[0][k], e[1][k], e[2][k]
                    turn = (
                        (ahead_y(e[2], u, t) - ez) - (ahead_z(e[1], u, t) - ey),
                        (ahead_z(e[0], u, t) - ex) - (ez_x[k] - ez),
                        (ey_x[k] - ey) - (ahead_y(e[0], u, t) - ex),
                    )
                    for c in range(3):
                        value = box[3 + c, x, k] - 0.5 * turn[c]
                        box[3 + c, x, k] = value
                        h[c].append(value)
            x_face = x == 0
            if x in (2, 5):
                x_face = 3 * lx - 1 == x
            for u in range(3):
                for t in range(3):
                    k = 3 * u + t
                    hx, hy, hz = h[0][k], h[1][k], h[2][k]
                    hy_x = box[4, x - 1, k] if x > 0 else zero
                    hz_x = box[5, x - 1, k] if x > 0 else zero
                    rotation = (
                        (hz - behind_y(h[2], u, t)) - (hy - behind_z(h[1], u, t)),
                        (hx - behind_z(h[0], u, t)) - (hz - hz_x),
                        (hy - hy_x) - (hx - behind_y(h[0], u, t)),
                    )
                    a, b, p, f3, g = (coef[q, x, k] for q in range(5))
                    faces = (
                        either(y_face[u], z_face[t]),
                        None if x_face is True else either(x_face if x in (2, 5) else None, z_face[t]),
                        None if x_face is True else either(x_face if x in (2, 5) else None, y_face[u]),
                    )
                    for c in range(3):
                        old = box[6 + c, x, k]
                        new = a * e[c][k] + b * rotation[c] + p * old
                        if c > 0 and x_face is True:
                            new = driven[c][part]
                        elif faces[c] is not None:
                            new = jnp.where(faces[c], driven[c][part], new)
                        new = jnp.where(inside[part], new, 0.0)
                        box[c, x, k] = new
                        box[6 + c, x, k] = f3 * old + g * new
        return carry

    lax.fori_loop(0, 3, substep, 0)
    restricted = [[zero, zero] for c in range(3)]
    for c in range(3):
        for i in range(2):
            total = zero
            for x in range(3 * i, 3 * i + 3):
                for k in range(9):
                    total = total + box[c, x, k]
            restricted[c][i] = total * F32(1.0 / 27.0)
    return restricted


def feed_back(restricted, latest, desc):
    covered = covered_of(desc)
    after = [[jnp.where(covered[i], restricted[c][i], latest[c][i]) for i in range(2)] for c in range(3)]
    return after, [[after[c][i] - latest[c][i] for i in range(2)] for c in range(3)]


def store_box(ref, values):
    for c in range(3):
        for i in range(2):
            ref[c, i] = values[c][i]


def load_box(ref):
    return [[ref[c, i] for i in range(2)] for c in range(3)]


def is_coarse():
    return lax.axis_index("grid") == 0


def is_fine():
    return lax.axis_index("grid") == 1


def edge_kernel(fields, *outs):
    @pl.when(is_coarse())
    def _():
        send_edges(fields.at[0, pl.ds(0, 3)], fields.at[0, pl.ds(3, 3)], outs)


def first_kernel(*refs):
    e, h, p, coef, desc, material, table = refs[:7]
    edges, refs = Edges(refs[7:13]), refs[13:]
    out_e, out_h, out_p, sent, slab_coef = refs[:5]
    outs = refs[5:]

    @pl.when(is_coarse())
    def _():
        spot = corner(desc)
        before = cut_region(e, desc, spot)
        step(e, h, p, coef, edges, out_e, out_h, out_p)
        send_edges(out_e, out_h, outs)
        after = cut_region(out_e, desc, spot)
        for c in range(3):
            for i in range(2):
                sent[0, c, i] = before[c][i]
                sent[1, c, i] = after[c][i]

    @pl.when(is_fine())
    def _():
        tiles = [table[k] for k in range(5)]
        for x in range(6):
            for yt in range(3):
                for zt in range(3):
                    index = material[0, x, pl.ds(8 * yt, 8), pl.ds(128 * zt, 128)]
                    for k in range(5):
                        slab_coef[k, x, 3 * yt + zt] = gather(tiles[k], index)


def second_kernel(*refs):
    e, h, p, coef, desc, box_in, region = refs[:7]
    edges, refs = Edges(refs[7:13]), refs[13:]
    out_e, out_h, out_p, sent, box, now, change = refs[:7]
    outs = refs[7:]

    @pl.when(is_coarse())
    def _():
        step(e, h, p, coef, edges, out_e, out_h, out_p)
        send_edges(out_e, out_h, outs)
        store_box(sent, cut_region(out_e, desc, corner(desc)))

    @pl.when(is_fine())
    def _():
        box[...] = box_in[...]
        out_e[...] = jnp.zeros(out_e.shape, F32)
        earlier = [[region[0, c, i] for i in range(2)] for c in range(3)]
        latest = [[region[1, c, i] for i in range(2)] for c in range(3)]
        restricted = fine_steps(box, coef, desc, earlier, latest)
        after, delta = feed_back(restricted, latest, desc)
        store_box(now, after)
        store_box(change, delta)
        put(out_e, lambda c, i: delta[c][i], desc, corner(desc))
        send_edges(out_e, None, outs)


def third_kernel(*refs):
    e, h, p, coef, slab_coef, desc, box_in, region, was, change = refs[:10]
    arrived, refs = refs[10:16], refs[16:]
    edges = Edges(arrived)
    out_e, out_h, out_p, sent, box, now, relay = refs[:7]
    outs = refs[7:]

    @pl.when(is_coarse())
    def _():
        step(e, h, p, coef, edges, out_e, out_h, out_p)
        store_box(sent, cut_region(out_e, desc, corner(desc)))

    @pl.when(is_fine())
    def _():
        box[...] = box_in[...]
        spot = corner(desc)
        step(e, None, None, slab_coef, edges, out_e, out_h, out_p)
        fix = cut_region(out_e, desc, spot)
        latest = [[region[c, i] + fix[c][i] for i in range(2)] for c in range(3)]
        restricted = fine_steps(box, coef, desc, load_box(was), latest)
        after, delta = feed_back(restricted, latest, desc)
        store_box(now, after)
        put(out_e, lambda c, i: delta[c][i], desc, spot)
        send_edges(out_e, out_h, outs)
        pack(relay, (load_box(change), delta), arrived)


def fourth_kernel(*refs):
    e, h, p, coef, slab_coef, desc, box_in, region, was, relay1 = refs[:10]
    arrived, refs = refs[10:16], refs[16:]
    edges = Edges(arrived)
    box, relay, fix_e, fix_h, fix_p, layer, one_e, new_h = refs

    @pl.when(is_coarse())
    def _():
        one_e[...] = jnp.zeros(one_e.shape, F32)
        spot = corner(desc)
        put(one_e, packed_box(relay1), desc, spot)
        step(one_e, None, None, coef, Edges(packed=relay1, at=32), fix_e, fix_h, fix_p)
        put(fix_e, packed_box(relay1, 16), desc, spot)

    @pl.when(is_fine())
    def _():
        box[...] = box_in[...]
        spot = corner(desc)
        magnetic(e, h, edges, new_h)
        hy_b, hz_b, hx_rows, hz_rows = behind(e, edges)
        for i in range(2):
            x = spot[0] + i
            before = jnp.maximum(x - 1, 0)
            number = jnp.full((24, 384), x, jnp.int32)
            hy_x = jnp.where(number == 0, hy_b, new_h[1, before])
            hz_x = jnp.where(number == 0, hz_b, new_h[2, before])
            hx_row, hz_row = hx_rows[0], hz_rows[0]
            for k in range(1, 6):
                hx_row = jnp.where(number[0:1] == k, hx_rows[k], hx_row)
                hz_row = jnp.where(number[0:1] == k, hz_rows[k], hz_row)
            rotation = curl_behind(new_h, x, hy_x, hz_x, hx_row, hz_row)
            a, b, q = (whole(slab_coef, k, x) for k in range(3))
            for c in range(3):
                layer[c, i] = a * e[c, x] + b * rotation[c] + q * p[c, x]
        fix = cut_region(layer, desc, (0, *spot[1:]))
        latest = [[region[c, i] + fix[c][i] for i in range(2)] for c in range(3)]
        restricted = fine_steps(box, coef, desc, load_box(was), latest)
        pack(relay, (restricted,), arrived)


def finish_kernel(e, h, p, fix_e, fix_h, fix_p, coef, desc, relay, box, out, mixed, new_h):
    @pl.when(is_coarse())
    def _():
        view_e, view_p = out.at[pl.ds(0, 3)], out.at[pl.ds(6, 3)]
        edges = Edges(packed=relay, at=16)
        step(fix_e, fix_h, fix_p, coef, edges, view_e, new_h, view_p, (e, p))
        out[3:6] = h[...] + new_h[...]
        covered = [jnp.where(value, F32(1.0), 0.0) for value in covered_of(desc)]
        put(view_e, packed_box(relay), desc, corner(desc), covered)

    @pl.when(is_fine())
    def _():
        for c in range(9):
            for x in range(6):
                for u in range(3):
                    parts = from_tiles([box[c, x, 3 * u + t] for t in range(3)])
                    for a in range(3):
                        mixed[c, x, a, pl.ds(u, 8, stride=3)] = parts[a]
                for a in range(3):
                    out[c, x, :, pl.ds(128 * a, 128)] = mixed[c, x, a]


def third(shape, a):
    return pl.BlockSpec(shape, lambda i: (0,) * (len(shape) - 1) + (a,))


def call(kernel, operands, outs, specs=None, scratch=(), grid=()):
    shapes = [out if isinstance(out, jax.ShapeDtypeStruct) else jax.ShapeDtypeStruct(out, F32) for out in outs]
    return pl.pallas_call(
        kernel,
        out_shape=shapes,
        in_specs=specs or [VM] * len(operands),
        out_specs=[VM] * len(outs),
        grid=grid,
        scratch_shapes=scratch,
        compiler_params=pltpu.CompilerParams(vmem_limit_bytes=LIMIT),
    )(*operands)


PART = (3, 6, 24, 384)
SLAB = (9, 6, 24, 384)
BOX = (9, 6, 9, 8, 128)
COEF = (5, 6, 9, 8, 128)
REGION = (3, 2, 8, 128)
EDGES = [(2, 24, 384), (2, 6, 384), (2, 24, 384), (2, 6, 384), (1, 384), (1, 384)]
WAYS = [(-1, 0), (0, -1), (1, 0), (0, 1), (1, -1), (-1, 1)]
AXES = ("grid", "gx", "gy")


def exchange(edges, groups):
    na, nb = lax.axis_size("gx"), lax.axis_size("gy")

    def pairs(da, db):
        return [
            ((g * na + a) * nb + b, (g * na + a + da) * nb + b + db)
            for g in groups
            for a in range(na)
            for b in range(nb)
            if 0 <= a + da < na and 0 <= b + db < nb
        ]

    return [lax.ppermute(edge, AXES, pairs(*way)) for edge, way in zip(edges, WAYS)]


def to_fine(value):
    return shifted(value, "grid", 1)


def to_coarse(value):
    return shifted(value, "grid", -1)


def body(fields, material, permittivity, conductivity, relax_rate, debye_strength, subgrids):
    edges = call(edge_kernel, (fields,), EDGES)
    edges = exchange(edges, (0,))
    slab_material = to_fine(material)
    e, h, p, box, coef, desc, table = call(
        prep_kernel,
        (fields,) * 3
        + (material,) * 3
        + (permittivity, conductivity, relax_rate, debye_strength, subgrids),
        [PART] * 3
        + [BOX, COEF, jax.ShapeDtypeStruct((6, 8, 128), jnp.int32), (5, 8, 128)],
        [third((1, 9, 6, 24, 128), a) for a in range(3)]
        + [third((1, 6, 24, 128), a) for a in range(3)]
        + [SM] * 5,
        grid=(1,),
    )
    e, h, p, sent, slab_coef, *edges = call(
        first_kernel,
        (e, h, p, coef, desc, slab_material, table, *edges),
        [PART] * 3 + [(2, *REGION), COEF] + EDGES,
    )
    region = to_fine(sent)
    edges = exchange(edges, (0,))
    e, h, p, sent, box, now, change, *edges = call(
        second_kernel,
        (e, h, p, coef, desc, box, region, *edges),
        [PART] * 3 + [REGION, BOX, REGION, REGION] + EDGES,
    )
    region = to_fine(sent)
    edges = exchange(edges, (0, 1))
    e, h, p, sent, box, now, relay, *edges = call(
        third_kernel,
        (e, h, p, coef, slab_coef, desc, box, region, now, change, *edges),
        [PART] * 3 + [REGION, BOX, REGION, (168, 384)] + EDGES,
    )
    region = to_fine(sent)
    relay = to_coarse(relay)
    edges = exchange(edges, (1,))
    box, last, *fix = call(
        fourth_kernel,
        (e, h, p, coef, slab_coef, desc, box, region, now, relay, *edges),
        [BOX, (152, 384)] + [PART] * 3,
        scratch=[
            pltpu.VMEM((3, 2, 24, 384), F32),
            pltpu.VMEM(PART, F32),
            pltpu.VMEM(PART, F32),
        ],
    )
    last = to_coarse(last)
    (out,) = call(
        finish_kernel,
        (e, h, p, *fix, coef, desc, last, box),
        [SLAB],
        scratch=[pltpu.VMEM((9, 6, 3, 24, 128), F32), pltpu.VMEM(PART, F32)],
    )
    return out[None]


def solution(mesh):
    in_specs = (
        P("grid", None, "gx", "gy", None),
        P("grid", "gx", "gy", None),
        P(),
        P(),
        P(),
        P(),
        P("gx", "gy", None),
    )
    out_specs = P("grid", None, "gx", "gy", None)
    return jax.shard_map(body, mesh=mesh, in_specs=in_specs, out_specs=out_specs, check_vma=False)
```

```python
import functools

import jax
import jax.numpy as jnp
from jax import lax
from jax.experimental import pallas as pl
from jax.experimental.pallas import tpu as pltpu
from jax.sharding import PartitionSpec as P

COARSE_STEPS = 3
LIMIT = 40 * 1024 * 1024
VM = pl.BlockSpec(memory_space=pltpu.VMEM)
SM = pl.BlockSpec(memory_space=pltpu.SMEM)
F32 = jnp.float32


def shifted(value, axis, by):
    peers = lax.axis_size(axis)
    pairs = [(i, i + by) for i in range(peers) if 0 <= i + by < peers]
    return lax.ppermute(value, axis, pairs)


def lanes(shape=(8, 128)):
    return lax.broadcasted_iota(jnp.int32, shape, len(shape) - 1)


def rows(shape=(8, 128)):
    return lax.broadcasted_iota(jnp.int32, shape, len(shape) - 2)


def gather(tile, index):
    return jnp.take_along_axis(tile, index, axis=1)


def tables(perm, cond, relax, debye, factor):
    lane = lanes()

    def spread(ref):
        value = jnp.full((8, 128), ref[0], F32)
        for k in range(1, ref.shape[0]):
            value = jnp.where(lane == k, ref[k], value)
        return value

    eps = spread(perm)
    damp = spread(cond) * factor / (2.0 * eps)
    rate = spread(relax) * factor
    f0 = (1.0 - damp) / (1.0 + damp)
    f1 = 1.0 / (eps * (1.0 + damp))
    f3 = jnp.exp(-rate)
    f4 = spread(debye)
    c = f1 * rate
    return (f0 - c * f4, 0.5 * f1, c, f3, (1.0 - f3) * f4)


def to_tiles(parts):
    lane = lanes()
    kind = lane % 3
    out = []
    for t in range(3):
        mixed = jnp.where(
            kind == t, parts[0], jnp.where(kind == (t + 1) % 3, parts[1], parts[2])
        )
        out.append(gather(mixed, (3 * lane + t) & 127))
    return out


def from_tiles(tiles):
    lane = lanes()
    spread = [gather(tiles[t], (43 * (lane - t + 128)) & 127) for t in range(3)]
    out = []
    for a in range(3):
        kind = (2 * a + lane) % 3
        out.append(jnp.where(kind == 0, spread[0], jnp.where(kind == 1, spread[1], spread[2])))
    return out


def prep_kernel(f0, f1, f2, m0, m1, m2, perm, cond, relax, debye, sub, e, h, p, box, coef, desc, wide):
    coarse = lax.axis_index("grid") == 0
    fields, material = (f0, f1, f2), (m0, m1, m2)
    for k in range(6):
        desc[k] = jnp.full((8, 128), sub[0, 0, k], jnp.int32)

    @pl.when(coarse)
    def _():
        table = tables(perm, cond, relax, debye, 1.0)
        for x in range(6):
            for yt in range(3):
                for zt in range(3):
                    index = material[zt][0, x, pl.ds(8 * yt, 8)]
                    for k in range(5):
                        coef[k, x, 3 * yt + zt] = gather(table[k], index)
        for a in range(3):
            for k, part in enumerate((e, h, p)):
                part[:, :, :, pl.ds(128 * a, 128)] = fields[a][0, 3 * k : 3 * k + 3]

    @pl.when(jnp.logical_not(coarse))
    def _():
        for k, tile in enumerate(tables(perm, cond, relax, debye, 1.0)):
            wide[k] = tile
        table = tables(perm, cond, relax, debye, F32(1.0 / 3.0))
        row, lane = rows(), lanes()
        ly, lz = sub[0, 0, 4], sub[0, 0, 5]
        within = (row < ly) & (lane < lz)
        for x in range(6):
            inside = within & (x < 3 * sub[0, 0, 3])
            for u in range(3):
                cut = pl.ds(u, 8, stride=3)
                parts = [material[a][0, x, cut] for a in range(3)]
                for t, index in enumerate(to_tiles(parts)):
                    for k in range(5):
                        coef[k, x, 3 * u + t] = gather(table[k], index)
                for c in range(9):
                    parts = [fields[a][0, c, x, cut] for a in range(3)]
                    for t, tile in enumerate(to_tiles(parts)):
                        box[c, x, 3 * u + t] = jnp.where(inside, tile, 0.0)


def whole(ref, *index):
    return jnp.concatenate(
        [
            jnp.concatenate([ref[(*index, 3 * yt + zt)] for zt in range(3)], axis=1)
            for yt in range(3)
        ],
        axis=0,
    )


def magnetic(e, h, next_x, next_y, out):
    row, lane = rows((24, 384)), lanes((24, 384))

    def ahead_y(value, edge):
        return jnp.where(row == 23, edge, pltpu.roll(value, 23, 0))

    def ahead_z(value):
        return jnp.where(lane == 383, 0.0, pltpu.roll(value, 383, 1))

    for x in range(6):
        ex, ey, ez = (e[c, x] for c in range(3))
        if x < 5:
            ey_x, ez_x = e[1, x + 1], e[2, x + 1]
        else:
            ey_x, ez_x = next_x(0), next_x(1)
        ex_y = ahead_y(ex, next_y(0, x))
        ez_y = ahead_y(ez, next_y(1, x))
        ex_z, ey_z = ahead_z(ex), ahead_z(ey)
        turn = ((ez_y - ez) - (ey_z - ey), (ex_z - ex) - (ez_x - ez), (ey_x - ey) - (ex_y - ex))
        for c in range(3):
            if h is None:
                out[c, x] = -0.5 * turn[c]
            else:
                out[c, x] = h[c, x] - 0.5 * turn[c]


def last_layers(h, out_x, out_y):
    out_x[0], out_x[1] = h[1, 5], h[2, 5]
    for x in range(6):
        out_y[0, x : x + 1] = h[0, x, 23:24]
        out_y[1, x : x + 1] = h[2, x, 23:24]


def first_layers(e, out_x, out_y):
    out_x[0], out_x[1] = e[1, 0], e[2, 0]
    for x in range(6):
        out_y[0, x : x + 1] = e[0, x, 0:1]
        out_y[1, x : x + 1] = e[2, x, 0:1]


def curl_behind(h, x, prev_x, prev_y):
    row, lane = rows((24, 384)), lanes((24, 384))

    def behind_y(value, edge):
        return jnp.where(row == 0, edge, pltpu.roll(value, 1, 0))

    def behind_z(value):
        return jnp.where(lane == 0, 0.0, pltpu.roll(value, 1, 1))

    hx, hy, hz = (h[c, x] for c in range(3))
    if isinstance(x, int):
        hy_x, hz_x = (h[1, x - 1], h[2, x - 1]) if x > 0 else (prev_x(0), prev_x(1))
    else:
        before = jnp.maximum(x - 1, 0)
        first = jnp.full((24, 384), x, jnp.int32) == 0
        hy_x = jnp.where(first, prev_x(0), h[1, before])
        hz_x = jnp.where(first, prev_x(1), h[2, before])
    hx_y = behind_y(hx, prev_y(0, x))
    hz_y = behind_y(hz, prev_y(1, x))
    hx_z, hy_z = behind_z(hx), behind_z(hy)
    return ((hz - hz_y) - (hy - hy_z), (hx - hx_z) - (hz - hz_x), (hy - hy_x) - (hx - hx_y))


def electric(e, h, p, coef, prev_x, prev_y, out_e, out_p, more=None):
    for x in range(6):
        rotation = curl_behind(h, x, prev_x, prev_y)
        a, b, q, f3, g = (whole(coef, k, x) for k in range(5))
        for c in range(3):
            new = a * e[c, x] + b * rotation[c]
            old = None if p is None else p[c, x]
            if old is not None:
                new = new + q * old
            last = g * new if old is None else f3 * old + g * new
            if more is not None:
                new, last = new + more[0][c, x], last + more[1][c, x]
            out_e[c, x] = new
            out_p[c, x] = last


def edge_x(ref):
    return lambda k: ref[k]


def edge_y(ref):
    return lambda k, x: ref[k, pl.ds(x, 1)]


def corner(desc):
    x0 = jnp.max(desc[0].astype(F32)).astype(jnp.int32)
    y0 = jnp.max(desc[1].astype(F32)).astype(jnp.int32)
    base = pl.multiple_of(8 * jnp.minimum(y0 // 8, 1), 8)
    return x0, base, y0 - base


def cut_region(e, desc, spot):
    x0, base, over = spot
    place = lanes() + desc[2]
    index, part = place & 127, place >> 7

    def cut(c, i):
        tiles = []
        for a in range(3):
            pair = e[c, x0 + i, pl.ds(base, 16), pl.ds(128 * a, 128)]
            tiles.append(gather(pltpu.roll(pair, (16 - over) & 15, 0)[0:8], index))
        return jnp.where(part == 0, tiles[0], jnp.where(part == 1, tiles[1], tiles[2]))

    return [[cut(c, i) for i in range(2)] for c in range(3)]


def covered_of(desc):
    within = (rows() < desc[4]) & (lanes() < desc[5])
    return [within & (desc[3] > i) for i in range(2)]


def put(e, values, desc, spot, replace=None):
    x0, base, over = spot
    empty = jnp.zeros((8, 128), F32)
    for a in range(3):
        place = lanes() + (128 * a) - desc[2]
        index = place & 127
        here = (place >= 0) & (place < 128)
        for i in range(2):
            keep = None
            if replace is not None:
                keep = jnp.where(here, gather(replace[i], index), 0.0)
                keep = pltpu.roll(jnp.concatenate([keep, empty]), over, 0) > 0.5
            for c in range(3):
                spot = (c, x0 + i, pl.ds(base, 16), pl.ds(128 * a, 128))
                tile = jnp.where(here, gather(values(c, i), index), 0.0)
                pair = pltpu.roll(jnp.concatenate([tile, empty]), over, 0)
                if replace is None:
                    e[spot] = e[spot] + pair
                else:
                    e[spot] = jnp.where(keep, pair, e[spot])


def pack(out, box, in_x, in_y, at):
    if box is not None:
        for c in range(3):
            for i in range(2):
                out[pl.ds(at + 8 * i, 8), pl.ds(128 * c, 128)] = box[c][i]
        at += 16
    for k in range(2):
        out[pl.ds(at + 24 * k, 24)] = in_x[k]
        out[pl.ds(at + 48 + 8 * k, 6)] = in_y[k, 0:6]


def packed_box(ref, at):
    return lambda c, i: ref[pl.ds(at + 8 * i, 8), pl.ds(128 * c, 128)]


def packed_x(ref, at):
    return lambda k: ref[pl.ds(at + 24 * k, 24)]


def packed_y(ref, at):
    return lambda k, x: ref[pl.ds(at + 48 + 8 * k + x, 1)]


def fine_steps(box, coef, desc, earlier, latest):
    row, lane = rows(), lanes()
    lx, ly, lz = desc[3], desc[4], desc[5]
    inside = covered_of(desc)
    y_face = [row == 0, None, row == ly - 1]
    z_face = [lane == 0, None, lane == lz - 1]

    def up(value):
        return jnp.where(row == 7, 0.0, pltpu.roll(value, 7, 0))

    def left(value):
        return jnp.where(lane == 127, 0.0, pltpu.roll(value, 127, 1))

    def down(value):
        return jnp.where(row == 0, 0.0, pltpu.roll(value, 1, 0))

    def right(value):
        return jnp.where(lane == 0, 0.0, pltpu.roll(value, 1, 1))

    def ahead_y(values, u, t):
        return values[3 * u + 3 + t] if u < 2 else up(values[t])

    def ahead_z(values, u, t):
        return values[3 * u + t + 1] if t < 2 else left(values[3 * u])

    def behind_y(values, u, t):
        return values[3 * u - 3 + t] if u > 0 else down(values[6 + t])

    def behind_z(values, u, t):
        return values[3 * u + t - 1] if t > 0 else right(values[3 * u + 2])

    def either(p, q):
        if p is None:
            return q
        return p if q is None else p | q

    zero = jnp.zeros((8, 128), F32)

    def substep(number, carry):
        weight = (number.astype(F32) + 1.0) / 3.0
        driven = [
            [earlier[c][i] + weight * (latest[c][i] - earlier[c][i]) for i in range(2)]
            for c in range(3)
        ]
        for x in range(6):
            part = x // 3
            e = [[box[c, x, k] for k in range(9)] for c in range(3)]
            if x < 5:
                ey_x = [box[1, x + 1, k] for k in range(9)]
                ez_x = [box[2, x + 1, k] for k in range(9)]
            else:
                ey_x = ez_x = [zero] * 9
            h = [[], [], []]
            for u in range(3):
                for t in range(3):
                    k = 3 * u + t
                    ex, ey, ez = e[0][k], e[1][k], e[2][k]
                    turn = (
                        (ahead_y(e[2], u, t) - ez) - (ahead_z(e[1], u, t) - ey),
                        (ahead_z(e[0], u, t) - ex) - (ez_x[k] - ez),
                        (ey_x[k] - ey) - (ahead_y(e[0], u, t) - ex),
                    )
                    for c in range(3):
                        value = box[3 + c, x, k] - 0.5 * turn[c]
                        box[3 + c, x, k] = value
                        h[c].append(value)
            x_face = x == 0
            if x in (2, 5):
                x_face = 3 * lx - 1 == x
            for u in range(3):
                for t in range(3):
                    k = 3 * u + t
                    hx, hy, hz = h[0][k], h[1][k], h[2][k]
                    hy_x = box[4, x - 1, k] if x > 0 else zero
                    hz_x = box[5, x - 1, k] if x > 0 else zero
                    rotation = (
                        (hz - behind_y(h[2], u, t)) - (hy - behind_z(h[1], u, t)),
                        (hx - behind_z(h[0], u, t)) - (hz - hz_x),
                        (hy - hy_x) - (hx - behind_y(h[0], u, t)),
                    )
                    a, b, p, f3, g = (coef[q, x, k] for q in range(5))
                    faces = (
                        either(y_face[u], z_face[t]),
                        None if x_face is True else either(x_face if x in (2, 5) else None, z_face[t]),
                        None if x_face is True else either(x_face if x in (2, 5) else None, y_face[u]),
                    )
                    for c in range(3):
                        old = box[6 + c, x, k]
                        new = a * e[c][k] + b * rotation[c] + p * old
                        if c > 0 and x_face is True:
                            new = driven[c][part]
                        elif faces[c] is not None:
                            new = jnp.where(faces[c], driven[c][part], new)
                        new = jnp.where(inside[part], new, 0.0)
                        box[c, x, k] = new
                        box[6 + c, x, k] = f3 * old + g * new
        return carry

    lax.fori_loop(0, 3, substep, 0)
    restricted = [[zero, zero] for c in range(3)]
    for c in range(3):
        for i in range(2):
            total = zero
            for x in range(3 * i, 3 * i + 3):
                for k in range(9):
                    total = total + box[c, x, k]
            restricted[c][i] = total * F32(1.0 / 27.0)
    return restricted


def feed_back(restricted, latest, desc):
    covered = covered_of(desc)
    after = [[jnp.where(covered[i], restricted[c][i], latest[c][i]) for i in range(2)] for c in range(3)]
    return after, [[after[c][i] - latest[c][i] for i in range(2)] for c in range(3)]


def store_box(ref, values):
    for c in range(3):
        for i in range(2):
            ref[c, i] = values[c][i]


def load_box(ref):
    return [[ref[c, i] for i in range(2)] for c in range(3)]


def is_coarse():
    return lax.axis_index("grid") == 0


def is_fine():
    return lax.axis_index("grid") == 1


def edge_kernel(near_x, near_y, ax, ay):
    @pl.when(is_coarse())
    def _():
        ax[0], ax[1] = near_x[0, 1, 0], near_x[0, 2, 0]
        for x in range(6):
            ay[0, x : x + 1] = near_y[0, 0, x, 0:1]
            ay[1, x : x + 1] = near_y[0, 2, x, 0:1]


def h1_kernel(e, h, ax, ay, out_h, bx, by):
    @pl.when(is_coarse())
    def _():
        magnetic(e, h, edge_x(ax), edge_y(ay), out_h)
        last_layers(out_h, bx, by)


def e1_kernel(e, h, p, coef, bx, by, desc, material, table, out_e, out_p, sent, slab_coef):
    @pl.when(is_coarse())
    def _():
        spot = corner(desc)
        before = cut_region(e, desc, spot)
        electric(e, h, p, coef, edge_x(bx), edge_y(by), out_e, out_p)
        after = cut_region(out_e, desc, spot)
        for c in range(3):
            for i in range(2):
                sent[0, c, i] = before[c][i]
                sent[1, c, i] = after[c][i]
        slab_coef[...] = coef[...]

    @pl.when(is_fine())
    def _():
        tiles = [table[k] for k in range(5)]
        for x in range(6):
            for yt in range(3):
                for zt in range(3):
                    index = material[0, x, pl.ds(8 * yt, 8), pl.ds(128 * zt, 128)]
                    for k in range(5):
                        slab_coef[k, x, 3 * yt + zt] = gather(tiles[k], index)


def f1_kernel(e, h, p, box_in, coef, region, desc, out_e, out_h, out_p, ax, ay, box, now, change):
    @pl.when(is_coarse())
    def _():
        out_e[...], out_h[...], out_p[...] = e[...], h[...], p[...]
        first_layers(e, ax, ay)

    @pl.when(is_fine())
    def _():
        box[...] = box_in[...]
        for out in (out_e, out_h, out_p):
            out[...] = jnp.zeros(out.shape, F32)
        earlier = [[region[0, c, i] for i in range(2)] for c in range(3)]
        latest = [[region[1, c, i] for i in range(2)] for c in range(3)]
        restricted = fine_steps(box, coef, desc, earlier, latest)
        after, delta = feed_back(restricted, latest, desc)
        store_box(now, after)
        store_box(change, delta)
        put(out_e, lambda c, i: delta[c][i], desc, corner(desc))
        first_layers(out_e, ax, ay)


def h2_kernel(e, h, ax, ay, out_h, bx, by):
    magnetic(e, h, edge_x(ax), edge_y(ay), out_h)
    last_layers(out_h, bx, by)


def base_kernel(e, h, p, coef, bx, by, desc, out_e, out_p, sent):
    @pl.when(is_coarse())
    def _():
        electric(e, h, p, coef, edge_x(bx), edge_y(by), out_e, out_p)
        store_box(sent, cut_region(out_e, desc, corner(desc)))


def f2_kernel(
    e, h, p, base_e, base_p, coef, slab_coef, bx, by, desc, box_in, region, was,
    out_e, out_p, ax, ay, box, now, change,
):
    @pl.when(is_coarse())
    def _():
        out_e[...], out_p[...] = base_e[...], base_p[...]
        first_layers(base_e, ax, ay)

    @pl.when(is_fine())
    def _():
        box[...] = box_in[...]
        spot = corner(desc)
        electric(e, h, p, slab_coef, edge_x(bx), edge_y(by), out_e, out_p)
        fix = cut_region(out_e, desc, spot)
        latest = [[region[c, i] + fix[c][i] for i in range(2)] for c in range(3)]
        restricted = fine_steps(box, coef, desc, load_box(was), latest)
        after, delta = feed_back(restricted, latest, desc)
        store_box(now, after)
        store_box(change, delta)
        put(out_e, lambda c, i: delta[c][i], desc, spot)
        first_layers(out_e, ax, ay)


def h3_kernel(
    e, h, ax, ay, change1, ax2, ay2, change2, bx2, by2, out_h, bx, by, relay,
):
    magnetic(e, h, edge_x(ax), edge_y(ay), out_h)
    last_layers(out_h, bx, by)

    @pl.when(is_fine())
    def _():
        pack(relay, load_box(change1), ax2, ay2, 0)
        pack(relay, load_box(change2), bx2, by2, 80)
        pack(relay, None, ax, ay, 160)


def f3_kernel(
    e, h, p, coef, slab_coef, bx, by, desc, box_in, region, was, relay_in,
    box, relay, fix_e, fix_h, fix_p, layer, one_e, one_h,
):
    @pl.when(is_coarse())
    def _():
        one_e[...] = jnp.zeros(one_e.shape, F32)
        spot = corner(desc)
        put(one_e, packed_box(relay_in, 0), desc, spot)
        magnetic(one_e, None, packed_x(relay_in, 16), packed_y(relay_in, 16), one_h)
        electric(
            one_e, one_h, None, coef, packed_x(relay_in, 96), packed_y(relay_in, 96), fix_e, fix_p
        )
        put(fix_e, packed_box(relay_in, 80), desc, spot)
        magnetic(fix_e, one_h, packed_x(relay_in, 160), packed_y(relay_in, 160), fix_h)

    @pl.when(is_fine())
    def _():
        box[...] = box_in[...]
        spot = corner(desc)
        x0 = spot[0]
        for i in range(2):
            x = x0 + i
            rotation = curl_behind(h, x, edge_x(bx), edge_y(by))
            a, b, q = (whole(slab_coef, k, x) for k in range(3))
            for c in range(3):
                layer[c, i] = a * e[c, x] + b * rotation[c] + q * p[c, x]
        fix = cut_region(layer, desc, (0, *spot[1:]))
        latest = [[region[c, i] + fix[c][i] for i in range(2)] for c in range(3)]
        restricted = fine_steps(box, coef, desc, load_box(was), latest)
        pack(relay, restricted, bx, by, 0)


def finish_kernel(e, h, p, fix_e, fix_h, fix_p, coef, desc, relay, box, out, mixed):
    @pl.when(is_coarse())
    def _():
        view_e, view_p = out.at[pl.ds(0, 3)], out.at[pl.ds(6, 3)]
        electric(
            fix_e, fix_h, fix_p, coef, packed_x(relay, 16), packed_y(relay, 16),
            view_e, view_p, (e, p),
        )
        out[3:6] = h[...] + fix_h[...]
        covered = [jnp.where(value, F32(1.0), 0.0) for value in covered_of(desc)]
        put(view_e, packed_box(relay, 0), desc, corner(desc), covered)

    @pl.when(is_fine())
    def _():
        for c in range(9):
            for x in range(6):
                for u in range(3):
                    parts = from_tiles([box[c, x, 3 * u + t] for t in range(3)])
                    for a in range(3):
                        mixed[c, x, a, pl.ds(u, 8, stride=3)] = parts[a]
                for a in range(3):
                    out[c, x, :, pl.ds(128 * a, 128)] = mixed[c, x, a]


def third(shape, a):
    return pl.BlockSpec(shape, lambda i: (0,) * (len(shape) - 1) + (a,))


def call(kernel, operands, outs, specs=None, scratch=(), grid=()):
    shapes = [out if isinstance(out, jax.ShapeDtypeStruct) else jax.ShapeDtypeStruct(out, F32) for out in outs]
    return pl.pallas_call(
        kernel,
        out_shape=shapes,
        in_specs=specs or [VM] * len(operands),
        out_specs=[VM] * len(outs),
        grid=grid,
        scratch_shapes=scratch,
        compiler_params=pltpu.CompilerParams(vmem_limit_bytes=LIMIT),
    )(*operands)


PART = (3, 6, 24, 384)
SLAB = (9, 6, 24, 384)
BOX = (9, 6, 9, 8, 128)
COEF = (5, 6, 9, 8, 128)
REGION = (3, 2, 8, 128)
X_EDGE = (2, 24, 384)
Y_EDGE = (2, 6, 384)
EDGES = [X_EDGE, Y_EDGE]
LAST = [X_EDGE, (2, 16, 384)]
AXES = ("grid", "gx", "gy")


def exchange(x_edge, y_edge, by, groups):
    na, nb = lax.axis_size("gx"), lax.axis_size("gy")

    def pairs(da, db):
        return [
            ((g * na + a) * nb + b, (g * na + a + da) * nb + b + db)
            for g in groups
            for a in range(na)
            for b in range(nb)
            if 0 <= a + da < na and 0 <= b + db < nb
        ]

    return (
        lax.ppermute(x_edge, AXES, pairs(by, 0)),
        lax.ppermute(y_edge, AXES, pairs(0, by)),
    )


def to_fine(value):
    return shifted(value, "grid", 1)


def to_coarse(value):
    return shifted(value, "grid", -1)


def body(fields, material, permittivity, conductivity, relax_rate, debye_strength, subgrids):
    ax, ay = call(
        edge_kernel,
        (fields, fields),
        EDGES,
        [
            pl.BlockSpec((1, 3, 1, 24, 384), lambda i: (0, 0, 0, 0, 0)),
            pl.BlockSpec((1, 3, 6, 8, 384), lambda i: (0, 0, 0, 0, 0)),
        ],
        grid=(1,),
    )
    ax, ay = exchange(ax, ay, -1, (0,))
    e, h, p, box, coef, desc, table = call(
        prep_kernel,
        (fields,) * 3
        + (material,) * 3
        + (permittivity, conductivity, relax_rate, debye_strength, subgrids),
        [PART] * 3
        + [BOX, COEF, jax.ShapeDtypeStruct((6, 8, 128), jnp.int32), (5, 8, 128)],
        [third((1, 9, 6, 24, 128), a) for a in range(3)]
        + [third((1, 6, 24, 128), a) for a in range(3)]
        + [SM] * 5,
        grid=(1,),
    )
    slab_material = to_fine(material)
    h, bx, by = call(h1_kernel, (e, h, ax, ay), [PART] + LAST)
    bx, by = exchange(bx, by, 1, (0,))
    e, p, sent, slab_coef = call(
        e1_kernel,
        (e, h, p, coef, bx, by, desc, slab_material, table),
        [PART] * 2 + [(2, *REGION), COEF],
    )
    region = to_fine(sent)
    e, h, p, ax, ay, box, now, change1 = call(
        f1_kernel,
        (e, h, p, box, coef, region, desc),
        [PART] * 3 + EDGES + [BOX, REGION, REGION],
    )
    ax2, ay2 = exchange(ax, ay, -1, (0, 1))
    h, bx, by = call(h2_kernel, (e, h, ax2, ay2), [PART] + LAST)
    bx2, by2 = exchange(bx, by, 1, (1,))
    bx, by = exchange(bx, by, 1, (0,))
    base_e, base_p, sent = call(
        base_kernel, (e, h, p, slab_coef, bx, by, desc), [PART] * 2 + [REGION]
    )
    region = to_fine(sent)
    e, p, ax, ay, box, now, change2 = call(
        f2_kernel,
        (e, h, p, base_e, base_p, coef, slab_coef, bx2, by2, desc, box, region, now),
        [PART] * 2 + EDGES + [BOX, REGION, REGION],
    )
    ax, ay = exchange(ax, ay, -1, (0, 1))
    h, bx, by, relay = call(
        h3_kernel,
        (e, h, ax, ay, change1, ax2, ay2, change2, bx2, by2),
        [PART] + LAST + [(224, 384)],
    )
    relay = to_coarse(relay)
    fine_bx, fine_by = exchange(bx, by, 1, (1,))
    bx, by = exchange(bx, by, 1, (0,))
    base_e, base_p, sent = call(
        base_kernel, (e, h, p, slab_coef, bx, by, desc), [PART] * 2 + [REGION]
    )
    region = to_fine(sent)
    box, relay4, *fix = call(
        f3_kernel,
        (e, h, p, coef, slab_coef, fine_bx, fine_by, desc, box, region, now, relay),
        [BOX, (80, 384)] + [PART] * 3,
        scratch=[
            pltpu.VMEM((3, 2, 24, 384), F32),
            pltpu.VMEM(PART, F32),
            pltpu.VMEM(PART, F32),
        ],
    )
    relay4 = to_coarse(relay4)
    (out,) = call(
        finish_kernel,
        (base_e, h, base_p, *fix, coef, desc, relay4, box),
        [SLAB],
        scratch=[pltpu.VMEM((9, 6, 3, 24, 128), F32)],
    )
    return out[None]


def solution(mesh):
    in_specs = (
        P("grid", None, "gx", "gy", None),
        P("grid", "gx", "gy", None),
        P(),
        P(),
        P(),
        P(),
        P("gx", "gy", None),
    )
    out_specs = P("grid", None, "gx", "gy", None)
    return jax.shard_map(body, mesh=mesh, in_specs=in_specs, out_specs=out_specs, check_vma=False)
```

```python
import functools

import jax
import jax.numpy as jnp
from jax import lax
from jax.experimental import pallas as pl
from jax.experimental.pallas import tpu as pltpu
from jax.sharding import PartitionSpec as P

COARSE_STEPS = 3
LIMIT = 40 * 1024 * 1024
VM = pl.BlockSpec(memory_space=pltpu.VMEM)
SM = pl.BlockSpec(memory_space=pltpu.SMEM)
F32 = jnp.float32


def shifted(value, axis, by):
    peers = lax.axis_size(axis)
    pairs = [(i, i + by) for i in range(peers) if 0 <= i + by < peers]
    return lax.ppermute(value, axis, pairs)


def lanes(shape=(8, 128)):
    return lax.broadcasted_iota(jnp.int32, shape, len(shape) - 1)


def rows(shape=(8, 128)):
    return lax.broadcasted_iota(jnp.int32, shape, len(shape) - 2)


def gather(tile, index):
    return jnp.take_along_axis(tile, index, axis=1)


def tables(perm, cond, relax, debye, factor):
    lane = lanes()

    def spread(ref):
        value = jnp.full((8, 128), ref[0], F32)
        for k in range(1, ref.shape[0]):
            value = jnp.where(lane == k, ref[k], value)
        return value

    eps = spread(perm)
    damp = spread(cond) * factor / (2.0 * eps)
    rate = spread(relax) * factor
    f0 = (1.0 - damp) / (1.0 + damp)
    f1 = 1.0 / (eps * (1.0 + damp))
    f3 = jnp.exp(-rate)
    f4 = spread(debye)
    c = f1 * rate
    return (f0 - c * f4, 0.5 * f1, c, f3, (1.0 - f3) * f4)


def to_tiles(parts):
    lane = lanes()
    kind = lane % 3
    out = []
    for t in range(3):
        mixed = jnp.where(
            kind == t, parts[0], jnp.where(kind == (t + 1) % 3, parts[1], parts[2])
        )
        out.append(gather(mixed, (3 * lane + t) & 127))
    return out


def from_tiles(tiles):
    lane = lanes()
    spread = [gather(tiles[t], (43 * (lane - t + 128)) & 127) for t in range(3)]
    out = []
    for a in range(3):
        kind = (2 * a + lane) % 3
        out.append(jnp.where(kind == 0, spread[0], jnp.where(kind == 1, spread[1], spread[2])))
    return out


def prep_kernel(f0, f1, f2, m0, m1, m2, perm, cond, relax, debye, sub, e, h, p, box, coef, desc, wide):
    coarse = lax.axis_index("grid") == 0
    fields, material = (f0, f1, f2), (m0, m1, m2)
    for k in range(6):
        desc[k] = jnp.full((8, 128), sub[0, 0, k], jnp.int32)

    @pl.when(coarse)
    def _():
        table = tables(perm, cond, relax, debye, 1.0)
        for x in range(6):
            for yt in range(3):
                for zt in range(3):
                    index = material[zt][0, x, pl.ds(8 * yt, 8)]
                    for k in range(5):
                        coef[k, x, 3 * yt + zt] = gather(table[k], index)
        for a in range(3):
            for k, part in enumerate((e, h, p)):
                part[:, :, :, pl.ds(128 * a, 128)] = fields[a][0, 3 * k : 3 * k + 3]

    @pl.when(jnp.logical_not(coarse))
    def _():
        for k, tile in enumerate(tables(perm, cond, relax, debye, 1.0)):
            wide[k] = tile
        table = tables(perm, cond, relax, debye, F32(1.0 / 3.0))
        row, lane = rows(), lanes()
        ly, lz = sub[0, 0, 4], sub[0, 0, 5]
        within = (row < ly) & (lane < lz)
        for x in range(6):
            inside = within & (x < 3 * sub[0, 0, 3])
            for u in range(3):
                cut = pl.ds(u, 8, stride=3)
                parts = [material[a][0, x, cut] for a in range(3)]
                for t, index in enumerate(to_tiles(parts)):
                    for k in range(5):
                        coef[k, x, 3 * u + t] = gather(table[k], index)
                for c in range(9):
                    parts = [fields[a][0, c, x, cut] for a in range(3)]
                    for t, tile in enumerate(to_tiles(parts)):
                        box[c, x, 3 * u + t] = jnp.where(inside, tile, 0.0)


def whole(ref, *index):
    return jnp.concatenate(
        [
            jnp.concatenate([ref[(*index, 3 * yt + zt)] for zt in range(3)], axis=1)
            for yt in range(3)
        ],
        axis=0,
    )


def magnetic(e, h, next_x, next_y, out):
    row, lane = rows((24, 384)), lanes((24, 384))

    def ahead_y(value, edge):
        return jnp.where(row == 23, edge, pltpu.roll(value, 23, 0))

    def ahead_z(value):
        return jnp.where(lane == 383, 0.0, pltpu.roll(value, 383, 1))

    for x in range(6):
        ex, ey, ez = (e[c, x] for c in range(3))
        if x < 5:
            ey_x, ez_x = e[1, x + 1], e[2, x + 1]
        else:
            ey_x, ez_x = next_x(0), next_x(1)
        ex_y = ahead_y(ex, next_y(0, x))
        ez_y = ahead_y(ez, next_y(1, x))
        ex_z, ey_z = ahead_z(ex), ahead_z(ey)
        turn = ((ez_y - ez) - (ey_z - ey), (ex_z - ex) - (ez_x - ez), (ey_x - ey) - (ex_y - ex))
        for c in range(3):
            if h is None:
                out[c, x] = -0.5 * turn[c]
            else:
                out[c, x] = h[c, x] - 0.5 * turn[c]


def last_layers(h, out_x, out_y):
    out_x[0], out_x[1] = h[1, 5], h[2, 5]
    for x in range(6):
        out_y[0, x : x + 1] = h[0, x, 23:24]
        out_y[1, x : x + 1] = h[2, x, 23:24]


def first_layers(e, out_x, out_y):
    out_x[0], out_x[1] = e[1, 0], e[2, 0]
    for x in range(6):
        out_y[0, x : x + 1] = e[0, x, 0:1]
        out_y[1, x : x + 1] = e[2, x, 0:1]


def curl_behind(h, x, prev_x, prev_y):
    row, lane = rows((24, 384)), lanes((24, 384))

    def behind_y(value, edge):
        return jnp.where(row == 0, edge, pltpu.roll(value, 1, 0))

    def behind_z(value):
        return jnp.where(lane == 0, 0.0, pltpu.roll(value, 1, 1))

    hx, hy, hz = (h[c, x] for c in range(3))
    if isinstance(x, int):
        hy_x, hz_x = (h[1, x - 1], h[2, x - 1]) if x > 0 else (prev_x(0), prev_x(1))
    else:
        before = jnp.maximum(x - 1, 0)
        first = jnp.full((24, 384), x, jnp.int32) == 0
        hy_x = jnp.where(first, prev_x(0), h[1, before])
        hz_x = jnp.where(first, prev_x(1), h[2, before])
    hx_y = behind_y(hx, prev_y(0, x))
    hz_y = behind_y(hz, prev_y(1, x))
    hx_z, hy_z = behind_z(hx), behind_z(hy)
    return ((hz - hz_y) - (hy - hy_z), (hx - hx_z) - (hz - hz_x), (hy - hy_x) - (hx - hx_y))


def electric(e, h, p, coef, prev_x, prev_y, out_e, out_p, more=None):
    for x in range(6):
        rotation = curl_behind(h, x, prev_x, prev_y)
        a, b, q, f3, g = (whole(coef, k, x) for k in range(5))
        for c in range(3):
            new = a * e[c, x] + b * rotation[c]
            old = None if p is None else p[c, x]
            if old is not None:
                new = new + q * old
            last = g * new if old is None else f3 * old + g * new
            if more is not None:
                new, last = new + more[0][c, x], last + more[1][c, x]
            out_e[c, x] = new
            out_p[c, x] = last


def edge_x(ref):
    return lambda k: ref[k]


def edge_y(ref):
    return lambda k, x: ref[k, pl.ds(x, 1)]


def corner(desc):
    x0 = jnp.max(desc[0].astype(F32)).astype(jnp.int32)
    y0 = jnp.max(desc[1].astype(F32)).astype(jnp.int32)
    base = pl.multiple_of(8 * jnp.minimum(y0 // 8, 1), 8)
    return x0, base, y0 - base


def cut_region(e, desc, spot):
    x0, base, over = spot
    place = lanes() + desc[2]
    index, part = place & 127, place >> 7

    def cut(c, i):
        tiles = []
        for a in range(3):
            pair = e[c, x0 + i, pl.ds(base, 16), pl.ds(128 * a, 128)]
            tiles.append(gather(pltpu.roll(pair, (16 - over) & 15, 0)[0:8], index))
        return jnp.where(part == 0, tiles[0], jnp.where(part == 1, tiles[1], tiles[2]))

    return [[cut(c, i) for i in range(2)] for c in range(3)]


def covered_of(desc):
    within = (rows() < desc[4]) & (lanes() < desc[5])
    return [within & (desc[3] > i) for i in range(2)]


def put(e, values, desc, spot, replace=None):
    x0, base, over = spot
    empty = jnp.zeros((8, 128), F32)
    for a in range(3):
        place = lanes() + (128 * a) - desc[2]
        index = place & 127
        here = (place >= 0) & (place < 128)
        for i in range(2):
            keep = None
            if replace is not None:
                keep = jnp.where(here, gather(replace[i], index), 0.0)
                keep = pltpu.roll(jnp.concatenate([keep, empty]), over, 0) > 0.5
            for c in range(3):
                spot = (c, x0 + i, pl.ds(base, 16), pl.ds(128 * a, 128))
                tile = jnp.where(here, gather(values(c, i), index), 0.0)
                pair = pltpu.roll(jnp.concatenate([tile, empty]), over, 0)
                if replace is None:
                    e[spot] = e[spot] + pair
                else:
                    e[spot] = jnp.where(keep, pair, e[spot])


def pack(out, box, in_x, in_y, at):
    if box is not None:
        for c in range(3):
            for i in range(2):
                out[pl.ds(at + 8 * i, 8), pl.ds(128 * c, 128)] = box[c][i]
        at += 16
    for k in range(2):
        out[pl.ds(at + 24 * k, 24)] = in_x[k]
        out[pl.ds(at + 48 + 8 * k, 6)] = in_y[k, 0:6]


def packed_box(ref, at):
    return lambda c, i: ref[pl.ds(at + 8 * i, 8), pl.ds(128 * c, 128)]


def packed_x(ref, at):
    return lambda k: ref[pl.ds(at + 24 * k, 24)]


def packed_y(ref, at):
    return lambda k, x: ref[pl.ds(at + 48 + 8 * k + x, 1)]


def fine_steps(box, coef, desc, earlier, latest):
    row, lane = rows(), lanes()
    lx, ly, lz = desc[3], desc[4], desc[5]
    inside = covered_of(desc)
    y_face = [row == 0, None, row == ly - 1]
    z_face = [lane == 0, None, lane == lz - 1]

    def up(value):
        return jnp.where(row == 7, 0.0, pltpu.roll(value, 7, 0))

    def left(value):
        return jnp.where(lane == 127, 0.0, pltpu.roll(value, 127, 1))

    def down(value):
        return jnp.where(row == 0, 0.0, pltpu.roll(value, 1, 0))

    def right(value):
        return jnp.where(lane == 0, 0.0, pltpu.roll(value, 1, 1))

    def ahead_y(values, u, t):
        return values[3 * u + 3 + t] if u < 2 else up(values[t])

    def ahead_z(values, u, t):
        return values[3 * u + t + 1] if t < 2 else left(values[3 * u])

    def behind_y(values, u, t):
        return values[3 * u - 3 + t] if u > 0 else down(values[6 + t])

    def behind_z(values, u, t):
        return values[3 * u + t - 1] if t > 0 else right(values[3 * u + 2])

    def either(p, q):
        if p is None:
            return q
        return p if q is None else p | q

    zero = jnp.zeros((8, 128), F32)

    def substep(number, carry):
        weight = (number.astype(F32) + 1.0) / 3.0
        driven = [
            [earlier[c][i] + weight * (latest[c][i] - earlier[c][i]) for i in range(2)]
            for c in range(3)
        ]
        for x in range(6):
            part = x // 3
            e = [[box[c, x, k] for k in range(9)] for c in range(3)]
            if x < 5:
                ey_x = [box[1, x + 1, k] for k in range(9)]
                ez_x = [box[2, x + 1, k] for k in range(9)]
            else:
                ey_x = ez_x = [zero] * 9
            h = [[], [], []]
            for u in range(3):
                for t in range(3):
                    k = 3 * u + t
                    ex, ey, ez = e[0][k], e[1][k], e[2][k]
                    turn = (
                        (ahead_y(e[2], u, t) - ez) - (ahead_z(e[1], u, t) - ey),
                        (ahead_z(e[0], u, t) - ex) - (ez_x[k] - ez),
                        (ey_x[k] - ey) - (ahead_y(e[0], u, t) - ex),
                    )
                    for c in range(3):
                        value = box[3 + c, x, k] - 0.5 * turn[c]
                        box[3 + c, x, k] = value
                        h[c].append(value)
            x_face = x == 0
            if x in (2, 5):
                x_face = 3 * lx - 1 == x
            for u in range(3):
                for t in range(3):
                    k = 3 * u + t
                    hx, hy, hz = h[0][k], h[1][k], h[2][k]
                    hy_x = box[4, x - 1, k] if x > 0 else zero
                    hz_x = box[5, x - 1, k] if x > 0 else zero
                    rotation = (
                        (hz - behind_y(h[2], u, t)) - (hy - behind_z(h[1], u, t)),
                        (hx - behind_z(h[0], u, t)) - (hz - hz_x),
                        (hy - hy_x) - (hx - behind_y(h[0], u, t)),
                    )
                    a, b, p, f3, g = (coef[q, x, k] for q in range(5))
                    faces = (
                        either(y_face[u], z_face[t]),
                        None if x_face is True else either(x_face if x in (2, 5) else None, z_face[t]),
                        None if x_face is True else either(x_face if x in (2, 5) else None, y_face[u]),
                    )
                    for c in range(3):
                        old = box[6 + c, x, k]
                        new = a * e[c][k] + b * rotation[c] + p * old
                        if c > 0 and x_face is True:
                            new = driven[c][part]
                        elif faces[c] is not None:
                            new = jnp.where(faces[c], driven[c][part], new)
                        new = jnp.where(inside[part], new, 0.0)
                        box[c, x, k] = new
                        box[6 + c, x, k] = f3 * old + g * new
        return carry

    lax.fori_loop(0, 3, substep, 0)
    restricted = [[zero, zero] for c in range(3)]
    for c in range(3):
        for i in range(2):
            total = zero
            for x in range(3 * i, 3 * i + 3):
                for k in range(9):
                    total = total + box[c, x, k]
            restricted[c][i] = total * F32(1.0 / 27.0)
    return restricted


def feed_back(restricted, latest, desc):
    covered = covered_of(desc)
    after = [[jnp.where(covered[i], restricted[c][i], latest[c][i]) for i in range(2)] for c in range(3)]
    return after, [[after[c][i] - latest[c][i] for i in range(2)] for c in range(3)]


def store_box(ref, values):
    for c in range(3):
        for i in range(2):
            ref[c, i] = values[c][i]


def store_tiles(ref, values):
    for c in range(3):
        for i in range(2):
            ref[2 * c + i] = values[c][i]


def load_box(ref):
    return [[ref[c, i] for i in range(2)] for c in range(3)]


def is_coarse():
    return lax.axis_index("grid") == 0


def is_fine():
    return lax.axis_index("grid") == 1


def edge_kernel(near_x, near_y, ax, ay):
    @pl.when(is_coarse())
    def _():
        ax[0], ax[1] = near_x[0, 1, 0], near_x[0, 2, 0]
        for x in range(6):
            ay[0, x : x + 1] = near_y[0, 0, x, 0:1]
            ay[1, x : x + 1] = near_y[0, 2, x, 0:1]


def h1_kernel(e, h, ax, ay, material, out_h, bx, by, sent):
    @pl.when(is_coarse())
    def _():
        sent[...] = material[...]
        magnetic(e, h, edge_x(ax), edge_y(ay), out_h)
        last_layers(out_h, bx, by)


def e1_kernel(e, h, p, coef, bx, by, desc, material, table, out_e, out_p, sent, slab_coef):
    @pl.when(is_coarse())
    def _():
        spot = corner(desc)
        before = cut_region(e, desc, spot)
        electric(e, h, p, coef, edge_x(bx), edge_y(by), out_e, out_p)
        after = cut_region(out_e, desc, spot)
        for c in range(3):
            for i in range(2):
                sent[0, c, i] = before[c][i]
                sent[1, c, i] = after[c][i]
        slab_coef[...] = coef[...]

    @pl.when(is_fine())
    def _():
        tiles = [table[k] for k in range(5)]
        for x in range(6):
            for yt in range(3):
                for zt in range(3):
                    index = material[0, x, pl.ds(8 * yt, 8), pl.ds(128 * zt, 128)]
                    for k in range(5):
                        slab_coef[k, x, 3 * yt + zt] = gather(tiles[k], index)


def f1_kernel(e, h, p, box_in, coef, region, desc, out_e, out_h, out_p, ax, ay, box, now, change):
    @pl.when(is_coarse())
    def _():
        out_e[...], out_h[...], out_p[...] = e[...], h[...], p[...]
        first_layers(e, ax, ay)

    @pl.when(is_fine())
    def _():
        box[...] = box_in[...]
        for out in (out_e, out_h, out_p):
            out[...] = jnp.zeros(out.shape, F32)
        earlier = [[region[0, c, i] for i in range(2)] for c in range(3)]
        latest = [[region[1, c, i] for i in range(2)] for c in range(3)]
        restricted = fine_steps(box, coef, desc, earlier, latest)
        after, delta = feed_back(restricted, latest, desc)
        store_box(now, after)
        store_box(change, delta)
        put(out_e, lambda c, i: delta[c][i], desc, corner(desc))
        first_layers(out_e, ax, ay)


def h2_kernel(e, h, ax, ay, out_h, bx, by):
    magnetic(e, h, edge_x(ax), edge_y(ay), out_h)
    last_layers(out_h, bx, by)


def base_kernel(e, h, p, coef, bx, by, desc, out_e, out_p, sent):
    @pl.when(is_coarse())
    def _():
        electric(e, h, p, coef, edge_x(bx), edge_y(by), out_e, out_p)
        store_tiles(sent, cut_region(out_e, desc, corner(desc)))


def f2_kernel(
    e, h, p, base_e, base_p, coef, slab_coef, bx, by, desc, box_in, region, was,
    out_e, out_p, ax, ay, box, now, change,
):
    @pl.when(is_coarse())
    def _():
        out_e[...], out_p[...] = base_e[...], base_p[...]
        first_layers(base_e, ax, ay)

    @pl.when(is_fine())
    def _():
        box[...] = box_in[...]
        spot = corner(desc)
        electric(e, h, p, slab_coef, edge_x(bx), edge_y(by), out_e, out_p)
        fix = cut_region(out_e, desc, spot)
        latest = [[region[2 * c + i] + fix[c][i] for i in range(2)] for c in range(3)]
        restricted = fine_steps(box, coef, desc, load_box(was), latest)
        after, delta = feed_back(restricted, latest, desc)
        store_box(now, after)
        store_box(change, delta)
        put(out_e, lambda c, i: delta[c][i], desc, spot)
        first_layers(out_e, ax, ay)


def h3_kernel(
    e, h, ax, ay, change1, ax2, ay2, change2, bx2, by2, out_h, bx, by, relay,
):
    magnetic(e, h, edge_x(ax), edge_y(ay), out_h)
    last_layers(out_h, bx, by)

    @pl.when(is_fine())
    def _():
        pack(relay, load_box(change1), ax2, ay2, 0)
        pack(relay, load_box(change2), bx2, by2, 80)
        pack(relay, None, ax, ay, 160)


def f3_kernel(
    e, h, p, coef, slab_coef, bx, by, desc, box_in, region, was, relay_in,
    box, relay, fix_e, fix_h, fix_p, layer, one_e, one_h,
):
    @pl.when(is_coarse())
    def _():
        one_e[...] = jnp.zeros(one_e.shape, F32)
        spot = corner(desc)
        put(one_e, packed_box(relay_in, 0), desc, spot)
        magnetic(one_e, None, packed_x(relay_in, 16), packed_y(relay_in, 16), one_h)
        electric(
            one_e, one_h, None, coef, packed_x(relay_in, 96), packed_y(relay_in, 96), fix_e, fix_p
        )
        put(fix_e, packed_box(relay_in, 80), desc, spot)
        magnetic(fix_e, one_h, packed_x(relay_in, 160), packed_y(relay_in, 160), fix_h)

    @pl.when(is_fine())
    def _():
        box[...] = box_in[...]
        spot = corner(desc)
        x0 = spot[0]
        for i in range(2):
            x = x0 + i
            rotation = curl_behind(h, x, edge_x(bx), edge_y(by))
            a, b, q = (whole(slab_coef, k, x) for k in range(3))
            for c in range(3):
                layer[c, i] = a * e[c, x] + b * rotation[c] + q * p[c, x]
        fix = cut_region(layer, desc, (0, *spot[1:]))
        latest = [[region[2 * c + i] + fix[c][i] for i in range(2)] for c in range(3)]
        restricted = fine_steps(box, coef, desc, load_box(was), latest)
        pack(relay, restricted, bx, by, 0)


def finish_kernel(e, h, p, fix_e, fix_h, fix_p, coef, desc, relay, box, out, mixed):
    @pl.when(is_coarse())
    def _():
        view_e, view_p = out.at[pl.ds(0, 3)], out.at[pl.ds(6, 3)]
        electric(
            fix_e, fix_h, fix_p, coef, packed_x(relay, 16), packed_y(relay, 16),
            view_e, view_p, (e, p),
        )
        out[3:6] = h[...] + fix_h[...]
        covered = [jnp.where(value, F32(1.0), 0.0) for value in covered_of(desc)]
        put(view_e, packed_box(relay, 0), desc, corner(desc), covered)

    @pl.when(is_fine())
    def _():
        for c in range(9):
            for x in range(6):
                for u in range(3):
                    parts = from_tiles([box[c, x, 3 * u + t] for t in range(3)])
                    for a in range(3):
                        mixed[c, x, a, pl.ds(u, 8, stride=3)] = parts[a]
                for a in range(3):
                    out[c, x, :, pl.ds(128 * a, 128)] = mixed[c, x, a]


def third(shape, a):
    return pl.BlockSpec(shape, lambda i: (0,) * (len(shape) - 1) + (a,))


def call(kernel, operands, outs, specs=None, scratch=(), grid=()):
    shapes = [out if isinstance(out, jax.ShapeDtypeStruct) else jax.ShapeDtypeStruct(out, F32) for out in outs]
    return pl.pallas_call(
        kernel,
        out_shape=shapes,
        in_specs=specs or [VM] * len(operands),
        out_specs=[VM] * len(outs),
        grid=grid,
        scratch_shapes=scratch,
        compiler_params=pltpu.CompilerParams(vmem_limit_bytes=LIMIT),
    )(*operands)


PART = (3, 6, 24, 384)
SLAB = (9, 6, 24, 384)
BOX = (9, 6, 9, 8, 128)
COEF = (5, 6, 9, 8, 128)
REGION = (3, 2, 8, 128)
X_EDGE = (2, 24, 384)
Y_EDGE = (2, 6, 384)
EDGES = [X_EDGE, Y_EDGE]
LAST = [X_EDGE, (2, 16, 384)]
AXES = ("grid", "gx", "gy")


def exchange(x_edge, y_edge, by, groups):
    na, nb = lax.axis_size("gx"), lax.axis_size("gy")

    def pairs(da, db):
        return [
            ((g * na + a) * nb + b, (g * na + a + da) * nb + b + db)
            for g in groups
            for a in range(na)
            for b in range(nb)
            if 0 <= a + da < na and 0 <= b + db < nb
        ]

    return (
        lax.ppermute(x_edge, AXES, pairs(by, 0)),
        lax.ppermute(y_edge, AXES, pairs(0, by)),
    )


def to_fine(value):
    return shifted(value, "grid", 1)


def to_coarse(value):
    return shifted(value, "grid", -1)


def body(fields, material, permittivity, conductivity, relax_rate, debye_strength, subgrids):
    ax, ay = call(
        edge_kernel,
        (fields, fields),
        EDGES,
        [
            pl.BlockSpec((1, 3, 1, 24, 384), lambda i: (0, 0, 0, 0, 0)),
            pl.BlockSpec((1, 3, 6, 8, 384), lambda i: (0, 0, 0, 0, 0)),
        ],
        grid=(1,),
    )
    ax, ay = exchange(ax, ay, -1, (0,))
    e, h, p, box, coef, desc, table = call(
        prep_kernel,
        (fields,) * 3
        + (material,) * 3
        + (permittivity, conductivity, relax_rate, debye_strength, subgrids),
        [PART] * 3
        + [BOX, COEF, jax.ShapeDtypeStruct((6, 8, 128), jnp.int32), (5, 8, 128)],
        [third((1, 9, 6, 24, 128), a) for a in range(3)]
        + [third((1, 6, 24, 128), a) for a in range(3)]
        + [SM] * 5,
        grid=(1,),
    )
    h, bx, by, slab_material = call(
        h1_kernel,
        (e, h, ax, ay, material),
        [PART] + LAST + [jax.ShapeDtypeStruct(material.shape, jnp.int32)],
    )
    slab_material = to_fine(slab_material)
    bx, by = exchange(bx, by, 1, (0,))
    e, p, sent, slab_coef = call(
        e1_kernel,
        (e, h, p, coef, bx, by, desc, slab_material, table),
        [PART] * 2 + [(2, *REGION), COEF],
    )
    region = to_fine(sent)
    e, h, p, ax, ay, box, now, change1 = call(
        f1_kernel,
        (e, h, p, box, coef, region, desc),
        [PART] * 3 + EDGES + [BOX, REGION, REGION],
    )
    ax2, ay2 = exchange(ax, ay, -1, (0, 1))
    h, bx, by = call(h2_kernel, (e, h, ax2, ay2), [PART] + LAST)
    bx2, by2 = exchange(bx, by, 1, (1,))
    bx, by = exchange(bx, by, 1, (0,))
    base_e, base_p, sent = call(
        base_kernel, (e, h, p, slab_coef, bx, by, desc), [PART] * 2 + [(19, 8, 128)]
    )
    region = to_fine(sent)
    e, p, ax, ay, box, now, change2 = call(
        f2_kernel,
        (e, h, p, base_e, base_p, coef, slab_coef, bx2, by2, desc, box, region, now),
        [PART] * 2 + EDGES + [BOX, REGION, REGION],
    )
    ax, ay = exchange(ax, ay, -1, (0, 1))
    h, bx, by, relay = call(
        h3_kernel,
        (e, h, ax, ay, change1, ax2, ay2, change2, bx2, by2),
        [PART] + LAST + [(224, 384)],
    )
    relay = to_coarse(relay)
    fine_bx, fine_by = exchange(bx, by, 1, (1,))
    bx, by = exchange(bx, by, 1, (0,))
    base_e, base_p, sent = call(
        base_kernel, (e, h, p, slab_coef, bx, by, desc), [PART] * 2 + [(19, 8, 128)]
    )
    region = to_fine(sent)
    box, relay4, *fix = call(
        f3_kernel,
        (e, h, p, coef, slab_coef, fine_bx, fine_by, desc, box, region, now, relay),
        [BOX, (80, 384)] + [PART] * 3,
        scratch=[
            pltpu.VMEM((3, 2, 24, 384), F32),
            pltpu.VMEM(PART, F32),
            pltpu.VMEM(PART, F32),
        ],
    )
    relay4 = to_coarse(relay4)
    (out,) = call(
        finish_kernel,
        (base_e, h, base_p, *fix, coef, desc, relay4, box),
        [SLAB],
        scratch=[pltpu.VMEM((9, 6, 3, 24, 128), F32)],
    )
    return out[None]


def solution(mesh):
    in_specs = (
        P("grid", None, "gx", "gy", None),
        P("grid", "gx", "gy", None),
        P(),
        P(),
        P(),
        P(),
        P("gx", "gy", None),
    )
    out_specs = P("grid", None, "gx", "gy", None)
    return jax.shard_map(body, mesh=mesh, in_specs=in_specs, out_specs=out_specs, check_vma=False)
```

```python
import functools

import jax
import jax.numpy as jnp
from jax import lax
from jax.experimental import pallas as pl
from jax.experimental.pallas import tpu as pltpu
from jax.sharding import PartitionSpec as P

COARSE_STEPS = 3
LIMIT = 40 * 1024 * 1024
VM = pl.BlockSpec(memory_space=pltpu.VMEM)
SM = pl.BlockSpec(memory_space=pltpu.SMEM)
F32 = jnp.float32


def shifted(value, axis, by):
    peers = lax.axis_size(axis)
    pairs = [(i, i + by) for i in range(peers) if 0 <= i + by < peers]
    return lax.ppermute(value, axis, pairs)


def lanes(shape=(8, 128)):
    return lax.broadcasted_iota(jnp.int32, shape, len(shape) - 1)


def rows(shape=(8, 128)):
    return lax.broadcasted_iota(jnp.int32, shape, len(shape) - 2)


def gather(tile, index):
    return jnp.take_along_axis(tile, index, axis=1)


def tables(perm, cond, relax, debye, factor):
    lane = lanes()

    def spread(ref):
        value = jnp.full((8, 128), ref[0], F32)
        for k in range(1, ref.shape[0]):
            value = jnp.where(lane == k, ref[k], value)
        return value

    eps = spread(perm)
    damp = spread(cond) * factor / (2.0 * eps)
    rate = spread(relax) * factor
    f0 = (1.0 - damp) / (1.0 + damp)
    f1 = 1.0 / (eps * (1.0 + damp))
    f3 = jnp.exp(-rate)
    f4 = spread(debye)
    c = f1 * rate
    return (f0 - c * f4, 0.5 * f1, c, f3, (1.0 - f3) * f4)


def to_tiles(parts):
    lane = lanes()
    kind = lane % 3
    out = []
    for t in range(3):
        mixed = jnp.where(
            kind == t, parts[0], jnp.where(kind == (t + 1) % 3, parts[1], parts[2])
        )
        out.append(gather(mixed, (3 * lane + t) & 127))
    return out


def from_tiles(tiles):
    lane = lanes()
    spread = [gather(tiles[t], (43 * (lane - t + 128)) & 127) for t in range(3)]
    out = []
    for a in range(3):
        kind = (2 * a + lane) % 3
        out.append(jnp.where(kind == 0, spread[0], jnp.where(kind == 1, spread[1], spread[2])))
    return out


def prep_kernel(fields, material, perm, cond, relax, debye, sub, e, h, p, coef, desc, wide):
    for k in range(6):
        desc[k] = jnp.full((8, 128), sub[0, 0, k], jnp.int32)

    @pl.when(is_coarse())
    def _():
        table = tables(perm, cond, relax, debye, 1.0)
        for x in range(6):
            for yt in range(3):
                for zt in range(3):
                    index = material[0, x, pl.ds(8 * yt, 8), pl.ds(128 * zt, 128)]
                    for k in range(5):
                        coef[k, x, 3 * yt + zt] = gather(table[k], index)
        for k, part in enumerate((e, h, p)):
            part[...] = fields[0, 3 * k : 3 * k + 3]

    @pl.when(is_fine())
    def _():
        for k, tile in enumerate(tables(perm, cond, relax, debye, 1.0)):
            wide[k] = tile
        for k, tile in enumerate(tables(perm, cond, relax, debye, F32(1.0 / 3.0))):
            wide[5 + k] = tile


def fine_prep_kernel(f0, f1, f2, m0, m1, m2, table, desc, box, coef):
    fields, material = (f0, f1, f2), (m0, m1, m2)

    @pl.when(is_fine())
    def _():
        tiles = [table[5 + k] for k in range(5)]
        covered = covered_of(desc)
        for x in range(6):
            inside = covered[x // 3]
            for u in range(3):
                cut = pl.ds(u, 8, stride=3)
                parts = [material[a][0, x, cut] for a in range(3)]
                for t, index in enumerate(to_tiles(parts)):
                    for k in range(5):
                        coef[k, x, 3 * u + t] = gather(tiles[k], index)
                for c in range(9):
                    parts = [fields[a][0, c, x, cut] for a in range(3)]
                    for t, tile in enumerate(to_tiles(parts)):
                        box[c, x, 3 * u + t] = jnp.where(inside, tile, 0.0)


def whole(ref, *index):
    return jnp.concatenate(
        [
            jnp.concatenate([ref[(*index, 3 * yt + zt)] for zt in range(3)], axis=1)
            for yt in range(3)
        ],
        axis=0,
    )


def magnetic(e, h, next_x, next_y, out):
    row, lane = rows((24, 384)), lanes((24, 384))

    def ahead_y(value, edge):
        return jnp.where(row == 23, edge, pltpu.roll(value, 23, 0))

    def ahead_z(value):
        return jnp.where(lane == 383, 0.0, pltpu.roll(value, 383, 1))

    for x in range(6):
        ex, ey, ez = (e[c, x] for c in range(3))
        if x < 5:
            ey_x, ez_x = e[1, x + 1], e[2, x + 1]
        else:
            ey_x, ez_x = next_x(0), next_x(1)
        ex_y = ahead_y(ex, next_y(0, x))
        ez_y = ahead_y(ez, next_y(1, x))
        ex_z, ey_z = ahead_z(ex), ahead_z(ey)
        turn = ((ez_y - ez) - (ey_z - ey), (ex_z - ex) - (ez_x - ez), (ey_x - ey) - (ex_y - ex))
        for c in range(3):
            if h is None:
                out[c, x] = -0.5 * turn[c]
            else:
                out[c, x] = h[c, x] - 0.5 * turn[c]


def last_layers(h, out_x, out_y):
    out_x[0], out_x[1] = h[1, 5], h[2, 5]
    for x in range(6):
        out_y[0, x : x + 1] = h[0, x, 23:24]
        out_y[1, x : x + 1] = h[2, x, 23:24]


def first_layers(e, out_x, out_y):
    out_x[0], out_x[1] = e[1, 0], e[2, 0]
    for x in range(6):
        out_y[0, x : x + 1] = e[0, x, 0:1]
        out_y[1, x : x + 1] = e[2, x, 0:1]


def curl_behind(h, x, prev_x, prev_y):
    row, lane = rows((24, 384)), lanes((24, 384))

    def behind_y(value, edge):
        return jnp.where(row == 0, edge, pltpu.roll(value, 1, 0))

    def behind_z(value):
        return jnp.where(lane == 0, 0.0, pltpu.roll(value, 1, 1))

    hx, hy, hz = (h[c, x] for c in range(3))
    if isinstance(x, int):
        hy_x, hz_x = (h[1, x - 1], h[2, x - 1]) if x > 0 else (prev_x(0), prev_x(1))
    else:
        before = jnp.maximum(x - 1, 0)
        first = jnp.full((24, 384), x, jnp.int32) == 0
        hy_x = jnp.where(first, prev_x(0), h[1, before])
        hz_x = jnp.where(first, prev_x(1), h[2, before])
    hx_y = behind_y(hx, prev_y(0, x))
    hz_y = behind_y(hz, prev_y(1, x))
    hx_z, hy_z = behind_z(hx), behind_z(hy)
    return ((hz - hz_y) - (hy - hy_z), (hx - hx_z) - (hz - hz_x), (hy - hy_x) - (hx - hx_y))


def electric(e, h, p, coef, prev_x, prev_y, out_e, out_p, more=None):
    for x in range(6):
        rotation = curl_behind(h, x, prev_x, prev_y)
        a, b, q, f3, g = (whole(coef, k, x) for k in range(5))
        for c in range(3):
            new = a * e[c, x] + b * rotation[c]
            old = None if p is None else p[c, x]
            if old is not None:
                new = new + q * old
            last = g * new if old is None else f3 * old + g * new
            if more is not None:
                new, last = new + more[0][c, x], last + more[1][c, x]
            out_e[c, x] = new
            out_p[c, x] = last


def edge_x(ref):
    return lambda k: ref[k]


def edge_y(ref):
    return lambda k, x: ref[k, pl.ds(x, 1)]


def corner(desc):
    x0 = jnp.max(desc[0].astype(F32)).astype(jnp.int32)
    y0 = jnp.max(desc[1].astype(F32)).astype(jnp.int32)
    base = pl.multiple_of(8 * jnp.minimum(y0 // 8, 1), 8)
    return x0, base, y0 - base


def cut_region(e, desc, spot):
    x0, base, over = spot
    place = lanes() + desc[2]
    index, part = place & 127, place >> 7

    def cut(c, i):
        tiles = []
        for a in range(3):
            pair = e[c, x0 + i, pl.ds(base, 16), pl.ds(128 * a, 128)]
            tiles.append(gather(pltpu.roll(pair, (16 - over) & 15, 0)[0:8], index))
        return jnp.where(part == 0, tiles[0], jnp.where(part == 1, tiles[1], tiles[2]))

    return [[cut(c, i) for i in range(2)] for c in range(3)]


def covered_of(desc):
    within = (rows() < desc[4]) & (lanes() < desc[5])
    return [within & (desc[3] > i) for i in range(2)]


def put(e, values, desc, spot, replace=None):
    x0, base, over = spot
    empty = jnp.zeros((8, 128), F32)
    for a in range(3):
        place = lanes() + (128 * a) - desc[2]
        index = place & 127
        here = (place >= 0) & (place < 128)
        for i in range(2):
            keep = None
            if replace is not None:
                keep = jnp.where(here, gather(replace[i], index), 0.0)
                keep = pltpu.roll(jnp.concatenate([keep, empty]), over, 0) > 0.5
            for c in range(3):
                spot = (c, x0 + i, pl.ds(base, 16), pl.ds(128 * a, 128))
                tile = jnp.where(here, gather(values(c, i), index), 0.0)
                pair = pltpu.roll(jnp.concatenate([tile, empty]), over, 0)
                if replace is None:
                    e[spot] = e[spot] + pair
                else:
                    e[spot] = jnp.where(keep, pair, e[spot])


def pack(out, box, in_x, in_y, at):
    if box is not None:
        for c in range(3):
            for i in range(2):
                out[pl.ds(at + 8 * i, 8), pl.ds(128 * c, 128)] = box[c][i]
        at += 16
    for k in range(2):
        out[pl.ds(at + 24 * k, 24)] = in_x[k]
        out[pl.ds(at + 48 + 8 * k, 6)] = in_y[k, 0:6]


def packed_box(ref, at):
    return lambda c, i: ref[pl.ds(at + 8 * i, 8), pl.ds(128 * c, 128)]


def packed_x(ref, at):
    return lambda k: ref[pl.ds(at + 24 * k, 24)]


def packed_y(ref, at):
    return lambda k, x: ref[pl.ds(at + 48 + 8 * k + x, 1)]


def fine_steps(box_in, box, coef, desc, earlier, latest):
    row, lane = rows(), lanes()
    lx, ly, lz = desc[3], desc[4], desc[5]
    inside = covered_of(desc)
    y_face = [row == 0, None, row == ly - 1]
    z_face = [lane == 0, None, lane == lz - 1]

    def up(value):
        return jnp.where(row == 7, 0.0, pltpu.roll(value, 7, 0))

    def left(value):
        return jnp.where(lane == 127, 0.0, pltpu.roll(value, 127, 1))

    def down(value):
        return jnp.where(row == 0, 0.0, pltpu.roll(value, 1, 0))

    def right(value):
        return jnp.where(lane == 0, 0.0, pltpu.roll(value, 1, 1))

    def ahead_y(values, u, t):
        return values[3 * u + 3 + t] if u < 2 else up(values[t])

    def ahead_z(values, u, t):
        return values[3 * u + t + 1] if t < 2 else left(values[3 * u])

    def behind_y(values, u, t):
        return values[3 * u - 3 + t] if u > 0 else down(values[6 + t])

    def behind_z(values, u, t):
        return values[3 * u + t - 1] if t > 0 else right(values[3 * u + 2])

    def either(p, q):
        if p is None:
            return q
        return p if q is None else p | q

    zero = jnp.zeros((8, 128), F32)

    def substep(number, old_box):
        weight = (jnp.asarray(number, F32) + 1.0) / 3.0
        driven = [
            [earlier[c][i] + weight * (latest[c][i] - earlier[c][i]) for i in range(2)]
            for c in range(3)
        ]
        for x in range(6):
            part = x // 3
            e = [[old_box[c, x, k] for k in range(9)] for c in range(3)]
            if x < 5:
                ey_x = [old_box[1, x + 1, k] for k in range(9)]
                ez_x = [old_box[2, x + 1, k] for k in range(9)]
            else:
                ey_x = ez_x = [zero] * 9
            h = [[], [], []]
            for u in range(3):
                for t in range(3):
                    k = 3 * u + t
                    ex, ey, ez = e[0][k], e[1][k], e[2][k]
                    turn = (
                        (ahead_y(e[2], u, t) - ez) - (ahead_z(e[1], u, t) - ey),
                        (ahead_z(e[0], u, t) - ex) - (ez_x[k] - ez),
                        (ey_x[k] - ey) - (ahead_y(e[0], u, t) - ex),
                    )
                    for c in range(3):
                        value = old_box[3 + c, x, k] - 0.5 * turn[c]
                        box[3 + c, x, k] = value
                        h[c].append(value)
            x_face = x == 0
            if x in (2, 5):
                x_face = 3 * lx - 1 == x
            for u in range(3):
                for t in range(3):
                    k = 3 * u + t
                    hx, hy, hz = h[0][k], h[1][k], h[2][k]
                    hy_x = box[4, x - 1, k] if x > 0 else zero
                    hz_x = box[5, x - 1, k] if x > 0 else zero
                    rotation = (
                        (hz - behind_y(h[2], u, t)) - (hy - behind_z(h[1], u, t)),
                        (hx - behind_z(h[0], u, t)) - (hz - hz_x),
                        (hy - hy_x) - (hx - behind_y(h[0], u, t)),
                    )
                    a, b, p, f3, g = (coef[q, x, k] for q in range(5))
                    faces = (
                        either(y_face[u], z_face[t]),
                        None if x_face is True else either(x_face if x in (2, 5) else None, z_face[t]),
                        None if x_face is True else either(x_face if x in (2, 5) else None, y_face[u]),
                    )
                    for c in range(3):
                        old = old_box[6 + c, x, k]
                        new = a * e[c][k] + b * rotation[c] + p * old
                        if c > 0 and x_face is True:
                            new = driven[c][part]
                        elif faces[c] is not None:
                            new = jnp.where(faces[c], driven[c][part], new)
                        new = jnp.where(inside[part], new, 0.0)
                        box[c, x, k] = new
                        box[6 + c, x, k] = f3 * old + g * new

    substep(0, box_in)

    def further(number, carry):
        substep(number, box)
        return carry

    lax.fori_loop(1, 3, further, 0)
    restricted = [[zero, zero] for c in range(3)]
    for c in range(3):
        for i in range(2):
            total = zero
            for x in range(3 * i, 3 * i + 3):
                for k in range(9):
                    total = total + box[c, x, k]
            restricted[c][i] = total * F32(1.0 / 27.0)
    return restricted


def feed_back(restricted, latest, desc):
    covered = covered_of(desc)
    after = [[jnp.where(covered[i], restricted[c][i], latest[c][i]) for i in range(2)] for c in range(3)]
    return after, [[after[c][i] - latest[c][i] for i in range(2)] for c in range(3)]


def store_box(ref, values):
    for c in range(3):
        for i in range(2):
            ref[c, i] = values[c][i]


def store_tiles(ref, values):
    for c in range(3):
        for i in range(2):
            ref[2 * c + i] = values[c][i]


def load_box(ref):
    return [[ref[c, i] for i in range(2)] for c in range(3)]


def is_coarse():
    return lax.axis_index("grid") == 0


def is_fine():
    return lax.axis_index("grid") == 1


def edge_kernel(near_x, near_y, ax, ay):
    @pl.when(is_coarse())
    def _():
        ax[0], ax[1] = near_x[0, 1, 0], near_x[0, 2, 0]
        for x in range(6):
            ay[0, x : x + 1] = near_y[0, 0, x, 0:1]
            ay[1, x : x + 1] = near_y[0, 2, x, 0:1]


def h1_kernel(e, h, ax, ay, material, desc, out_h, bx, by, sent):
    @pl.when(is_coarse())
    def _():
        sent[0:6] = material[0].astype(F32)
        before = cut_region(e, desc, corner(desc))
        for c in range(3):
            for i in range(2):
                sent[6, pl.ds(8 * i, 8), pl.ds(128 * c, 128)] = before[c][i]
        magnetic(e, h, edge_x(ax), edge_y(ay), out_h)
        last_layers(out_h, bx, by)


def e1_kernel(
    e, h, p, coef, bx, by, desc, material, table, out_e, out_p, sent, slab_coef, first
):
    @pl.when(is_coarse())
    def _():
        electric(e, h, p, coef, edge_x(bx), edge_y(by), out_e, out_p)
        for k, tile in enumerate(sum(cut_region(out_e, desc, corner(desc)), [])):
            sent[k] = tile
        slab_coef[...] = coef[...]

    @pl.when(is_fine())
    def _():
        for c in range(3):
            for i in range(2):
                first[c, i] = material[6, pl.ds(8 * i, 8), pl.ds(128 * c, 128)]
        tiles = [table[k] for k in range(5)]
        for x in range(6):
            for yt in range(3):
                for zt in range(3):
                    index = material[x, pl.ds(8 * yt, 8), pl.ds(128 * zt, 128)].astype(jnp.int32)
                    for k in range(5):
                        slab_coef[k, x, 3 * yt + zt] = gather(tiles[k], index)


def f1_kernel(
    e, h, p, box_in, coef, first, region, desc, out_e, out_h, out_p, ax, ay, box, now, change
):
    @pl.when(is_coarse())
    def _():
        out_e[...], out_h[...], out_p[...] = e[...], h[...], p[...]
        first_layers(e, ax, ay)

    @pl.when(is_fine())
    def _():
        for out in (out_e, out_h, out_p):
            out[...] = jnp.zeros(out.shape, F32)
        earlier = load_box(first)
        latest = [[region[2 * c + i] for i in range(2)] for c in range(3)]
        restricted = fine_steps(box_in, box, coef, desc, earlier, latest)
        after, delta = feed_back(restricted, latest, desc)
        store_box(now, after)
        store_box(change, delta)
        put(out_e, lambda c, i: delta[c][i], desc, corner(desc))
        first_layers(out_e, ax, ay)


def h2_kernel(e, h, ax, ay, out_h, bx, by):
    magnetic(e, h, edge_x(ax), edge_y(ay), out_h)
    last_layers(out_h, bx, by)


def base_kernel(e, h, p, coef, bx, by, desc, out_e, out_p, sent):
    @pl.when(is_coarse())
    def _():
        electric(e, h, p, coef, edge_x(bx), edge_y(by), out_e, out_p)
        store_tiles(sent, cut_region(out_e, desc, corner(desc)))


def f2_kernel(
    e, h, p, base_e, base_p, coef, slab_coef, bx, by, desc, box_in, region, was,
    out_e, out_p, ax, ay, box, now, change,
):
    @pl.when(is_coarse())
    def _():
        out_e[...], out_p[...] = base_e[...], base_p[...]
        first_layers(base_e, ax, ay)

    @pl.when(is_fine())
    def _():
        spot = corner(desc)
        electric(e, h, p, slab_coef, edge_x(bx), edge_y(by), out_e, out_p)
        fix = cut_region(out_e, desc, spot)
        latest = [[region[2 * c + i] + fix[c][i] for i in range(2)] for c in range(3)]
        restricted = fine_steps(box_in, box, coef, desc, load_box(was), latest)
        after, delta = feed_back(restricted, latest, desc)
        store_box(now, after)
        store_box(change, delta)
        put(out_e, lambda c, i: delta[c][i], desc, spot)
        first_layers(out_e, ax, ay)


def h3_kernel(
    e, h, ax, ay, change1, ax2, ay2, change2, bx2, by2, out_h, bx, by, relay,
):
    magnetic(e, h, edge_x(ax), edge_y(ay), out_h)
    last_layers(out_h, bx, by)

    @pl.when(is_fine())
    def _():
        pack(relay, load_box(change1), ax2, ay2, 0)
        pack(relay, load_box(change2), bx2, by2, 80)
        pack(relay, None, ax, ay, 160)


def f3_kernel(
    e, h, p, coef, slab_coef, bx, by, desc, box_in, region, was, relay_in,
    box, relay, fix_e, fix_h, fix_p, layer, one_e, one_h,
):
    @pl.when(is_coarse())
    def _():
        one_e[...] = jnp.zeros(one_e.shape, F32)
        spot = corner(desc)
        put(one_e, packed_box(relay_in, 0), desc, spot)
        magnetic(one_e, None, packed_x(relay_in, 16), packed_y(relay_in, 16), one_h)
        electric(
            one_e, one_h, None, slab_coef, packed_x(relay_in, 96), packed_y(relay_in, 96), fix_e, fix_p
        )
        put(fix_e, packed_box(relay_in, 80), desc, spot)
        magnetic(fix_e, one_h, packed_x(relay_in, 160), packed_y(relay_in, 160), fix_h)

    @pl.when(is_fine())
    def _():
        spot = corner(desc)
        x0 = spot[0]
        for i in range(2):
            x = x0 + i
            rotation = curl_behind(h, x, edge_x(bx), edge_y(by))
            a, b, q = (whole(slab_coef, k, x) for k in range(3))
            for c in range(3):
                layer[c, i] = a * e[c, x] + b * rotation[c] + q * p[c, x]
        fix = cut_region(layer, desc, (0, *spot[1:]))
        latest = [[region[2 * c + i] + fix[c][i] for i in range(2)] for c in range(3)]
        restricted = fine_steps(box_in, box, coef, desc, load_box(was), latest)
        pack(relay, restricted, bx, by, 0)


def finish_kernel(e, h, p, fix_e, fix_h, fix_p, coef, desc, relay, box, out, mixed):
    @pl.when(is_coarse())
    def _():
        view_e, view_p = out.at[pl.ds(0, 3)], out.at[pl.ds(6, 3)]
        electric(
            fix_e, fix_h, fix_p, coef, packed_x(relay, 16), packed_y(relay, 16),
            view_e, view_p, (e, p),
        )
        out[3:6] = h[...] + fix_h[...]
        covered = [jnp.where(value, F32(1.0), 0.0) for value in covered_of(desc)]
        put(view_e, packed_box(relay, 0), desc, corner(desc), covered)

    @pl.when(is_fine())
    def _():
        for c in range(9):
            for x in range(6):
                for u in range(3):
                    parts = from_tiles([box[c, x, 3 * u + t] for t in range(3)])
                    for a in range(3):
                        mixed[c, x, a, pl.ds(u, 8, stride=3)] = parts[a]
                for a in range(3):
                    out[c, x, :, pl.ds(128 * a, 128)] = mixed[c, x, a]


def third(shape, a):
    return pl.BlockSpec(shape, lambda i: (0,) * (len(shape) - 1) + (a,))


def call(kernel, operands, outs, specs=None, scratch=(), grid=()):
    shapes = [out if isinstance(out, jax.ShapeDtypeStruct) else jax.ShapeDtypeStruct(out, F32) for out in outs]
    return pl.pallas_call(
        kernel,
        out_shape=shapes,
        in_specs=specs or [VM] * len(operands),
        out_specs=[VM] * len(outs),
        grid=grid,
        scratch_shapes=scratch,
        compiler_params=pltpu.CompilerParams(vmem_limit_bytes=LIMIT),
    )(*operands)


PART = (3, 6, 24, 384)
SLAB = (9, 6, 24, 384)
BOX = (9, 6, 9, 8, 128)
COEF = (5, 6, 9, 8, 128)
REGION = (3, 2, 8, 128)
X_EDGE = (2, 24, 384)
Y_EDGE = (2, 6, 384)
EDGES = [X_EDGE, Y_EDGE]
LAST = EDGES
AXES = ("grid", "gx", "gy")


def exchange(x_edge, y_edge, by, groups):
    na, nb = lax.axis_size("gx"), lax.axis_size("gy")

    def pairs(da, db):
        return [
            ((g * na + a) * nb + b, (g * na + a + da) * nb + b + db)
            for g in groups
            for a in range(na)
            for b in range(nb)
            if 0 <= a + da < na and 0 <= b + db < nb
        ]

    return (
        lax.ppermute(x_edge, AXES, pairs(by, 0)),
        lax.ppermute(y_edge, AXES, pairs(0, by)),
    )


def to_fine(value):
    return shifted(value, "grid", 1)


def to_coarse(value):
    return shifted(value, "grid", -1)


def body(fields, material, permittivity, conductivity, relax_rate, debye_strength, subgrids):
    ax, ay = call(
        edge_kernel,
        (fields, fields),
        EDGES,
        [
            pl.BlockSpec((1, 3, 1, 24, 384), lambda i: (0, 0, 0, 0, 0)),
            pl.BlockSpec((1, 3, 6, 8, 384), lambda i: (0, 0, 0, 0, 0)),
        ],
        grid=(1,),
    )
    ax, ay = exchange(ax, ay, -1, (0,))
    e, h, p, coef, desc, table = call(
        prep_kernel,
        (fields, material, permittivity, conductivity, relax_rate, debye_strength, subgrids),
        [PART] * 3 + [COEF, jax.ShapeDtypeStruct((6, 8, 128), jnp.int32), (10, 8, 128)],
        [VM] * 2 + [SM] * 5,
    )
    box, fine_coef = call(
        fine_prep_kernel,
        (fields,) * 3 + (material,) * 3 + (table, desc),
        [BOX, COEF],
        [third((1, 9, 6, 24, 128), a) for a in range(3)]
        + [third((1, 6, 24, 128), a) for a in range(3)]
        + [VM] * 2,
        grid=(1,),
    )
    h, bx, by, slab_material = call(
        h1_kernel,
        (e, h, ax, ay, material, desc),
        [PART] + LAST + [(7, 24, 384)],
    )
    slab_material = to_fine(slab_material)
    bx, by = exchange(bx, by, 1, (0,))
    e, p, sent, slab_coef, first = call(
        e1_kernel,
        (e, h, p, coef, bx, by, desc, slab_material, table),
        [PART] * 2 + [(6, 8, 128), COEF, REGION],
    )
    region = to_fine(sent)
    e, h, p, ax, ay, box, now, change1 = call(
        f1_kernel,
        (e, h, p, box, fine_coef, first, region, desc),
        [PART] * 3 + EDGES + [BOX, REGION, REGION],
    )
    ax2, ay2 = exchange(ax, ay, -1, (0, 1))
    h, bx, by = call(h2_kernel, (e, h, ax2, ay2), [PART] + LAST)
    bx2, by2 = exchange(bx, by, 1, (1,))
    bx, by = exchange(bx, by, 1, (0,))
    base_e, base_p, sent = call(
        base_kernel, (e, h, p, slab_coef, bx, by, desc), [PART] * 2 + [(19, 8, 128)]
    )
    region = to_fine(sent)
    e, p, ax, ay, box, now, change2 = call(
        f2_kernel,
        (e, h, p, base_e, base_p, fine_coef, slab_coef, bx2, by2, desc, box, region, now),
        [PART] * 2 + EDGES + [BOX, REGION, REGION],
    )
    ax, ay = exchange(ax, ay, -1, (0, 1))
    h, bx, by, relay = call(
        h3_kernel,
        (e, h, ax, ay, change1, ax2, ay2, change2, bx2, by2),
        [PART] + LAST + [(224, 384)],
    )
    relay = to_coarse(relay)
    fine_bx, fine_by = exchange(bx, by, 1, (1,))
    bx, by = exchange(bx, by, 1, (0,))
    base_e, base_p, sent = call(
        base_kernel, (e, h, p, slab_coef, bx, by, desc), [PART] * 2 + [(19, 8, 128)]
    )
    region = to_fine(sent)
    box, relay4, *fix = call(
        f3_kernel,
        (e, h, p, fine_coef, slab_coef, fine_bx, fine_by, desc, box, region, now, relay),
        [BOX, (80, 384)] + [PART] * 3,
        scratch=[
            pltpu.VMEM((3, 2, 24, 384), F32),
            pltpu.VMEM(PART, F32),
            pltpu.VMEM(PART, F32),
        ],
    )
    relay4 = to_coarse(relay4)
    (out,) = call(
        finish_kernel,
        (base_e, h, base_p, *fix, coef, desc, relay4, box),
        [SLAB],
        scratch=[pltpu.VMEM((9, 6, 3, 24, 128), F32)],
    )
    return out[None]


def solution(mesh):
    in_specs = (
        P("grid", None, "gx", "gy", None),
        P("grid", "gx", "gy", None),
        P(),
        P(),
        P(),
        P(),
        P("gx", "gy", None),
    )
    out_specs = P("grid", None, "gx", "gy", None)
    return jax.shard_map(body, mesh=mesh, in_specs=in_specs, out_specs=out_specs, check_vma=False)
```

```python
import functools

import jax
import jax.numpy as jnp
from jax import lax
from jax.experimental import pallas as pl
from jax.experimental.pallas import tpu as pltpu
from jax.sharding import PartitionSpec as P

COARSE_STEPS = 3
LIMIT = 40 * 1024 * 1024
VM = pl.BlockSpec(memory_space=pltpu.VMEM)
SM = pl.BlockSpec(memory_space=pltpu.SMEM)
F32 = jnp.float32


def shifted(value, axis, by):
    peers = lax.axis_size(axis)
    pairs = [(i, i + by) for i in range(peers) if 0 <= i + by < peers]
    return lax.ppermute(value, axis, pairs)


def lanes(shape=(8, 128)):
    return lax.broadcasted_iota(jnp.int32, shape, len(shape) - 1)


def rows(shape=(8, 128)):
    return lax.broadcasted_iota(jnp.int32, shape, len(shape) - 2)


def gather(tile, index):
    return jnp.take_along_axis(tile, index, axis=1)


def tables(perm, cond, relax, debye, factor):
    lane = lanes()

    def spread(ref):
        value = jnp.full((8, 128), ref[0], F32)
        for k in range(1, ref.shape[0]):
            value = jnp.where(lane == k, ref[k], value)
        return value

    eps = spread(perm)
    damp = spread(cond) * factor / (2.0 * eps)
    rate = spread(relax) * factor
    f0 = (1.0 - damp) / (1.0 + damp)
    f1 = 1.0 / (eps * (1.0 + damp))
    f3 = jnp.exp(-rate)
    f4 = spread(debye)
    c = f1 * rate
    return (f0 - c * f4, 0.5 * f1, c, f3, (1.0 - f3) * f4)


def to_tiles(parts):
    lane = lanes()
    kind = lane % 3
    out = []
    for t in range(3):
        mixed = jnp.where(
            kind == t, parts[0], jnp.where(kind == (t + 1) % 3, parts[1], parts[2])
        )
        out.append(gather(mixed, (3 * lane + t) & 127))
    return out


def from_tiles(tiles):
    lane = lanes()
    spread = [gather(tiles[t], (43 * (lane - t + 128)) & 127) for t in range(3)]
    out = []
    for a in range(3):
        kind = (2 * a + lane) % 3
        out.append(jnp.where(kind == 0, spread[0], jnp.where(kind == 1, spread[1], spread[2])))
    return out


def prep_kernel(fields, material, perm, cond, relax, debye, sub, e, h, p, coef, desc, wide):
    for k in range(6):
        desc[k] = jnp.full((8, 128), sub[0, 0, k], jnp.int32)

    @pl.when(is_coarse())
    def _():
        table = tables(perm, cond, relax, debye, 1.0)
        for x in range(6):
            for yt in range(3):
                for zt in range(3):
                    index = material[0, x, pl.ds(8 * yt, 8), pl.ds(128 * zt, 128)]
                    for k in range(5):
                        coef[k, x, 3 * yt + zt] = gather(table[k], index)
        for k, part in enumerate((e, h, p)):
            part[...] = fields[0, 3 * k : 3 * k + 3]

    @pl.when(is_fine())
    def _():
        for k, tile in enumerate(tables(perm, cond, relax, debye, 1.0)):
            wide[k] = tile
        for k, tile in enumerate(tables(perm, cond, relax, debye, F32(1.0 / 3.0))):
            wide[5 + k] = tile


def fine_prep_kernel(f0, f1, f2, m0, m1, m2, table, desc, box, coef):
    fields, material = (f0, f1, f2), (m0, m1, m2)

    @pl.when(is_fine())
    def _():
        tiles = [table[5 + k] for k in range(5)]
        covered = covered_of(desc)
        for x in range(6):
            inside = covered[x // 3]
            for u in range(3):
                cut = pl.ds(u, 8, stride=3)
                parts = [material[a][0, x, cut] for a in range(3)]
                for t, index in enumerate(to_tiles(parts)):
                    for k in range(5):
                        coef[k, x, 3 * u + t] = gather(tiles[k], index)
                for c in range(9):
                    parts = [fields[a][0, c, x, cut] for a in range(3)]
                    for t, tile in enumerate(to_tiles(parts)):
                        box[c, x, 3 * u + t] = jnp.where(inside, tile, 0.0)


def whole(ref, *index):
    return jnp.concatenate(
        [
            jnp.concatenate([ref[(*index, 3 * yt + zt)] for zt in range(3)], axis=1)
            for yt in range(3)
        ],
        axis=0,
    )


def magnetic(e, h, next_x, next_y, out):
    row, lane = rows((24, 384)), lanes((24, 384))

    def ahead_y(value, edge):
        return jnp.where(row == 23, edge, pltpu.roll(value, 23, 0))

    def ahead_z(value):
        return jnp.where(lane == 383, 0.0, pltpu.roll(value, 383, 1))

    for x in range(6):
        ex, ey, ez = (e[c, x] for c in range(3))
        if x < 5:
            ey_x, ez_x = e[1, x + 1], e[2, x + 1]
        else:
            ey_x, ez_x = next_x(0), next_x(1)
        ex_y = ahead_y(ex, next_y(0, x))
        ez_y = ahead_y(ez, next_y(1, x))
        ex_z, ey_z = ahead_z(ex), ahead_z(ey)
        turn = ((ez_y - ez) - (ey_z - ey), (ex_z - ex) - (ez_x - ez), (ey_x - ey) - (ex_y - ex))
        for c in range(3):
            if h is None:
                out[c, x] = -0.5 * turn[c]
            else:
                out[c, x] = h[c, x] - 0.5 * turn[c]


def last_layers(h, out_x, out_y):
    out_x[0], out_x[1] = h[1, 5], h[2, 5]
    for x in range(6):
        out_y[0, x : x + 1] = h[0, x, 23:24]
        out_y[1, x : x + 1] = h[2, x, 23:24]


def first_layers(e, out_x, out_y):
    out_x[0], out_x[1] = e[1, 0], e[2, 0]
    for x in range(6):
        out_y[0, x : x + 1] = e[0, x, 0:1]
        out_y[1, x : x + 1] = e[2, x, 0:1]


def curl_behind(h, x, prev_x, prev_y):
    row, lane = rows((24, 384)), lanes((24, 384))

    def behind_y(value, edge):
        return jnp.where(row == 0, edge, pltpu.roll(value, 1, 0))

    def behind_z(value):
        return jnp.where(lane == 0, 0.0, pltpu.roll(value, 1, 1))

    hx, hy, hz = (h[c, x] for c in range(3))
    if prev_x is None:
        prev_x, prev_y = lambda k: 0.0, lambda k, x: 0.0
    if isinstance(x, int):
        hy_x, hz_x = (h[1, x - 1], h[2, x - 1]) if x > 0 else (prev_x(0), prev_x(1))
    else:
        before = jnp.maximum(x - 1, 0)
        first = jnp.full((24, 384), x, jnp.int32) == 0
        hy_x = jnp.where(first, prev_x(0), h[1, before])
        hz_x = jnp.where(first, prev_x(1), h[2, before])
    hx_y = behind_y(hx, prev_y(0, x))
    hz_y = behind_y(hz, prev_y(1, x))
    hx_z, hy_z = behind_z(hx), behind_z(hy)
    return ((hz - hz_y) - (hy - hy_z), (hx - hx_z) - (hz - hz_x), (hy - hy_x) - (hx - hx_y))


def electric(e, h, p, coef, prev_x, prev_y, out_e, out_p, more=None):
    for x in range(6):
        rotation = curl_behind(h, x, prev_x, prev_y)
        a, b, q, f3, g = (whole(coef, k, x) for k in range(5))
        for c in range(3):
            new = a * e[c, x] + b * rotation[c]
            old = None if p is None else p[c, x]
            if old is not None:
                new = new + q * old
            last = g * new if old is None else f3 * old + g * new
            if more is not None:
                new, last = new + more[0][c, x], last + more[1][c, x]
            out_e[c, x] = new
            out_p[c, x] = last


def complete(part_e, part_p, coef, prev_x, prev_y, out_e, out_p):
    for x in range(6):
        b, g = (jnp.concatenate([coef[k, x, zt, 0:1] for zt in range(3)], axis=1) for k in (1, 4))
        for c in range(3):
            new, last = part_e[c, x], part_p[c, x]
            if x == 0 and c > 0:
                more = whole(coef, 1, 0) * (prev_x(1) if c == 1 else -prev_x(0))
                new, last = new + more, last + whole(coef, 4, 0) * more
            out_e[c, x], out_p[c, x] = new, last
            if c != 1:
                more = b * (-prev_y(1, x) if c == 0 else prev_y(0, x))
                out_e[c, x, 0:1] = new[0:1] + more
                out_p[c, x, 0:1] = last[0:1] + g * more


def edge_x(ref):
    return lambda k: ref[k]


def edge_y(ref):
    return lambda k, x: ref[k, pl.ds(x, 1)]


def corner(desc):
    x0 = jnp.max(desc[0].astype(F32)).astype(jnp.int32)
    y0 = jnp.max(desc[1].astype(F32)).astype(jnp.int32)
    base = pl.multiple_of(8 * jnp.minimum(y0 // 8, 1), 8)
    return x0, base, y0 - base


def cut_region(e, desc, spot):
    x0, base, over = spot
    place = lanes() + desc[2]
    index, part = place & 127, place >> 7

    def cut(c, i):
        tiles = []
        for a in range(3):
            pair = e[c, x0 + i, pl.ds(base, 16), pl.ds(128 * a, 128)]
            tiles.append(gather(pltpu.roll(pair, (16 - over) & 15, 0)[0:8], index))
        return jnp.where(part == 0, tiles[0], jnp.where(part == 1, tiles[1], tiles[2]))

    return [[cut(c, i) for i in range(2)] for c in range(3)]


def covered_of(desc):
    within = (rows() < desc[4]) & (lanes() < desc[5])
    return [within & (desc[3] > i) for i in range(2)]


def put(e, values, desc, spot, replace=None):
    x0, base, over = spot
    empty = jnp.zeros((8, 128), F32)
    for a in range(3):
        place = lanes() + (128 * a) - desc[2]
        index = place & 127
        here = (place >= 0) & (place < 128)
        for i in range(2):
            keep = None
            if replace is not None:
                keep = jnp.where(here, gather(replace[i], index), 0.0)
                keep = pltpu.roll(jnp.concatenate([keep, empty]), over, 0) > 0.5
            for c in range(3):
                spot = (c, x0 + i, pl.ds(base, 16), pl.ds(128 * a, 128))
                tile = jnp.where(here, gather(values(c, i), index), 0.0)
                pair = pltpu.roll(jnp.concatenate([tile, empty]), over, 0)
                if replace is None:
                    e[spot] = e[spot] + pair
                else:
                    e[spot] = jnp.where(keep, pair, e[spot])


def pack(out, box, in_x, in_y, at):
    if box is not None:
        for c in range(3):
            for i in range(2):
                out[pl.ds(at + 8 * i, 8), pl.ds(128 * c, 128)] = box[c][i]
        at += 16
    for k in range(2):
        out[pl.ds(at + 24 * k, 24)] = in_x[k]
        out[pl.ds(at + 48 + 8 * k, 6)] = in_y[k, 0:6]


def packed_box(ref, at):
    return lambda c, i: ref[pl.ds(at + 8 * i, 8), pl.ds(128 * c, 128)]


def packed_x(ref, at):
    return lambda k: ref[pl.ds(at + 24 * k, 24)]


def packed_y(ref, at):
    return lambda k, x: ref[pl.ds(at + 48 + 8 * k + x, 1)]


def fine_steps(box_in, box, coef, desc, earlier, latest):
    row, lane = rows(), lanes()
    lx, ly, lz = desc[3], desc[4], desc[5]
    inside = covered_of(desc)
    y_face = [row == 0, None, row == ly - 1]
    z_face = [lane == 0, None, lane == lz - 1]

    def up(value):
        return jnp.where(row == 7, 0.0, pltpu.roll(value, 7, 0))

    def left(value):
        return jnp.where(lane == 127, 0.0, pltpu.roll(value, 127, 1))

    def down(value):
        return jnp.where(row == 0, 0.0, pltpu.roll(value, 1, 0))

    def right(value):
        return jnp.where(lane == 0, 0.0, pltpu.roll(value, 1, 1))

    def ahead_y(values, u, t):
        return values[3 * u + 3 + t] if u < 2 else up(values[t])

    def ahead_z(values, u, t):
        return values[3 * u + t + 1] if t < 2 else left(values[3 * u])

    def behind_y(values, u, t):
        return values[3 * u - 3 + t] if u > 0 else down(values[6 + t])

    def behind_z(values, u, t):
        return values[3 * u + t - 1] if t > 0 else right(values[3 * u + 2])

    def either(p, q):
        if p is None:
            return q
        return p if q is None else p | q

    zero = jnp.zeros((8, 128), F32)

    def substep(number, old_box):
        weight = (jnp.asarray(number, F32) + 1.0) / 3.0
        driven = [
            [earlier[c][i] + weight * (latest[c][i] - earlier[c][i]) for i in range(2)]
            for c in range(3)
        ]
        for x in range(6):
            part = x // 3
            e = [[old_box[c, x, k] for k in range(9)] for c in range(3)]
            if x < 5:
                ey_x = [old_box[1, x + 1, k] for k in range(9)]
                ez_x = [old_box[2, x + 1, k] for k in range(9)]
            else:
                ey_x = ez_x = [zero] * 9
            h = [[], [], []]
            for u in range(3):
                for t in range(3):
                    k = 3 * u + t
                    ex, ey, ez = e[0][k], e[1][k], e[2][k]
                    turn = (
                        (ahead_y(e[2], u, t) - ez) - (ahead_z(e[1], u, t) - ey),
                        (ahead_z(e[0], u, t) - ex) - (ez_x[k] - ez),
                        (ey_x[k] - ey) - (ahead_y(e[0], u, t) - ex),
                    )
                    for c in range(3):
                        value = old_box[3 + c, x, k] - 0.5 * turn[c]
                        box[3 + c, x, k] = value
                        h[c].append(value)
            x_face = x == 0
            if x in (2, 5):
                x_face = 3 * lx - 1 == x
            for u in range(3):
                for t in range(3):
                    k = 3 * u + t
                    hx, hy, hz = h[0][k], h[1][k], h[2][k]
                    hy_x = box[4, x - 1, k] if x > 0 else zero
                    hz_x = box[5, x - 1, k] if x > 0 else zero
                    rotation = (
                        (hz - behind_y(h[2], u, t)) - (hy - behind_z(h[1], u, t)),
                        (hx - behind_z(h[0], u, t)) - (hz - hz_x),
                        (hy - hy_x) - (hx - behind_y(h[0], u, t)),
                    )
                    a, b, p, f3, g = (coef[q, x, k] for q in range(5))
                    faces = (
                        either(y_face[u], z_face[t]),
                        None if x_face is True else either(x_face if x in (2, 5) else None, z_face[t]),
                        None if x_face is True else either(x_face if x in (2, 5) else None, y_face[u]),
                    )
                    for c in range(3):
                        old = old_box[6 + c, x, k]
                        new = a * e[c][k] + b * rotation[c] + p * old
                        if c > 0 and x_face is True:
                            new = driven[c][part]
                        elif faces[c] is not None:
                            new = jnp.where(faces[c], driven[c][part], new)
                        new = jnp.where(inside[part], new, 0.0)
                        box[c, x, k] = new
                        box[6 + c, x, k] = f3 * old + g * new

    substep(0, box_in)

    def further(number, carry):
        substep(number, box)
        return carry

    lax.fori_loop(1, 3, further, 0)
    restricted = [[zero, zero] for c in range(3)]
    for c in range(3):
        for i in range(2):
            total = zero
            for x in range(3 * i, 3 * i + 3):
                for k in range(9):
                    total = total + box[c, x, k]
            restricted[c][i] = total * F32(1.0 / 27.0)
    return restricted


def feed_back(restricted, latest, desc):
    covered = covered_of(desc)
    after = [[jnp.where(covered[i], restricted[c][i], latest[c][i]) for i in range(2)] for c in range(3)]
    return after, [[after[c][i] - latest[c][i] for i in range(2)] for c in range(3)]


def store_box(ref, values):
    for c in range(3):
        for i in range(2):
            ref[c, i] = values[c][i]


def store_tiles(ref, values):
    for c in range(3):
        for i in range(2):
            ref[2 * c + i] = values[c][i]


def load_box(ref):
    return [[ref[c, i] for i in range(2)] for c in range(3)]


def is_coarse():
    return lax.axis_index("grid") == 0


def is_fine():
    return lax.axis_index("grid") == 1


def edge_kernel(near_x, near_y, ax, ay):
    @pl.when(is_coarse())
    def _():
        ax[0], ax[1] = near_x[0, 1, 0], near_x[0, 2, 0]
        for x in range(6):
            ay[0, x : x + 1] = near_y[0, 0, x, 0:1]
            ay[1, x : x + 1] = near_y[0, 2, x, 0:1]


def coarse_part_kernel(e, h, p, coef, out_e, out_p):
    @pl.when(is_coarse())
    def _():
        electric(e, h, p, coef, None, None, out_e, out_p)


def fine_part_kernel(e, h, p, coef, out_e, out_p):
    @pl.when(is_fine())
    def _():
        electric(e, h, p, coef, None, None, out_e, out_p)


def h1_kernel(e, h, ax, ay, material, desc, out_h, bx, by, sent):
    @pl.when(is_coarse())
    def _():
        sent[0:6] = material[0].astype(F32)
        before = cut_region(e, desc, corner(desc))
        for c in range(3):
            for i in range(2):
                sent[6, pl.ds(8 * i, 8), pl.ds(128 * c, 128)] = before[c][i]
        magnetic(e, h, edge_x(ax), edge_y(ay), out_h)
        last_layers(out_h, bx, by)


def e1_kernel(
    e, p, coef, bx, by, desc, material, table, out_e, out_p, sent, slab_coef, first
):
    @pl.when(is_coarse())
    def _():
        complete(e, p, coef, edge_x(bx), edge_y(by), out_e, out_p)
        for k, tile in enumerate(sum(cut_region(out_e, desc, corner(desc)), [])):
            sent[k] = tile
        slab_coef[...] = coef[...]

    @pl.when(is_fine())
    def _():
        for c in range(3):
            for i in range(2):
                first[c, i] = material[6, pl.ds(8 * i, 8), pl.ds(128 * c, 128)]
        tiles = [table[k] for k in range(5)]
        for x in range(6):
            for yt in range(3):
                for zt in range(3):
                    index = material[x, pl.ds(8 * yt, 8), pl.ds(128 * zt, 128)].astype(jnp.int32)
                    for k in range(5):
                        slab_coef[k, x, 3 * yt + zt] = gather(tiles[k], index)


def f1_kernel(
    e, h, p, box_in, coef, first, region, desc, out_e, out_h, out_p, ax, ay, box, now, change
):
    @pl.when(is_coarse())
    def _():
        out_e[...], out_h[...], out_p[...] = e[...], h[...], p[...]
        first_layers(e, ax, ay)

    @pl.when(is_fine())
    def _():
        for out in (out_e, out_h, out_p):
            out[...] = jnp.zeros(out.shape, F32)
        earlier = load_box(first)
        latest = [[region[2 * c + i] for i in range(2)] for c in range(3)]
        restricted = fine_steps(box_in, box, coef, desc, earlier, latest)
        after, delta = feed_back(restricted, latest, desc)
        store_box(now, after)
        store_box(change, delta)
        put(out_e, lambda c, i: delta[c][i], desc, corner(desc))
        first_layers(out_e, ax, ay)


def h2_kernel(e, h, ax, ay, out_h, bx, by):
    magnetic(e, h, edge_x(ax), edge_y(ay), out_h)
    last_layers(out_h, bx, by)


def base_kernel(e, h, p, coef, bx, by, desc, out_e, out_p, sent):
    @pl.when(is_coarse())
    def _():
        electric(e, h, p, coef, edge_x(bx), edge_y(by), out_e, out_p)
        store_tiles(sent, cut_region(out_e, desc, corner(desc)))


def f2_kernel(
    e, p, base_e, base_p, coef, slab_coef, bx, by, desc, box_in, region, was,
    out_e, out_p, ax, ay, box, now, change,
):
    @pl.when(is_coarse())
    def _():
        out_e[...], out_p[...] = base_e[...], base_p[...]
        first_layers(base_e, ax, ay)

    @pl.when(is_fine())
    def _():
        spot = corner(desc)
        complete(e, p, slab_coef, edge_x(bx), edge_y(by), out_e, out_p)
        fix = cut_region(out_e, desc, spot)
        latest = [[region[2 * c + i] + fix[c][i] for i in range(2)] for c in range(3)]
        restricted = fine_steps(box_in, box, coef, desc, load_box(was), latest)
        after, delta = feed_back(restricted, latest, desc)
        store_box(now, after)
        store_box(change, delta)
        put(out_e, lambda c, i: delta[c][i], desc, spot)
        first_layers(out_e, ax, ay)


def h3_kernel(
    e, h, ax, ay, change1, ax2, ay2, change2, bx2, by2, out_h, bx, by, relay,
):
    magnetic(e, h, edge_x(ax), edge_y(ay), out_h)
    last_layers(out_h, bx, by)

    @pl.when(is_fine())
    def _():
        pack(relay, load_box(change1), ax2, ay2, 0)
        pack(relay, load_box(change2), bx2, by2, 80)
        pack(relay, None, ax, ay, 160)


def f3_kernel(
    e, h, p, coef, slab_coef, bx, by, desc, box_in, region, was, relay_in,
    box, relay, fix_e, fix_h, fix_p, layer, one_e, one_h,
):
    @pl.when(is_coarse())
    def _():
        one_e[...] = jnp.zeros(one_e.shape, F32)
        spot = corner(desc)
        put(one_e, packed_box(relay_in, 0), desc, spot)
        magnetic(one_e, None, packed_x(relay_in, 16), packed_y(relay_in, 16), one_h)
        electric(
            one_e, one_h, None, slab_coef, packed_x(relay_in, 96), packed_y(relay_in, 96), fix_e, fix_p
        )
        put(fix_e, packed_box(relay_in, 80), desc, spot)
        magnetic(fix_e, one_h, packed_x(relay_in, 160), packed_y(relay_in, 160), fix_h)

    @pl.when(is_fine())
    def _():
        spot = corner(desc)
        x0 = spot[0]
        for i in range(2):
            x = x0 + i
            rotation = curl_behind(h, x, edge_x(bx), edge_y(by))
            a, b, q = (whole(slab_coef, k, x) for k in range(3))
            for c in range(3):
                layer[c, i] = a * e[c, x] + b * rotation[c] + q * p[c, x]
        fix = cut_region(layer, desc, (0, *spot[1:]))
        latest = [[region[2 * c + i] + fix[c][i] for i in range(2)] for c in range(3)]
        restricted = fine_steps(box_in, box, coef, desc, load_box(was), latest)
        pack(relay, restricted, bx, by, 0)


def late_kernel(e, h, p, fix_e, fix_h, fix_p, coef, box, out, mixed):
    @pl.when(is_coarse())
    def _():
        view_e, view_p = out.at[pl.ds(0, 3)], out.at[pl.ds(6, 3)]
        electric(fix_e, fix_h, fix_p, coef, None, None, view_e, view_p, (e, p))
        out[3:6] = h[...] + fix_h[...]

    @pl.when(is_fine())
    def _():
        for c in range(9):
            for x in range(6):
                for u in range(3):
                    parts = from_tiles([box[c, x, 3 * u + t] for t in range(3)])
                    for a in range(3):
                        mixed[c, x, a, pl.ds(u, 8, stride=3)] = parts[a]
                for a in range(3):
                    out[c, x, :, pl.ds(128 * a, 128)] = mixed[c, x, a]


def finish_kernel(late, coef, desc, relay, out):
    @pl.when(is_coarse())
    def _():
        view_e, view_p = out.at[pl.ds(0, 3)], out.at[pl.ds(6, 3)]
        out[3:6] = late[3:6]
        complete(
            late.at[pl.ds(0, 3)], late.at[pl.ds(6, 3)], coef,
            packed_x(relay, 16), packed_y(relay, 16), view_e, view_p,
        )
        covered = [jnp.where(value, F32(1.0), 0.0) for value in covered_of(desc)]
        put(view_e, packed_box(relay, 0), desc, corner(desc), covered)

    @pl.when(is_fine())
    def _():
        out[...] = late[...]


def third(shape, a):
    return pl.BlockSpec(shape, lambda i: (0,) * (len(shape) - 1) + (a,))


def call(kernel, operands, outs, specs=None, scratch=(), grid=()):
    shapes = [out if isinstance(out, jax.ShapeDtypeStruct) else jax.ShapeDtypeStruct(out, F32) for out in outs]
    return pl.pallas_call(
        kernel,
        out_shape=shapes,
        in_specs=specs or [VM] * len(operands),
        out_specs=[VM] * len(outs),
        grid=grid,
        scratch_shapes=scratch,
        compiler_params=pltpu.CompilerParams(vmem_limit_bytes=LIMIT),
    )(*operands)


PART = (3, 6, 24, 384)
SLAB = (9, 6, 24, 384)
BOX = (9, 6, 9, 8, 128)
COEF = (5, 6, 9, 8, 128)
REGION = (3, 2, 8, 128)
X_EDGE = (2, 24, 384)
Y_EDGE = (2, 6, 384)
EDGES = [X_EDGE, Y_EDGE]
LAST = EDGES
AXES = ("grid", "gx", "gy")


def exchange(x_edge, y_edge, by, groups):
    na, nb = lax.axis_size("gx"), lax.axis_size("gy")

    def pairs(da, db):
        return [
            ((g * na + a) * nb + b, (g * na + a + da) * nb + b + db)
            for g in groups
            for a in range(na)
            for b in range(nb)
            if 0 <= a + da < na and 0 <= b + db < nb
        ]

    return (
        lax.ppermute(x_edge, AXES, pairs(by, 0)),
        lax.ppermute(y_edge, AXES, pairs(0, by)),
    )


def to_fine(value):
    return shifted(value, "grid", 1)


def to_coarse(value):
    return shifted(value, "grid", -1)


def body(fields, material, permittivity, conductivity, relax_rate, debye_strength, subgrids):
    ax, ay = call(
        edge_kernel,
        (fields, fields),
        EDGES,
        [
            pl.BlockSpec((1, 3, 1, 24, 384), lambda i: (0, 0, 0, 0, 0)),
            pl.BlockSpec((1, 3, 6, 8, 384), lambda i: (0, 0, 0, 0, 0)),
        ],
        grid=(1,),
    )
    ax, ay = exchange(ax, ay, -1, (0,))
    e, h, p, coef, desc, table = call(
        prep_kernel,
        (fields, material, permittivity, conductivity, relax_rate, debye_strength, subgrids),
        [PART] * 3 + [COEF, jax.ShapeDtypeStruct((6, 8, 128), jnp.int32), (10, 8, 128)],
        [VM] * 2 + [SM] * 5,
    )
    box, fine_coef = call(
        fine_prep_kernel,
        (fields,) * 3 + (material,) * 3 + (table, desc),
        [BOX, COEF],
        [third((1, 9, 6, 24, 128), a) for a in range(3)]
        + [third((1, 6, 24, 128), a) for a in range(3)]
        + [VM] * 2,
        grid=(1,),
    )
    h, bx, by, slab_material = call(
        h1_kernel,
        (e, h, ax, ay, material, desc),
        [PART] + LAST + [(7, 24, 384)],
    )
    slab_material = to_fine(slab_material)
    bx, by = exchange(bx, by, 1, (0,))
    e, p = call(coarse_part_kernel, (e, h, p, coef), [PART] * 2)
    e, p, sent, slab_coef, first = call(
        e1_kernel,
        (e, p, coef, bx, by, desc, slab_material, table),
        [PART] * 2 + [(6, 8, 128), COEF, REGION],
    )
    region = to_fine(sent)
    e, h, p, ax, ay, box, now, change1 = call(
        f1_kernel,
        (e, h, p, box, fine_coef, first, region, desc),
        [PART] * 3 + EDGES + [BOX, REGION, REGION],
    )
    ax2, ay2 = exchange(ax, ay, -1, (0, 1))
    h, bx, by = call(h2_kernel, (e, h, ax2, ay2), [PART] + LAST)
    bx2, by2 = exchange(bx, by, 1, (1,))
    bx, by = exchange(bx, by, 1, (0,))
    base_e, base_p, sent = call(
        base_kernel, (e, h, p, slab_coef, bx, by, desc), [PART] * 2 + [(19, 8, 128)]
    )
    region = to_fine(sent)
    e, p = call(fine_part_kernel, (e, h, p, slab_coef), [PART] * 2)
    e, p, ax, ay, box, now, change2 = call(
        f2_kernel,
        (e, p, base_e, base_p, fine_coef, slab_coef, bx2, by2, desc, box, region, now),
        [PART] * 2 + EDGES + [BOX, REGION, REGION],
    )
    ax, ay = exchange(ax, ay, -1, (0, 1))
    h, bx, by, relay = call(
        h3_kernel,
        (e, h, ax, ay, change1, ax2, ay2, change2, bx2, by2),
        [PART] + LAST + [(224, 384)],
    )
    relay = to_coarse(relay)
    fine_bx, fine_by = exchange(bx, by, 1, (1,))
    bx, by = exchange(bx, by, 1, (0,))
    base_e, base_p, sent = call(
        base_kernel, (e, h, p, slab_coef, bx, by, desc), [PART] * 2 + [(19, 8, 128)]
    )
    region = to_fine(sent)
    box, relay4, *fix = call(
        f3_kernel,
        (e, h, p, fine_coef, slab_coef, fine_bx, fine_by, desc, box, region, now, relay),
        [BOX, (80, 384)] + [PART] * 3,
        scratch=[
            pltpu.VMEM((3, 2, 24, 384), F32),
            pltpu.VMEM(PART, F32),
            pltpu.VMEM(PART, F32),
        ],
    )
    relay4 = to_coarse(relay4)
    (late,) = call(
        late_kernel,
        (base_e, h, base_p, *fix, slab_coef, box),
        [SLAB],
        scratch=[pltpu.VMEM((9, 6, 3, 24, 128), F32)],
    )
    (out,) = call(finish_kernel, (late, slab_coef, desc, relay4), [SLAB])
    return out[None]


def solution(mesh):
    in_specs = (
        P("grid", None, "gx", "gy", None),
        P("grid", "gx", "gy", None),
        P(),
        P(),
        P(),
        P(),
        P("gx", "gy", None),
    )
    out_specs = P("grid", None, "gx", "gy", None)
    return jax.shard_map(body, mesh=mesh, in_specs=in_specs, out_specs=out_specs, check_vma=False)
```

```python
import functools

import jax
import jax.numpy as jnp
from jax import lax
from jax.experimental import pallas as pl
from jax.experimental.pallas import tpu as pltpu
from jax.sharding import PartitionSpec as P

COARSE_STEPS = 3
LIMIT = 40 * 1024 * 1024
VM = pl.BlockSpec(memory_space=pltpu.VMEM)
SM = pl.BlockSpec(memory_space=pltpu.SMEM)
F32 = jnp.float32


def shifted(value, axis, by):
    peers = lax.axis_size(axis)
    pairs = [(i, i + by) for i in range(peers) if 0 <= i + by < peers]
    return lax.ppermute(value, axis, pairs)


def lanes(shape=(8, 128)):
    return lax.broadcasted_iota(jnp.int32, shape, len(shape) - 1)


def rows(shape=(8, 128)):
    return lax.broadcasted_iota(jnp.int32, shape, len(shape) - 2)


def gather(tile, index):
    return jnp.take_along_axis(tile, index, axis=1)


def tables(perm, cond, relax, debye, factor):
    lane = lanes()

    def spread(ref):
        value = jnp.full((8, 128), ref[0], F32)
        for k in range(1, ref.shape[0]):
            value = jnp.where(lane == k, ref[k], value)
        return value

    eps = spread(perm)
    damp = spread(cond) * factor / (2.0 * eps)
    rate = spread(relax) * factor
    f0 = (1.0 - damp) / (1.0 + damp)
    f1 = 1.0 / (eps * (1.0 + damp))
    f3 = jnp.exp(-rate)
    f4 = spread(debye)
    c = f1 * rate
    return (f0 - c * f4, 0.5 * f1, c, f3, (1.0 - f3) * f4)


def to_tiles(parts):
    lane = lanes()
    kind = lane % 3
    out = []
    for t in range(3):
        mixed = jnp.where(
            kind == t, parts[0], jnp.where(kind == (t + 1) % 3, parts[1], parts[2])
        )
        out.append(gather(mixed, (3 * lane + t) & 127))
    return out


def from_tiles(tiles):
    lane = lanes()
    spread = [gather(tiles[t], (43 * (lane - t + 128)) & 127) for t in range(3)]
    out = []
    for a in range(3):
        kind = (2 * a + lane) % 3
        out.append(jnp.where(kind == 0, spread[0], jnp.where(kind == 1, spread[1], spread[2])))
    return out


def prep_kernel(fields, material, perm, cond, relax, debye, sub, e, h, p, coef, desc, wide):
    for k in range(6):
        desc[k] = jnp.full((8, 128), sub[0, 0, k], jnp.int32)

    @pl.when(is_coarse())
    def _():
        table = tables(perm, cond, relax, debye, 1.0)
        for x in range(6):
            for yt in range(3):
                for zt in range(3):
                    index = material[0, x, pl.ds(8 * yt, 8), pl.ds(128 * zt, 128)]
                    for k in range(5):
                        coef[k, x, 3 * yt + zt] = gather(table[k], index)
        for k, part in enumerate((e, h, p)):
            part[...] = fields[0, 3 * k : 3 * k + 3]

    @pl.when(is_fine())
    def _():
        for k, tile in enumerate(tables(perm, cond, relax, debye, 1.0)):
            wide[k] = tile
        for k, tile in enumerate(tables(perm, cond, relax, debye, F32(1.0 / 3.0))):
            wide[5 + k] = tile


def fine_prep_kernel(f0, f1, f2, m0, m1, m2, table, desc, box, coef):
    fields, material = (f0, f1, f2), (m0, m1, m2)

    @pl.when(is_fine())
    def _():
        tiles = [table[5 + k] for k in range(5)]
        covered = covered_of(desc)
        for x in range(6):
            inside = covered[x // 3]
            for u in range(3):
                cut = pl.ds(u, 8, stride=3)
                parts = [material[a][0, x, cut] for a in range(3)]
                for t, index in enumerate(to_tiles(parts)):
                    for k in range(5):
                        coef[k, x, 3 * u + t] = gather(tiles[k], index)
                for c in range(9):
                    parts = [fields[a][0, c, x, cut] for a in range(3)]
                    for t, tile in enumerate(to_tiles(parts)):
                        box[c, x, 3 * u + t] = jnp.where(inside, tile, 0.0)


def whole(ref, *index):
    return jnp.concatenate(
        [
            jnp.concatenate([ref[(*index, 3 * yt + zt)] for zt in range(3)], axis=1)
            for yt in range(3)
        ],
        axis=0,
    )


def magnetic(e, h, next_x, next_y, out):
    row, lane = rows((24, 384)), lanes((24, 384))

    def ahead_y(value, edge):
        return jnp.where(row == 23, edge, pltpu.roll(value, 23, 0))

    def ahead_z(value):
        return jnp.where(lane == 383, 0.0, pltpu.roll(value, 383, 1))

    for x in range(6):
        ex, ey, ez = (e[c, x] for c in range(3))
        if x < 5:
            ey_x, ez_x = e[1, x + 1], e[2, x + 1]
        else:
            ey_x, ez_x = next_x(0), next_x(1)
        ex_y = ahead_y(ex, next_y(0, x))
        ez_y = ahead_y(ez, next_y(1, x))
        ex_z, ey_z = ahead_z(ex), ahead_z(ey)
        turn = ((ez_y - ez) - (ey_z - ey), (ex_z - ex) - (ez_x - ez), (ey_x - ey) - (ex_y - ex))
        for c in range(3):
            if h is None:
                out[c, x] = -0.5 * turn[c]
            else:
                out[c, x] = h[c, x] - 0.5 * turn[c]


def last_layers(h, out_x, out_y):
    out_x[0], out_x[1] = h[1, 5], h[2, 5]
    for x in range(6):
        out_y[0, x : x + 1] = h[0, x, 23:24]
        out_y[1, x : x + 1] = h[2, x, 23:24]


def first_layers(e, out_x, out_y):
    out_x[0], out_x[1] = e[1, 0], e[2, 0]
    for x in range(6):
        out_y[0, x : x + 1] = e[0, x, 0:1]
        out_y[1, x : x + 1] = e[2, x, 0:1]


def curl_behind(h, x, prev_x, prev_y):
    row, lane = rows((24, 384)), lanes((24, 384))

    def behind_y(value, edge):
        return jnp.where(row == 0, edge, pltpu.roll(value, 1, 0))

    def behind_z(value):
        return jnp.where(lane == 0, 0.0, pltpu.roll(value, 1, 1))

    hx, hy, hz = (h[c, x] for c in range(3))
    if prev_x is None:
        prev_x, prev_y = lambda k: 0.0, lambda k, x: 0.0
    if isinstance(x, int):
        hy_x, hz_x = (h[1, x - 1], h[2, x - 1]) if x > 0 else (prev_x(0), prev_x(1))
    else:
        before = jnp.maximum(x - 1, 0)
        first = jnp.full((24, 384), x, jnp.int32) == 0
        hy_x = jnp.where(first, prev_x(0), h[1, before])
        hz_x = jnp.where(first, prev_x(1), h[2, before])
    hx_y = behind_y(hx, prev_y(0, x))
    hz_y = behind_y(hz, prev_y(1, x))
    hx_z, hy_z = behind_z(hx), behind_z(hy)
    return ((hz - hz_y) - (hy - hy_z), (hx - hx_z) - (hz - hz_x), (hy - hy_x) - (hx - hx_y))


def electric(e, h, p, coef, prev_x, prev_y, out_e, out_p, more=None):
    for x in range(6):
        rotation = curl_behind(h, x, prev_x, prev_y)
        a, b, q, f3, g = (whole(coef, k, x) for k in range(5))
        for c in range(3):
            new = a * e[c, x] + b * rotation[c]
            old = None if p is None else p[c, x]
            if old is not None:
                new = new + q * old
            last = g * new if old is None else f3 * old + g * new
            if more is not None:
                new, last = new + more[0][c, x], last + more[1][c, x]
            out_e[c, x] = new
            out_p[c, x] = last


def complete(part_e, part_p, coef, prev_x, prev_y, out_e, out_p):
    for x in range(6):
        b, g = (jnp.concatenate([coef[k, x, zt, 0:1] for zt in range(3)], axis=1) for k in (1, 4))
        for c in range(3):
            new, last = part_e[c, x], part_p[c, x]
            if x == 0 and c > 0:
                more = whole(coef, 1, 0) * (prev_x(1) if c == 1 else -prev_x(0))
                new, last = new + more, last + whole(coef, 4, 0) * more
            out_e[c, x], out_p[c, x] = new, last
            if c != 1:
                more = b * (-prev_y(1, x) if c == 0 else prev_y(0, x))
                out_e[c, x, 0:1] = new[0:1] + more
                out_p[c, x, 0:1] = last[0:1] + g * more


def edge_x(ref):
    return lambda k: ref[k]


def edge_y(ref):
    return lambda k, x: ref[k, pl.ds(x, 1)]


def corner(desc):
    x0 = jnp.max(desc[0].astype(F32)).astype(jnp.int32)
    y0 = jnp.max(desc[1].astype(F32)).astype(jnp.int32)
    base = pl.multiple_of(8 * jnp.minimum(y0 // 8, 1), 8)
    return x0, base, y0 - base


def cut_region(e, desc, spot):
    x0, base, over = spot
    place = lanes() + desc[2]
    index, part = place & 127, place >> 7

    def cut(c, i):
        tiles = []
        for a in range(3):
            pair = e[c, x0 + i, pl.ds(base, 16), pl.ds(128 * a, 128)]
            tiles.append(gather(pltpu.roll(pair, (16 - over) & 15, 0)[0:8], index))
        return jnp.where(part == 0, tiles[0], jnp.where(part == 1, tiles[1], tiles[2]))

    return [[cut(c, i) for i in range(2)] for c in range(3)]


def covered_of(desc):
    within = (rows() < desc[4]) & (lanes() < desc[5])
    return [within & (desc[3] > i) for i in range(2)]


def put(e, values, desc, spot, replace=None):
    x0, base, over = spot
    empty = jnp.zeros((8, 128), F32)
    for a in range(3):
        place = lanes() + (128 * a) - desc[2]
        index = place & 127
        here = (place >= 0) & (place < 128)
        for i in range(2):
            keep = None
            if replace is not None:
                keep = jnp.where(here, gather(replace[i], index), 0.0)
                keep = pltpu.roll(jnp.concatenate([keep, empty]), over, 0) > 0.5
            for c in range(3):
                spot = (c, x0 + i, pl.ds(base, 16), pl.ds(128 * a, 128))
                tile = jnp.where(here, gather(values(c, i), index), 0.0)
                pair = pltpu.roll(jnp.concatenate([tile, empty]), over, 0)
                if replace is None:
                    e[spot] = e[spot] + pair
                else:
                    e[spot] = jnp.where(keep, pair, e[spot])


def pack(out, box, in_x, in_y, at):
    if box is not None:
        for c in range(3):
            for i in range(2):
                out[pl.ds(at + 8 * i, 8), pl.ds(128 * c, 128)] = box[c][i]
        at += 16
    for k in range(2):
        out[pl.ds(at + 24 * k, 24)] = in_x[k]
        out[pl.ds(at + 48 + 8 * k, 6)] = in_y[k, 0:6]


def packed_box(ref, at):
    return lambda c, i: ref[pl.ds(at + 8 * i, 8), pl.ds(128 * c, 128)]


def packed_x(ref, at):
    return lambda k: ref[pl.ds(at + 24 * k, 24)]


def packed_y(ref, at):
    return lambda k, x: ref[pl.ds(at + 48 + 8 * k + x, 1)]


def fine_steps(box_in, box, coef, desc, earlier, latest):
    row, lane = rows(), lanes()
    lx, ly, lz = desc[3], desc[4], desc[5]
    inside = covered_of(desc)
    y_face = [row == 0, None, row == ly - 1]
    z_face = [lane == 0, None, lane == lz - 1]

    def up(value):
        return jnp.where(row == 7, 0.0, pltpu.roll(value, 7, 0))

    def left(value):
        return jnp.where(lane == 127, 0.0, pltpu.roll(value, 127, 1))

    def down(value):
        return jnp.where(row == 0, 0.0, pltpu.roll(value, 1, 0))

    def right(value):
        return jnp.where(lane == 0, 0.0, pltpu.roll(value, 1, 1))

    def ahead_y(values, u, t):
        return values[3 * u + 3 + t] if u < 2 else up(values[t])

    def ahead_z(values, u, t):
        return values[3 * u + t + 1] if t < 2 else left(values[3 * u])

    def behind_y(values, u, t):
        return values[3 * u - 3 + t] if u > 0 else down(values[6 + t])

    def behind_z(values, u, t):
        return values[3 * u + t - 1] if t > 0 else right(values[3 * u + 2])

    def either(p, q):
        if p is None:
            return q
        return p if q is None else p | q

    zero = jnp.zeros((8, 128), F32)

    def substep(number, old_box):
        weight = (jnp.asarray(number, F32) + 1.0) / 3.0
        driven = [
            [earlier[c][i] + weight * (latest[c][i] - earlier[c][i]) for i in range(2)]
            for c in range(3)
        ]
        for x in range(6):
            part = x // 3
            e = [[old_box[c, x, k] for k in range(9)] for c in range(3)]
            if x < 5:
                ey_x = [old_box[1, x + 1, k] for k in range(9)]
                ez_x = [old_box[2, x + 1, k] for k in range(9)]
            else:
                ey_x = ez_x = [zero] * 9
            h = [[], [], []]
            for u in range(3):
                for t in range(3):
                    k = 3 * u + t
                    ex, ey, ez = e[0][k], e[1][k], e[2][k]
                    turn = (
                        (ahead_y(e[2], u, t) - ez) - (ahead_z(e[1], u, t) - ey),
                        (ahead_z(e[0], u, t) - ex) - (ez_x[k] - ez),
                        (ey_x[k] - ey) - (ahead_y(e[0], u, t) - ex),
                    )
                    for c in range(3):
                        value = old_box[3 + c, x, k] - 0.5 * turn[c]
                        box[3 + c, x, k] = value
                        h[c].append(value)
            x_face = x == 0
            if x in (2, 5):
                x_face = 3 * lx - 1 == x
            for u in range(3):
                for t in range(3):
                    k = 3 * u + t
                    hx, hy, hz = h[0][k], h[1][k], h[2][k]
                    hy_x = box[4, x - 1, k] if x > 0 else zero
                    hz_x = box[5, x - 1, k] if x > 0 else zero
                    rotation = (
                        (hz - behind_y(h[2], u, t)) - (hy - behind_z(h[1], u, t)),
                        (hx - behind_z(h[0], u, t)) - (hz - hz_x),
                        (hy - hy_x) - (hx - behind_y(h[0], u, t)),
                    )
                    a, b, p, f3, g = (coef[q, x, k] for q in range(5))
                    faces = (
                        either(y_face[u], z_face[t]),
                        None if x_face is True else either(x_face if x in (2, 5) else None, z_face[t]),
                        None if x_face is True else either(x_face if x in (2, 5) else None, y_face[u]),
                    )
                    for c in range(3):
                        old = old_box[6 + c, x, k]
                        new = a * e[c][k] + b * rotation[c] + p * old
                        if c > 0 and x_face is True:
                            new = driven[c][part]
                        elif faces[c] is not None:
                            new = jnp.where(faces[c], driven[c][part], new)
                        new = jnp.where(inside[part], new, 0.0)
                        box[c, x, k] = new
                        box[6 + c, x, k] = f3 * old + g * new

    substep(0, box_in)

    def further(number, carry):
        substep(number, box)
        return carry

    lax.fori_loop(1, 3, further, 0)
    restricted = [[zero, zero] for c in range(3)]
    for c in range(3):
        for i in range(2):
            total = zero
            for x in range(3 * i, 3 * i + 3):
                for k in range(9):
                    total = total + box[c, x, k]
            restricted[c][i] = total * F32(1.0 / 27.0)
    return restricted


def feed_back(restricted, latest, desc):
    covered = covered_of(desc)
    after = [[jnp.where(covered[i], restricted[c][i], latest[c][i]) for i in range(2)] for c in range(3)]
    return after, [[after[c][i] - latest[c][i] for i in range(2)] for c in range(3)]


def store_box(ref, values):
    for c in range(3):
        for i in range(2):
            ref[c, i] = values[c][i]


def store_tiles(ref, values):
    for c in range(3):
        for i in range(2):
            ref[2 * c + i] = values[c][i]


def load_box(ref):
    return [[ref[c, i] for i in range(2)] for c in range(3)]


def is_coarse():
    return lax.axis_index("grid") == 0


def is_fine():
    return lax.axis_index("grid") == 1


def edge_kernel(near_x, near_y, ax, ay):
    @pl.when(is_coarse())
    def _():
        ax[0], ax[1] = near_x[0, 1, 0], near_x[0, 2, 0]
        for x in range(6):
            ay[0, x : x + 1] = near_y[0, 0, x, 0:1]
            ay[1, x : x + 1] = near_y[0, 2, x, 0:1]


def coarse_part_kernel(e, h, p, coef, out_e, out_p):
    @pl.when(is_coarse())
    def _():
        electric(e, h, p, coef, None, None, out_e, out_p)


def fine_part_kernel(e, h, p, coef, out_e, out_p):
    @pl.when(is_fine())
    def _():
        electric(e, h, p, coef, None, None, out_e, out_p)


def h1_kernel(e, h, ax, ay, material, desc, out_h, bx, by, sent):
    @pl.when(is_coarse())
    def _():
        sent[0:6] = material[0].astype(F32)
        before = cut_region(e, desc, corner(desc))
        for c in range(3):
            for i in range(2):
                sent[6, pl.ds(8 * i, 8), pl.ds(128 * c, 128)] = before[c][i]
        magnetic(e, h, edge_x(ax), edge_y(ay), out_h)
        last_layers(out_h, bx, by)


def e1_kernel(
    e, p, coef, bx, by, desc, material, table, out_e, out_p, sent, slab_coef, first
):
    @pl.when(is_coarse())
    def _():
        complete(e, p, coef, edge_x(bx), edge_y(by), out_e, out_p)
        for k, tile in enumerate(sum(cut_region(out_e, desc, corner(desc)), [])):
            sent[k] = tile
        slab_coef[...] = coef[...]

    @pl.when(is_fine())
    def _():
        for c in range(3):
            for i in range(2):
                first[c, i] = material[6, pl.ds(8 * i, 8), pl.ds(128 * c, 128)]
        tiles = [table[k] for k in range(5)]
        for x in range(6):
            for yt in range(3):
                for zt in range(3):
                    index = material[x, pl.ds(8 * yt, 8), pl.ds(128 * zt, 128)].astype(jnp.int32)
                    for k in range(5):
                        slab_coef[k, x, 3 * yt + zt] = gather(tiles[k], index)


def f1_kernel(
    e, h, p, box_in, coef, first, region, desc, out_e, out_h, out_p, ax, ay, box, now, change
):
    @pl.when(is_coarse())
    def _():
        out_e[...], out_h[...], out_p[...] = e[...], h[...], p[...]
        first_layers(e, ax, ay)

    @pl.when(is_fine())
    def _():
        for out in (out_e, out_h, out_p):
            out[...] = jnp.zeros(out.shape, F32)
        earlier = load_box(first)
        latest = [[region[2 * c + i] for i in range(2)] for c in range(3)]
        restricted = fine_steps(box_in, box, coef, desc, earlier, latest)
        after, delta = feed_back(restricted, latest, desc)
        store_box(now, after)
        store_box(change, delta)
        put(out_e, lambda c, i: delta[c][i], desc, corner(desc))
        first_layers(out_e, ax, ay)


def h2_kernel(e, h, ax, ay, out_h, bx, by):
    magnetic(e, h, edge_x(ax), edge_y(ay), out_h)
    last_layers(out_h, bx, by)


def base_kernel(e, h, p, coef, bx, by, desc, out_e, out_p, sent):
    @pl.when(is_coarse())
    def _():
        electric(e, h, p, coef, edge_x(bx), edge_y(by), out_e, out_p)
        store_tiles(sent, cut_region(out_e, desc, corner(desc)))


def f2_kernel(
    e, p, base_e, base_p, coef, slab_coef, bx, by, desc, box_in, region, was,
    out_e, out_p, ax, ay, box, now, change,
):
    @pl.when(is_coarse())
    def _():
        out_e[...], out_p[...] = base_e[...], base_p[...]
        first_layers(base_e, ax, ay)

    @pl.when(is_fine())
    def _():
        spot = corner(desc)
        complete(e, p, slab_coef, edge_x(bx), edge_y(by), out_e, out_p)
        fix = cut_region(out_e, desc, spot)
        latest = [[region[2 * c + i] + fix[c][i] for i in range(2)] for c in range(3)]
        restricted = fine_steps(box_in, box, coef, desc, load_box(was), latest)
        after, delta = feed_back(restricted, latest, desc)
        store_box(now, after)
        store_box(change, delta)
        put(out_e, lambda c, i: delta[c][i], desc, spot)
        first_layers(out_e, ax, ay)


def h3_kernel(
    e, h, ax, ay, change1, ax2, ay2, change2, bx2, by2, out_h, bx, by, relay,
):
    magnetic(e, h, edge_x(ax), edge_y(ay), out_h)
    last_layers(out_h, bx, by)

    @pl.when(is_fine())
    def _():
        pack(relay, load_box(change1), ax2, ay2, 0)
        pack(relay, load_box(change2), bx2, by2, 80)
        pack(relay, None, ax, ay, 160)


def halo_kernel(bx, by, out):
    @pl.when(is_fine())
    def _():
        pack(out, None, bx, by, 0)


def f3_kernel(
    e, h, p, coef, slab_coef, bx, by, desc, box_in, region, was, relay_in,
    box, averaged, fix_e, fix_h, fix_p, layer, one_e, one_h,
):
    @pl.when(is_coarse())
    def _():
        one_e[...] = jnp.zeros(one_e.shape, F32)
        spot = corner(desc)
        put(one_e, packed_box(relay_in, 0), desc, spot)
        magnetic(one_e, None, packed_x(relay_in, 16), packed_y(relay_in, 16), one_h)
        electric(
            one_e, one_h, None, slab_coef, packed_x(relay_in, 96), packed_y(relay_in, 96), fix_e, fix_p
        )
        put(fix_e, packed_box(relay_in, 80), desc, spot)
        magnetic(fix_e, one_h, packed_x(relay_in, 160), packed_y(relay_in, 160), fix_h)

    @pl.when(is_fine())
    def _():
        spot = corner(desc)
        x0 = spot[0]
        for i in range(2):
            x = x0 + i
            rotation = curl_behind(h, x, edge_x(bx), edge_y(by))
            a, b, q = (whole(slab_coef, k, x) for k in range(3))
            for c in range(3):
                layer[c, i] = a * e[c, x] + b * rotation[c] + q * p[c, x]
        fix = cut_region(layer, desc, (0, *spot[1:]))
        latest = [[region[2 * c + i] + fix[c][i] for i in range(2)] for c in range(3)]
        restricted = fine_steps(box_in, box, coef, desc, load_box(was), latest)
        store_box(averaged, restricted)


def late_kernel(e, h, p, fix_e, fix_h, fix_p, coef, box, out, mixed):
    @pl.when(is_coarse())
    def _():
        view_e, view_p = out.at[pl.ds(0, 3)], out.at[pl.ds(6, 3)]
        electric(fix_e, fix_h, fix_p, coef, None, None, view_e, view_p, (e, p))
        out[3:6] = h[...] + fix_h[...]

    @pl.when(is_fine())
    def _():
        for c in range(9):
            for x in range(6):
                for u in range(3):
                    parts = from_tiles([box[c, x, 3 * u + t] for t in range(3)])
                    for a in range(3):
                        mixed[c, x, a, pl.ds(u, 8, stride=3)] = parts[a]
                for a in range(3):
                    out[c, x, :, pl.ds(128 * a, 128)] = mixed[c, x, a]


def finish_kernel(late, coef, desc, averaged, halos, out):
    @pl.when(is_coarse())
    def _():
        view_e, view_p = out.at[pl.ds(0, 3)], out.at[pl.ds(6, 3)]
        out[3:6] = late[3:6]
        complete(
            late.at[pl.ds(0, 3)], late.at[pl.ds(6, 3)], coef,
            packed_x(halos, 0), packed_y(halos, 0), view_e, view_p,
        )
        covered = [jnp.where(value, F32(1.0), 0.0) for value in covered_of(desc)]
        put(view_e, lambda c, i: averaged[c, i], desc, corner(desc), covered)

    @pl.when(is_fine())
    def _():
        out[...] = late[...]


def third(shape, a):
    return pl.BlockSpec(shape, lambda i: (0,) * (len(shape) - 1) + (a,))


def call(kernel, operands, outs, specs=None, scratch=(), grid=()):
    shapes = [out if isinstance(out, jax.ShapeDtypeStruct) else jax.ShapeDtypeStruct(out, F32) for out in outs]
    return pl.pallas_call(
        kernel,
        out_shape=shapes,
        in_specs=specs or [VM] * len(operands),
        out_specs=[VM] * len(outs),
        grid=grid,
        scratch_shapes=scratch,
        compiler_params=pltpu.CompilerParams(vmem_limit_bytes=LIMIT),
    )(*operands)


PART = (3, 6, 24, 384)
SLAB = (9, 6, 24, 384)
BOX = (9, 6, 9, 8, 128)
COEF = (5, 6, 9, 8, 128)
REGION = (3, 2, 8, 128)
X_EDGE = (2, 24, 384)
Y_EDGE = (2, 6, 384)
EDGES = [X_EDGE, Y_EDGE]
LAST = EDGES
AXES = ("grid", "gx", "gy")


def exchange(x_edge, y_edge, by, groups):
    na, nb = lax.axis_size("gx"), lax.axis_size("gy")

    def pairs(da, db):
        return [
            ((g * na + a) * nb + b, (g * na + a + da) * nb + b + db)
            for g in groups
            for a in range(na)
            for b in range(nb)
            if 0 <= a + da < na and 0 <= b + db < nb
        ]

    return (
        lax.ppermute(x_edge, AXES, pairs(by, 0)),
        lax.ppermute(y_edge, AXES, pairs(0, by)),
    )


def to_fine(value):
    return shifted(value, "grid", 1)


def to_coarse(value):
    return shifted(value, "grid", -1)


def body(fields, material, permittivity, conductivity, relax_rate, debye_strength, subgrids):
    ax, ay = call(
        edge_kernel,
        (fields, fields),
        EDGES,
        [
            pl.BlockSpec((1, 3, 1, 24, 384), lambda i: (0, 0, 0, 0, 0)),
            pl.BlockSpec((1, 3, 6, 8, 384), lambda i: (0, 0, 0, 0, 0)),
        ],
        grid=(1,),
    )
    ax, ay = exchange(ax, ay, -1, (0,))
    e, h, p, coef, desc, table = call(
        prep_kernel,
        (fields, material, permittivity, conductivity, relax_rate, debye_strength, subgrids),
        [PART] * 3 + [COEF, jax.ShapeDtypeStruct((6, 8, 128), jnp.int32), (10, 8, 128)],
        [VM] * 2 + [SM] * 5,
    )
    box, fine_coef = call(
        fine_prep_kernel,
        (fields,) * 3 + (material,) * 3 + (table, desc),
        [BOX, COEF],
        [third((1, 9, 6, 24, 128), a) for a in range(3)]
        + [third((1, 6, 24, 128), a) for a in range(3)]
        + [VM] * 2,
        grid=(1,),
    )
    h, bx, by, slab_material = call(
        h1_kernel,
        (e, h, ax, ay, material, desc),
        [PART] + LAST + [(7, 24, 384)],
    )
    slab_material = to_fine(slab_material)
    bx, by = exchange(bx, by, 1, (0,))
    e, p = call(coarse_part_kernel, (e, h, p, coef), [PART] * 2)
    e, p, sent, slab_coef, first = call(
        e1_kernel,
        (e, p, coef, bx, by, desc, slab_material, table),
        [PART] * 2 + [(6, 8, 128), COEF, REGION],
    )
    region = to_fine(sent)
    e, h, p, ax, ay, box, now, change1 = call(
        f1_kernel,
        (e, h, p, box, fine_coef, first, region, desc),
        [PART] * 3 + EDGES + [BOX, REGION, REGION],
    )
    ax2, ay2 = exchange(ax, ay, -1, (0, 1))
    h, bx, by = call(h2_kernel, (e, h, ax2, ay2), [PART] + LAST)
    bx2, by2 = exchange(bx, by, 1, (1,))
    bx, by = exchange(bx, by, 1, (0,))
    base_e, base_p, sent = call(
        base_kernel, (e, h, p, slab_coef, bx, by, desc), [PART] * 2 + [(19, 8, 128)]
    )
    region = to_fine(sent)
    e, p = call(fine_part_kernel, (e, h, p, slab_coef), [PART] * 2)
    e, p, ax, ay, box, now, change2 = call(
        f2_kernel,
        (e, p, base_e, base_p, fine_coef, slab_coef, bx2, by2, desc, box, region, now),
        [PART] * 2 + EDGES + [BOX, REGION, REGION],
    )
    ax, ay = exchange(ax, ay, -1, (0, 1))
    h, bx, by, relay = call(
        h3_kernel,
        (e, h, ax, ay, change1, ax2, ay2, change2, bx2, by2),
        [PART] + LAST + [(224, 384)],
    )
    relay = to_coarse(relay)
    fine_bx, fine_by = exchange(bx, by, 1, (1,))
    bx, by = exchange(bx, by, 1, (0,))
    base_e, base_p, sent = call(
        base_kernel, (e, h, p, slab_coef, bx, by, desc), [PART] * 2 + [(19, 8, 128)]
    )
    region = to_fine(sent)
    (halos,) = call(halo_kernel, (fine_bx, fine_by), [(64, 384)])
    halos = to_coarse(halos)
    box, averaged, *fix = call(
        f3_kernel,
        (e, h, p, fine_coef, slab_coef, fine_bx, fine_by, desc, box, region, now, relay),
        [BOX, REGION] + [PART] * 3,
        scratch=[
            pltpu.VMEM((3, 2, 24, 384), F32),
            pltpu.VMEM(PART, F32),
            pltpu.VMEM(PART, F32),
        ],
    )
    averaged = to_coarse(averaged)
    (late,) = call(
        late_kernel,
        (base_e, h, base_p, *fix, slab_coef, box),
        [SLAB],
        scratch=[pltpu.VMEM((9, 6, 3, 24, 128), F32)],
    )
    (out,) = call(finish_kernel, (late, slab_coef, desc, averaged, halos), [SLAB])
    return out[None]


def solution(mesh):
    in_specs = (
        P("grid", None, "gx", "gy", None),
        P("grid", "gx", "gy", None),
        P(),
        P(),
        P(),
        P(),
        P("gx", "gy", None),
    )
    out_specs = P("grid", None, "gx", "gy", None)
    return jax.shard_map(body, mesh=mesh, in_specs=in_specs, out_specs=out_specs, check_vma=False)
```
